32 devices in a mesh: st: 8 (over z, x), ta: 4 (over y, core).
Axes of the slice: x: 2, y: 2, z: 4, core: 2. Of those that a mesh axis runs over, the one named last changes fastest.
Arguments:
- samples: bfloat16 [128, 128, 8192], P('st', 'ta'), may hold values from -6 to 6
- coefficients: float32 [16, 8192], replicated, may hold values from -1.5 to 1.5
Outputs:
- visibilities: bfloat16 [32, 2, 128, 128], P(('st', 'ta'))
The draws below stay inside these ranges and needn't reach their ends.
All inputs are finite; a program needn't handle non-finite values.
Results may differ from the reference program's by a relative error of at most 0.0056.
Values may be sent and summed in bfloat16 or wider, within the bound.
No kernel may reach another device: no remote copies, remote signals or barrier semaphores. Data moves between devices by JAX's collectives and lax.ppermute only.
A program may use at most 128 MiB of HBM per device.

```python
import math
import jax
import jax.numpy as jnp
from jax import lax

NFFT = 8192
TAPS = 16
IN_DEV = 16
CH0 = 1024
INPUTS = 128
FRAMES = 128
CH = 32


def shard_levels(own_key, extent, split, least, largest):
    loudness, own = 1.0, jax.random.fold_in(own_key, 6)
    for position, shards_of in split:
        heights = jnp.exp(jax.random.uniform(jax.random.fold_in(own, position), (shards_of,), jnp.float32, least / len(split), largest / len(split)))
        loudness = loudness * jnp.repeat(heights, extent[position] // shards_of).reshape([-1 if axis == position else 1 for axis in range(len(extent))])
    return loudness


def normal_values(stream_key, extent, deviation, bound, shards=(), kind=jnp.bfloat16):
    result = deviation * jax.random.normal(stream_key, extent, jnp.float32)
    if shards:
        result = result * shard_levels(stream_key, extent, shards, -0.22, 0.18)
    return jnp.clip(result, -bound, bound).astype(kind)


def setup_inputs(seed: int = 0) -> dict:
    keys = jax.random.split(jax.random.key(seed), 3)
    return {
        "samples": normal_values(keys[0], (INPUTS, FRAMES, NFFT), 1.0, 6.0, ((0, 8), (1, 4))),
        "coefficients": normal_values(keys[1], (TAPS, NFFT), 0.25, 1.5, (), jnp.float32),
    }


def phase_table(frame_len, channel_count, first_channel):
    positions = jnp.arange(frame_len, dtype=jnp.int32)[:, None]
    channels = (first_channel + jnp.arange(channel_count, dtype=jnp.int32))[None, :]
    phases = (positions * channels) % frame_len
    angles = (2.0 * math.pi / frame_len) * phases.astype(jnp.float32)
    scale = jnp.float32(frame_len ** -0.5)
    stacked = jnp.stack([jnp.cos(angles) * scale, -jnp.sin(angles) * scale], axis=2)
    return stacked.reshape(frame_len, 2 * channel_count)


def filter_frames(extended, coefficients, frame_count):
    total_sum = jnp.zeros((extended.shape[0], frame_count, extended.shape[2]), jnp.float32)
    for tap_index in range(coefficients.shape[0]):
        window = extended[:, tap_index:tap_index + frame_count, :].astype(jnp.float32)
        total_sum = total_sum + coefficients[tap_index][None, None, :] * window
    return total_sum


def channelize_rows(filtered, table):
    return jnp.einsum("ifk,kc->cif", filtered, table, precision=lax.Precision.HIGHEST)


def correlate(channel_spectra):
    real_part = channel_spectra[0]
    imag_part = channel_spectra[1]
    left_rows = jnp.concatenate([jnp.concatenate([real_part, imag_part], 1), jnp.concatenate([imag_part, -real_part], 1)], 0)
    right_rows = jnp.concatenate([real_part, imag_part], 1)
    product = lax.dot_general(left_rows, right_rows, (((1,), (1,)), ((), ())), preferred_element_type=jnp.float32)
    return (product / jnp.float32(real_part.shape[1])).reshape(2, real_part.shape[0], real_part.shape[0]).astype(jnp.bfloat16)


def reference(samples, coefficients):
    table = phase_table(NFFT, CH, CH0)
    block_count = INPUTS // IN_DEV

    def channelize(input_block):
        zero_frames = jnp.zeros((IN_DEV, TAPS - 1, NFFT), jnp.bfloat16)
        extended = jnp.concatenate([input_block, zero_frames], 1)
        return channelize_rows(filter_frames(extended, coefficients, FRAMES), table).astype(jnp.bfloat16)

    spectra = lax.map(channelize, samples.reshape(block_count, IN_DEV, FRAMES, NFFT))
    spectra = spectra.transpose(1, 0, 2, 3).reshape(CH, 2, INPUTS, FRAMES)
    return lax.map(correlate, spectra)
```

```python
import functools
import math

import jax
import jax.numpy as jnp
import numpy as np
from jax import lax
from jax.experimental import pallas as pl
from jax.experimental.pallas import tpu as pltpu
from jax.sharding import PartitionSpec as P

CH0 = 1024
LANES = 128
CHANNEL_BLOCK = 32
K_BLOCK = 1024
NT = (((1,), (1,)), ((), ()))


def phase_table(frame_len, channel_count, first_channel):
    channels = first_channel + np.arange(channel_count, dtype=np.int64)
    phases = (channels[:, None] * np.arange(frame_len, dtype=np.int64)[None, :]) % frame_len
    angles = 2.0 * math.pi / frame_len * phases
    parts = np.stack([np.cos(angles), -np.sin(angles)]) * frame_len**-0.5
    blocks = parts.reshape(2, channel_count // CHANNEL_BLOCK, CHANNEL_BLOCK, frame_len)
    return blocks.transpose(1, 0, 2, 3).reshape(-1, 2 * CHANNEL_BLOCK, frame_len).astype(np.float32)


def channelize_kernel(frame_count, x_ref, coef_ref, table_ref, out_ref, folded, total, turned):
    step = pl.program_id(1)
    taps = coef_ref.shape[0]
    rows = table_ref.shape[1]
    table = table_ref[0]
    for tap in range(taps):
        folded[tap * rows : (tap + 1) * rows, :] = (table * coef_ref[tap : tap + 1, :]).astype(jnp.bfloat16)
    product = lax.dot_general(folded[...], x_ref[...], NT, preferred_element_type=jnp.float32)

    @pl.when(step == 0)
    def _():
        total[...] = product

    @pl.when(step > 0)
    def _():
        total[...] += product

    @pl.when(step == pl.num_programs(1) - 1)
    def _():
        half = rows // 2
        groups = total.shape[1] // LANES
        slots = 4 * groups
        frame = lax.broadcasted_iota(jnp.int32, (rows, LANES), 1) % frame_count
        for group in range(groups):
            lanes = slice(group * LANES, (group + 1) * LANES)
            both = total[0:rows, lanes]
            own = both
            for tap in range(1, taps):
                moved = pltpu.roll(total[tap * rows : (tap + 1) * rows, lanes], LANES - tap, 1)
                both = both + moved
                own = own + jnp.where(frame < frame_count - tap, moved, 0.0)
            ahead = pltpu.roll(both - own, frame_count, 1)
            for part in range(2):
                turned[pl.ds(part * groups + group, half, stride=slots), :] = own[part * half : (part + 1) * half]
                turned[pl.ds((2 + part) * groups + group, half, stride=slots), :] = ahead[
                    part * half : (part + 1) * half
                ]
        out_ref[...] = turned[...].astype(jnp.bfloat16).reshape(out_ref.shape)


def channelize(samples, coefficients, channel_count):
    inputs, frame_count, frame_len = samples.shape
    taps = coefficients.shape[0]
    rows = 2 * CHANNEL_BLOCK
    columns = inputs * frame_count
    blocks = channel_count // CHANNEL_BLOCK
    slots = 4 * columns // LANES
    k_block = min(K_BLOCK, frame_len)
    table = jnp.asarray(phase_table(frame_len, channel_count, CH0))
    return pl.pallas_call(
        functools.partial(channelize_kernel, frame_count),
        grid=(blocks, frame_len // k_block),
        in_specs=[
            pl.BlockSpec((columns, k_block), lambda b, k: (0, k)),
            pl.BlockSpec((taps, k_block), lambda b, k: (0, k)),
            pl.BlockSpec((1, rows, k_block), lambda b, k: (b, 0, k)),
        ],
        out_specs=pl.BlockSpec((CHANNEL_BLOCK, slots, LANES), lambda b, k: (b, 0, 0)),
        out_shape=jax.ShapeDtypeStruct((channel_count, slots, LANES), jnp.bfloat16),
        scratch_shapes=[
            pltpu.VMEM((taps * rows, k_block), jnp.bfloat16),
            pltpu.VMEM((taps * rows, columns), jnp.float32),
            pltpu.VMEM((CHANNEL_BLOCK * slots, LANES), jnp.float32),
        ],
        compiler_params=pltpu.CompilerParams(
            dimension_semantics=("arbitrary", "arbitrary"), vmem_limit_bytes=48 * 1024 * 1024
        ),
        cost_estimate=pl.CostEstimate(
            flops=2 * channel_count * 2 * taps * columns * frame_len,
            bytes_accessed=2 * columns * frame_len,
            transcendentals=0,
        ),
        name="channelize",
    )(samples.reshape(columns, frame_len), coefficients, table)


def correlate_kernel(frame_count, st_count, ta_count, in_ref, out_ref, spectra):
    slots = in_ref.shape[1]
    half = slots // 2
    groups = half // 2
    per_row = LANES // frame_count
    all_inputs = st_count * groups * per_row
    position = lax.broadcasted_iota(jnp.int32, (half, LANES), 1) // frame_count

    def station(st, _):
        sums = []
        for ta in range(ta_count):
            block = in_ref[st * ta_count + ta].astype(jnp.float32)
            value = block[:half]
            if ta < ta_count - 1:
                value = value + in_ref[st * ta_count + ta + 1].astype(jnp.float32)[half:]
            sums.append(value)
        for column in range(ta_count * frame_count // LANES):
            for slot in range(per_row):
                result = None
                for place in range(per_row):
                    value = sums[column * per_row + place]
                    shift = ((place - slot) * frame_count) % LANES
                    if shift:
                        value = pltpu.roll(value, shift, 1)
                    result = value if result is None else jnp.where(position == place, value, result)
                for part in range(2):
                    first = part * all_inputs + st * groups * per_row + slot
                    spectra[pl.ds(first, groups, stride=per_row), column * LANES : (column + 1) * LANES] = result[
                        part * groups : (part + 1) * groups
                    ]
        return 0

    if st_count <= 8:
        for st in range(st_count):
            station(st, 0)
    else:
        lax.fori_loop(0, st_count, station, 0)
    real_part = spectra[:all_inputs, :].astype(jnp.bfloat16)
    imag_part = spectra[all_inputs:, :].astype(jnp.bfloat16)
    right = jnp.concatenate([real_part, imag_part], 1)
    left = jnp.concatenate([imag_part, -real_part], 1)
    scale = 1.0 / (ta_count * frame_count)
    for part, rows in enumerate((right, left)):
        product = lax.dot_general(rows, right, NT, preferred_element_type=jnp.float32)
        out_ref[0, part] = (product * scale).astype(jnp.bfloat16)


def correlate(arrived, frame_count, st_count, ta_count, all_inputs):
    return pl.pallas_call(
        functools.partial(correlate_kernel, frame_count, st_count, ta_count),
        in_specs=[pl.BlockSpec(memory_space=pltpu.VMEM)],
        out_specs=pl.BlockSpec(memory_space=pltpu.VMEM),
        out_shape=jax.ShapeDtypeStruct((1, 2, all_inputs, all_inputs), jnp.bfloat16),
        scratch_shapes=[pltpu.VMEM((2 * all_inputs, ta_count * frame_count), jnp.float32)],
        compiler_params=pltpu.CompilerParams(vmem_limit_bytes=48 * 1024 * 1024),
        name="correlate",
    )(arrived)


def on_device(samples, coefficients):
    st_count = lax.axis_size("st")
    ta_count = lax.axis_size("ta")
    inputs, frame_count, _ = samples.shape
    partial = channelize(samples, coefficients, st_count * ta_count)
    arrived = lax.all_to_all(partial, ("st", "ta"), split_axis=0, concat_axis=0, tiled=True)
    return correlate(arrived, frame_count, st_count, ta_count, st_count * inputs)


def solution(mesh):
    return jax.shard_map(
        on_device,
        mesh=mesh,
        in_specs=(P("st", "ta", None), P()),
        out_specs=P(("st", "ta"), None, None, None),
        check_vma=False,
    )
```

```python
import functools
import math

import jax
import jax.numpy as jnp
import numpy as np
from jax import lax
from jax.experimental import pallas as pl
from jax.experimental.pallas import tpu as pltpu
from jax.sharding import PartitionSpec as P

CH0 = 1024
LANES = 128
CHANNEL_BLOCK = 32
K_BLOCK = 1024
ROW_BLOCK = 512
VMEM_LIMIT = 32 * 1024 * 1024
NT = (((1,), (1,)), ((), ()))


def phase_table(frame_len, channel_count, first_channel):
    channels = first_channel + np.arange(channel_count, dtype=np.int64)
    phases = (channels[:, None] * np.arange(frame_len, dtype=np.int64)[None, :]) % frame_len
    angles = 2.0 * math.pi / frame_len * phases
    parts = np.stack([np.cos(angles), -np.sin(angles)]) * frame_len**-0.5
    blocks = parts.reshape(2, channel_count // CHANNEL_BLOCK, CHANNEL_BLOCK, frame_len)
    return blocks.transpose(1, 0, 2, 3).reshape(-1, 2 * CHANNEL_BLOCK, frame_len).astype(np.float32)


def channelize_kernel(frame_count, x_hbm, coef_hbm, table_hbm, out_ref, x_in, coef_in, table_in, even, odd, total, turned, sems):
    block = pl.program_id(0)
    chunks, taps, k_block = coef_in.shape
    rows = table_in.shape[1]
    columns = x_in.shape[1]

    def table_copy(chunk):
        lanes = pl.ds(chunk * k_block, k_block)
        return pltpu.make_async_copy(table_hbm.at[block, :, lanes], table_in.at[chunk], sems.at[0, chunk])

    def coef_copy(chunk):
        lanes = pl.ds(chunk * k_block, k_block)
        return pltpu.make_async_copy(coef_hbm.at[:, lanes], coef_in.at[chunk], sems.at[1, chunk])

    def x_copy(chunk):
        lanes = pl.ds(chunk * k_block, k_block)
        return pltpu.make_async_copy(x_hbm.at[:, lanes], x_in.at[chunk], sems.at[2, chunk])

    for chunk in range(chunks):
        coef_copy(chunk).start()
        table_copy(chunk).start()
        x_copy(chunk).start()

    def fold(chunk, into):
        table = table_in[chunk]
        coef = coef_in[chunk]
        for tap in range(taps):
            into[tap * rows : (tap + 1) * rows, :] = (table * coef[tap : tap + 1, :]).astype(jnp.bfloat16)

    def multiply(chunk, folded):
        x = x_in[chunk]
        for first in range(0, taps * rows, ROW_BLOCK):
            part = slice(first, first + ROW_BLOCK)
            total[part, :] += lax.dot_general(folded[part, :], x, NT, preferred_element_type=jnp.float32)

    def wait_table(chunk):
        coef_copy(chunk).wait()
        table_copy(chunk).wait()

    total[...] = jnp.zeros_like(total)
    wait_table(0)
    fold(0, even)

    def pair(index, _):
        chunk = 2 * index
        wait_table(chunk + 1)
        x_copy(chunk).wait()
        fold(chunk + 1, odd)
        multiply(chunk, even)

        @pl.when(chunk + 2 < chunks)
        def _():
            wait_table(chunk + 2)

        x_copy(chunk + 1).wait()
        fold(jnp.minimum(chunk + 2, chunks - 1), even)
        multiply(chunk + 1, odd)
        return 0

    lax.fori_loop(0, chunks // 2, pair, 0)

    half = rows // 2
    groups = columns // LANES
    slots = 4 * groups
    frame = lax.broadcasted_iota(jnp.int32, (rows, LANES), 1) % frame_count
    for group in range(groups):
        lanes = slice(group * LANES, (group + 1) * LANES)
        both = total[0:rows, lanes]
        own = both
        for tap in range(1, taps):
            moved = pltpu.roll(total[tap * rows : (tap + 1) * rows, lanes], LANES - tap, 1)
            both = both + moved
            own = own + jnp.where(frame < frame_count - tap, moved, 0.0)
        ahead = pltpu.roll(both - own, frame_count, 1)
        for part in range(2):
            turned[pl.ds(part * groups + group, half, stride=slots), :] = own[part * half : (part + 1) * half]
            turned[pl.ds((2 + part) * groups + group, half, stride=slots), :] = ahead[part * half : (part + 1) * half]
    out_ref[...] = turned[...].astype(jnp.bfloat16).reshape(out_ref.shape)


def channelize(samples, coefficients, channel_count):
    inputs, frame_count, frame_len = samples.shape
    taps = coefficients.shape[0]
    rows = 2 * CHANNEL_BLOCK
    columns = inputs * frame_count
    blocks = channel_count // CHANNEL_BLOCK
    slots = 4 * columns // LANES
    k_block = min(K_BLOCK, frame_len // 2)
    chunks = frame_len // k_block
    table = jnp.asarray(phase_table(frame_len, channel_count, CH0))
    return pl.pallas_call(
        functools.partial(channelize_kernel, frame_count),
        grid=(blocks,),
        in_specs=[pl.BlockSpec(memory_space=pltpu.HBM)] * 3,
        out_specs=pl.BlockSpec((CHANNEL_BLOCK, slots, LANES), lambda b: (b, 0, 0)),
        out_shape=jax.ShapeDtypeStruct((channel_count, slots, LANES), jnp.bfloat16),
        scratch_shapes=[
            pltpu.VMEM((chunks, columns, k_block), jnp.bfloat16),
            pltpu.VMEM((chunks, taps, k_block), jnp.float32),
            pltpu.VMEM((chunks, rows, k_block), jnp.float32),
            pltpu.VMEM((taps * rows, k_block), jnp.bfloat16),
            pltpu.VMEM((taps * rows, k_block), jnp.bfloat16),
            pltpu.VMEM((taps * rows, columns), jnp.float32),
            pltpu.VMEM((CHANNEL_BLOCK * slots, LANES), jnp.float32),
            pltpu.SemaphoreType.DMA((3, chunks)),
        ],
        compiler_params=pltpu.CompilerParams(
            dimension_semantics=("arbitrary",), vmem_limit_bytes=VMEM_LIMIT
        ),
        cost_estimate=pl.CostEstimate(
            flops=2 * channel_count * 2 * taps * columns * frame_len,
            bytes_accessed=2 * columns * frame_len,
            transcendentals=0,
        ),
        name="channelize",
    )(samples.reshape(columns, frame_len), coefficients, table)


def correlate_kernel(frame_count, st_count, ta_count, in_ref, out_ref, spectra):
    slots = in_ref.shape[1]
    half = slots // 2
    groups = half // 2
    per_row = LANES // frame_count
    all_inputs = st_count * groups * per_row
    position = lax.broadcasted_iota(jnp.int32, (half, LANES), 1) // frame_count

    def station(st, _):
        sums = []
        for ta in range(ta_count):
            block = in_ref[st * ta_count + ta].astype(jnp.float32)
            value = block[:half]
            if ta < ta_count - 1:
                value = value + in_ref[st * ta_count + ta + 1].astype(jnp.float32)[half:]
            sums.append(value)
        for column in range(ta_count * frame_count // LANES):
            for slot in range(per_row):
                result = None
                for place in range(per_row):
                    value = sums[column * per_row + place]
                    shift = ((place - slot) * frame_count) % LANES
                    if shift:
                        value = pltpu.roll(value, shift, 1)
                    result = value if result is None else jnp.where(position == place, value, result)
                for part in range(2):
                    first = part * all_inputs + st * groups * per_row + slot
                    spectra[pl.ds(first, groups, stride=per_row), column * LANES : (column + 1) * LANES] = result[
                        part * groups : (part + 1) * groups
                    ]
        return 0

    if st_count <= 8:
        for st in range(st_count):
            station(st, 0)
    else:
        lax.fori_loop(0, st_count, station, 0)
    real_part = spectra[:all_inputs, :].astype(jnp.bfloat16)
    imag_part = spectra[all_inputs:, :].astype(jnp.bfloat16)
    right = jnp.concatenate([real_part, imag_part], 1)
    left = jnp.concatenate([imag_part, -real_part], 1)
    scale = 1.0 / (ta_count * frame_count)
    for part, rows in enumerate((right, left)):
        product = lax.dot_general(rows, right, NT, preferred_element_type=jnp.float32)
        out_ref[0, part] = (product * scale).astype(jnp.bfloat16)


def correlate(arrived, frame_count, st_count, ta_count, all_inputs):
    return pl.pallas_call(
        functools.partial(correlate_kernel, frame_count, st_count, ta_count),
        in_specs=[pl.BlockSpec(memory_space=pltpu.VMEM)],
        out_specs=pl.BlockSpec(memory_space=pltpu.VMEM),
        out_shape=jax.ShapeDtypeStruct((1, 2, all_inputs, all_inputs), jnp.bfloat16),
        scratch_shapes=[pltpu.VMEM((2 * all_inputs, ta_count * frame_count), jnp.float32)],
        compiler_params=pltpu.CompilerParams(vmem_limit_bytes=VMEM_LIMIT),
        name="correlate",
    )(arrived)


def on_device(samples, coefficients):
    st_count = lax.axis_size("st")
    ta_count = lax.axis_size("ta")
    inputs, frame_count, _ = samples.shape
    partial = channelize(samples, coefficients, st_count * ta_count)
    arrived = lax.all_to_all(partial, ("st", "ta"), split_axis=0, concat_axis=0, tiled=True)
    return correlate(arrived, frame_count, st_count, ta_count, st_count * inputs)


def solution(mesh):
    return jax.shard_map(
        on_device,
        mesh=mesh,
        in_specs=(P("st", "ta", None), P()),
        out_specs=P(("st", "ta"), None, None, None),
        check_vma=False,
    )
```

```python
import functools
import math

import jax
import jax.numpy as jnp
import numpy as np
from jax import lax
from jax.experimental import pallas as pl
from jax.experimental.pallas import tpu as pltpu
from jax.sharding import PartitionSpec as P

CH0 = 1024
LANES = 128
CHANNEL_BLOCK = 32
K_BLOCK = 2048
VMEM_LIMIT = 60 * 1024 * 1024
NT = (((1,), (1,)), ((), ()))


def phase_table(frame_len, channel_count, first_channel):
    channels = first_channel + np.arange(channel_count, dtype=np.int64)
    phases = (channels[:, None] * np.arange(frame_len, dtype=np.int64)[None, :]) % frame_len
    angles = 2.0 * math.pi / frame_len * phases
    parts = np.stack([np.cos(angles), -np.sin(angles)]) * frame_len**-0.5
    blocks = parts.reshape(2, channel_count // CHANNEL_BLOCK, CHANNEL_BLOCK, frame_len)
    return blocks.transpose(1, 0, 2, 3).reshape(-1, 2 * CHANNEL_BLOCK, frame_len).astype(np.float32)


def channelize_kernel(frame_count, x_ref, coef_ref, table_ref, out_ref, folded, total, turned):
    step = pl.program_id(1)
    taps = coef_ref.shape[0]
    rows = table_ref.shape[1]
    table = table_ref[0]
    for tap in range(taps):
        folded[tap * rows : (tap + 1) * rows, :] = (table * coef_ref[tap : tap + 1, :]).astype(jnp.bfloat16)
    product = lax.dot_general(folded[...], x_ref[...], NT, preferred_element_type=jnp.float32)

    @pl.when(step == 0)
    def _():
        total[...] = product

    @pl.when(step > 0)
    def _():
        total[...] += product

    @pl.when(step == pl.num_programs(1) - 1)
    def _():
        half = rows // 2
        groups = total.shape[1] // LANES
        slots = 4 * groups
        frame = lax.broadcasted_iota(jnp.int32, (rows, LANES), 1) % frame_count
        for group in range(groups):
            lanes = slice(group * LANES, (group + 1) * LANES)
            both = total[0:rows, lanes]
            own = both
            for tap in range(1, taps):
                moved = pltpu.roll(total[tap * rows : (tap + 1) * rows, lanes], LANES - tap, 1)
                both = both + moved
                own = own + jnp.where(frame < frame_count - tap, moved, 0.0)
            ahead = pltpu.roll(both - own, frame_count, 1)
            for part in range(2):
                turned[pl.ds(part * groups + group, half, stride=slots), :] = own[part * half : (part + 1) * half]
                turned[pl.ds((2 + part) * groups + group, half, stride=slots), :] = ahead[
                    part * half : (part + 1) * half
                ]
        out_ref[...] = turned[...].astype(jnp.bfloat16).reshape(out_ref.shape)


def channelize(samples, coefficients, channel_count):
    inputs, frame_count, frame_len = samples.shape
    taps = coefficients.shape[0]
    rows = 2 * CHANNEL_BLOCK
    columns = inputs * frame_count
    blocks = channel_count // CHANNEL_BLOCK
    slots = 4 * columns // LANES
    k_block = min(K_BLOCK, frame_len)
    table = jnp.asarray(phase_table(frame_len, channel_count, CH0))
    return pl.pallas_call(
        functools.partial(channelize_kernel, frame_count),
        grid=(blocks, frame_len // k_block),
        in_specs=[
            pl.BlockSpec((columns, k_block), lambda b, k: (0, k)),
            pl.BlockSpec((taps, k_block), lambda b, k: (0, k)),
            pl.BlockSpec((1, rows, k_block), lambda b, k: (b, 0, k)),
        ],
        out_specs=pl.BlockSpec((CHANNEL_BLOCK, slots, LANES), lambda b, k: (b, 0, 0)),
        out_shape=jax.ShapeDtypeStruct((channel_count, slots, LANES), jnp.bfloat16),
        scratch_shapes=[
            pltpu.VMEM((taps * rows, k_block), jnp.bfloat16),
            pltpu.VMEM((taps * rows, columns), jnp.float32),
            pltpu.VMEM((CHANNEL_BLOCK * slots, LANES), jnp.float32),
        ],
        compiler_params=pltpu.CompilerParams(
            dimension_semantics=("arbitrary", "arbitrary"), vmem_limit_bytes=VMEM_LIMIT
        ),
        cost_estimate=pl.CostEstimate(
            flops=2 * channel_count * 2 * taps * columns * frame_len,
            bytes_accessed=2 * columns * frame_len,
            transcendentals=0,
        ),
        name="channelize",
    )(samples.reshape(columns, frame_len), coefficients, table)


def correlate_kernel(frame_count, st_count, ta_count, in_ref, out_ref, spectra):
    slots = in_ref.shape[1]
    half = slots // 2
    groups = half // 2
    per_row = LANES // frame_count
    all_inputs = st_count * groups * per_row
    position = lax.broadcasted_iota(jnp.int32, (half, LANES), 1) // frame_count

    def station(st, _):
        sums = []
        for ta in range(ta_count):
            block = in_ref[st * ta_count + ta].astype(jnp.float32)
            value = block[:half]
            if ta < ta_count - 1:
                value = value + in_ref[st * ta_count + ta + 1].astype(jnp.float32)[half:]
            sums.append(value)
        for column in range(ta_count * frame_count // LANES):
            for slot in range(per_row):
                result = None
                for place in range(per_row):
                    value = sums[column * per_row + place]
                    shift = ((place - slot) * frame_count) % LANES
                    if shift:
                        value = pltpu.roll(value, shift, 1)
                    result = value if result is None else jnp.where(position == place, value, result)
                for part in range(2):
                    first = part * all_inputs + st * groups * per_row + slot
                    spectra[pl.ds(first, groups, stride=per_row), column * LANES : (column + 1) * LANES] = result[
                        part * groups : (part + 1) * groups
                    ]
        return 0

    if st_count <= 8:
        for st in range(st_count):
            station(st, 0)
    else:
        lax.fori_loop(0, st_count, station, 0)
    real_part = spectra[:all_inputs, :].astype(jnp.bfloat16)
    imag_part = spectra[all_inputs:, :].astype(jnp.bfloat16)
    right = jnp.concatenate([real_part, imag_part], 1)
    left = jnp.concatenate([imag_part, -real_part], 1)
    scale = 1.0 / (ta_count * frame_count)
    for part, rows in enumerate((right, left)):
        product = lax.dot_general(rows, right, NT, preferred_element_type=jnp.float32)
        out_ref[0, part] = (product * scale).astype(jnp.bfloat16)


def correlate(arrived, frame_count, st_count, ta_count, all_inputs):
    return pl.pallas_call(
        functools.partial(correlate_kernel, frame_count, st_count, ta_count),
        in_specs=[pl.BlockSpec(memory_space=pltpu.VMEM)],
        out_specs=pl.BlockSpec(memory_space=pltpu.VMEM),
        out_shape=jax.ShapeDtypeStruct((1, 2, all_inputs, all_inputs), jnp.bfloat16),
        scratch_shapes=[pltpu.VMEM((2 * all_inputs, ta_count * frame_count), jnp.float32)],
        compiler_params=pltpu.CompilerParams(vmem_limit_bytes=VMEM_LIMIT),
        name="correlate",
    )(arrived)


def on_device(samples, coefficients):
    st_count = lax.axis_size("st")
    ta_count = lax.axis_size("ta")
    inputs, frame_count, _ = samples.shape
    partial = channelize(samples, coefficients, st_count * ta_count)
    arrived = lax.all_to_all(partial, ("st", "ta"), split_axis=0, concat_axis=0, tiled=True)
    return correlate(arrived, frame_count, st_count, ta_count, st_count * inputs)


def solution(mesh):
    return jax.shard_map(
        on_device,
        mesh=mesh,
        in_specs=(P("st", "ta", None), P()),
        out_specs=P(("st", "ta"), None, None, None),
        check_vma=False,
    )
```

```python
import functools
import math

import jax
import jax.numpy as jnp
import numpy as np
from jax import lax
from jax.experimental import pallas as pl
from jax.experimental.pallas import tpu as pltpu
from jax.sharding import PartitionSpec as P

CH0 = 1024
LANES = 128
CHANNEL_BLOCK = 32
VMEM_LIMIT = 24 * 1024 * 1024
NT = (((1,), (1,)), ((), ()))


def phase_table(frame_len, channel_count, first_channel):
    channels = first_channel + np.arange(channel_count, dtype=np.int64)
    phases = (channels[:, None] * np.arange(frame_len, dtype=np.int64)[None, :]) % frame_len
    angles = 2.0 * math.pi / frame_len * phases
    parts = np.stack([np.cos(angles), -np.sin(angles)]) * frame_len**-0.5
    blocks = parts.reshape(2, channel_count // CHANNEL_BLOCK, CHANNEL_BLOCK, frame_len)
    return blocks.transpose(1, 0, 2, 3).reshape(-1, 2 * CHANNEL_BLOCK, frame_len).astype(np.float32)


def shift_kernel(frame_count, taps, total, out_ref, turned):
    rows = total.shape[0] // taps
    half = rows // 2
    groups = total.shape[1] // LANES
    slots = 4 * groups
    frame = lax.broadcasted_iota(jnp.int32, (rows, LANES), 1) % frame_count
    for group in range(groups):
        lanes = slice(group * LANES, (group + 1) * LANES)
        both = total[0:rows, lanes]
        own = both
        for tap in range(1, taps):
            moved = pltpu.roll(total[tap * rows : (tap + 1) * rows, lanes], LANES - tap, 1)
            both = both + moved
            own = own + jnp.where(frame < frame_count - tap, moved, 0.0)
        ahead = pltpu.roll(both - own, frame_count, 1)
        for part in range(2):
            turned[pl.ds(part * groups + group, half, stride=slots), :] = own[part * half : (part + 1) * half]
            turned[pl.ds((2 + part) * groups + group, half, stride=slots), :] = ahead[part * half : (part + 1) * half]
    out_ref[...] = turned[...].astype(jnp.bfloat16).reshape(out_ref.shape)


def channelize_block(rows_of_samples, coefficients, table, frame_count):
    taps = coefficients.shape[0]
    rows, frame_len = table.shape
    columns = rows_of_samples.shape[0]
    slots = 4 * columns // LANES
    folded = (coefficients[:, None, :] * table[None, :, :]).astype(jnp.bfloat16).reshape(taps * rows, frame_len)
    total = lax.dot_general(folded, rows_of_samples, NT, preferred_element_type=jnp.float32)
    return pl.pallas_call(
        functools.partial(shift_kernel, frame_count, taps),
        in_specs=[pl.BlockSpec(memory_space=pltpu.VMEM)],
        out_specs=pl.BlockSpec(memory_space=pltpu.VMEM),
        out_shape=jax.ShapeDtypeStruct((CHANNEL_BLOCK, slots, LANES), jnp.bfloat16),
        scratch_shapes=[pltpu.VMEM((CHANNEL_BLOCK * slots, LANES), jnp.float32)],
        compiler_params=pltpu.CompilerParams(vmem_limit_bytes=VMEM_LIMIT),
        name="shift",
    )(total)


def channelize(samples, coefficients, channel_count):
    inputs, frame_count, frame_len = samples.shape
    rows_of_samples = samples.reshape(inputs * frame_count, frame_len)
    table = jnp.asarray(phase_table(frame_len, channel_count, CH0))
    blocks = lax.map(lambda part: channelize_block(rows_of_samples, coefficients, part, frame_count), table)
    return blocks.reshape(channel_count, -1, LANES)


def correlate_kernel(frame_count, st_count, ta_count, in_ref, out_ref, spectra):
    slots = in_ref.shape[1]
    half = slots // 2
    groups = half // 2
    per_row = LANES // frame_count
    all_inputs = st_count * groups * per_row
    position = lax.broadcasted_iota(jnp.int32, (half, LANES), 1) // frame_count

    def station(st, _):
        sums = []
        for ta in range(ta_count):
            block = in_ref[st * ta_count + ta].astype(jnp.float32)
            value = block[:half]
            if ta < ta_count - 1:
                value = value + in_ref[st * ta_count + ta + 1].astype(jnp.float32)[half:]
            sums.append(value)
        for column in range(ta_count * frame_count // LANES):
            for slot in range(per_row):
                result = None
                for place in range(per_row):
                    value = sums[column * per_row + place]
                    shift = ((place - slot) * frame_count) % LANES
                    if shift:
                        value = pltpu.roll(value, shift, 1)
                    result = value if result is None else jnp.where(position == place, value, result)
                for part in range(2):
                    first = part * all_inputs + st * groups * per_row + slot
                    spectra[pl.ds(first, groups, stride=per_row), column * LANES : (column + 1) * LANES] = result[
                        part * groups : (part + 1) * groups
                    ]
        return 0

    if st_count <= 8:
        for st in range(st_count):
            station(st, 0)
    else:
        lax.fori_loop(0, st_count, station, 0)
    real_part = spectra[:all_inputs, :].astype(jnp.bfloat16)
    imag_part = spectra[all_inputs:, :].astype(jnp.bfloat16)
    right = jnp.concatenate([real_part, imag_part], 1)
    left = jnp.concatenate([imag_part, -real_part], 1)
    scale = 1.0 / (ta_count * frame_count)
    for part, rows in enumerate((right, left)):
        product = lax.dot_general(rows, right, NT, preferred_element_type=jnp.float32)
        out_ref[0, part] = (product * scale).astype(jnp.bfloat16)


def correlate(arrived, frame_count, st_count, ta_count, all_inputs):
    return pl.pallas_call(
        functools.partial(correlate_kernel, frame_count, st_count, ta_count),
        in_specs=[pl.BlockSpec(memory_space=pltpu.VMEM)],
        out_specs=pl.BlockSpec(memory_space=pltpu.VMEM),
        out_shape=jax.ShapeDtypeStruct((1, 2, all_inputs, all_inputs), jnp.bfloat16),
        scratch_shapes=[pltpu.VMEM((2 * all_inputs, ta_count * frame_count), jnp.float32)],
        compiler_params=pltpu.CompilerParams(vmem_limit_bytes=32 * 1024 * 1024),
        name="correlate",
    )(arrived)


def on_device(samples, coefficients):
    st_count = lax.axis_size("st")
    ta_count = lax.axis_size("ta")
    inputs, frame_count, _ = samples.shape
    partial = channelize(samples, coefficients, st_count * ta_count)
    arrived = lax.all_to_all(partial, ("st", "ta"), split_axis=0, concat_axis=0, tiled=True)
    return correlate(arrived, frame_count, st_count, ta_count, st_count * inputs)


def solution(mesh):
    return jax.shard_map(
        on_device,
        mesh=mesh,
        in_specs=(P("st", "ta", None), P()),
        out_specs=P(("st", "ta"), None, None, None),
        check_vma=False,
    )
```

```python
import functools
import math

import jax
import jax.numpy as jnp
import numpy as np
from jax import lax
from jax.experimental import pallas as pl
from jax.experimental.pallas import tpu as pltpu
from jax.sharding import PartitionSpec as P

CH0 = 1024
LANES = 128
CHANNEL_BLOCK = 32
K_BLOCK = 1024
ROW_BLOCK = 1024
VMEM_LIMIT = 60 * 1024 * 1024
NT = (((1,), (1,)), ((), ()))


def phase_table(frame_len, channel_count, first_channel):
    channels = first_channel + np.arange(channel_count, dtype=np.int64)
    phases = (channels[:, None] * np.arange(frame_len, dtype=np.int64)[None, :]) % frame_len
    angles = 2.0 * math.pi / frame_len * phases
    parts = np.stack([np.cos(angles), -np.sin(angles)]) * frame_len**-0.5
    blocks = parts.reshape(2, channel_count // CHANNEL_BLOCK, CHANNEL_BLOCK, frame_len)
    return blocks.transpose(1, 0, 2, 3).reshape(-1, 2 * CHANNEL_BLOCK, frame_len).astype(np.float32)


def channelize_kernel(frame_count, x_hbm, coef_hbm, table_hbm, out_ref, x_in, coef_in, table_in, even, odd, total, turned, sems):
    block = pl.program_id(0)
    chunks, taps, k_block = coef_in.shape
    rows = table_in.shape[1]
    columns = x_in.shape[1]

    def table_copy(chunk):
        lanes = pl.ds(chunk * k_block, k_block)
        return pltpu.make_async_copy(table_hbm.at[block, :, lanes], table_in.at[chunk], sems.at[0, chunk])

    def coef_copy(chunk):
        lanes = pl.ds(chunk * k_block, k_block)
        return pltpu.make_async_copy(coef_hbm.at[:, lanes], coef_in.at[chunk], sems.at[1, chunk])

    def x_copy(chunk):
        lanes = pl.ds(chunk * k_block, k_block)
        return pltpu.make_async_copy(x_hbm.at[:, lanes], x_in.at[chunk], sems.at[2, chunk])

    for chunk in range(chunks):
        coef_copy(chunk).start()
        table_copy(chunk).start()
        x_copy(chunk).start()

    def fold(chunk, into):
        table = table_in[chunk]
        coef = coef_in[chunk]
        for tap in range(taps):
            into[tap * rows : (tap + 1) * rows, :] = (table * coef[tap : tap + 1, :]).astype(jnp.bfloat16)

    def multiply(chunk, folded):
        x = x_in[chunk]
        for first in range(0, taps * rows, ROW_BLOCK):
            part = slice(first, first + ROW_BLOCK)
            total[part, :] += lax.dot_general(folded[part, :], x, NT, preferred_element_type=jnp.float32)

    def wait_table(chunk):
        coef_copy(chunk).wait()
        table_copy(chunk).wait()

    total[...] = jnp.zeros_like(total)
    wait_table(0)
    fold(0, even)

    def pair(index, _):
        chunk = 2 * index
        wait_table(chunk + 1)
        x_copy(chunk).wait()
        fold(chunk + 1, odd)
        multiply(chunk, even)

        @pl.when(chunk + 2 < chunks)
        def _():
            wait_table(chunk + 2)

        x_copy(chunk + 1).wait()
        fold(jnp.minimum(chunk + 2, chunks - 1), even)
        multiply(chunk + 1, odd)
        return 0

    lax.fori_loop(0, chunks // 2, pair, 0)

    half = rows // 2
    groups = columns // LANES
    slots = 4 * groups
    frame = lax.broadcasted_iota(jnp.int32, (rows, LANES), 1) % frame_count
    for group in range(groups):
        lanes = slice(group * LANES, (group + 1) * LANES)
        both = total[0:rows, lanes]
        own = both
        for tap in range(1, taps):
            moved = pltpu.roll(total[tap * rows : (tap + 1) * rows, lanes], LANES - tap, 1)
            both = both + moved
            own = own + jnp.where(frame < frame_count - tap, moved, 0.0)
        ahead = pltpu.roll(both - own, frame_count, 1)
        for part in range(2):
            turned[pl.ds(part * groups + group, half, stride=slots), :] = own[part * half : (part + 1) * half]
            turned[pl.ds((2 + part) * groups + group, half, stride=slots), :] = ahead[part * half : (part + 1) * half]
    out_ref[...] = turned[...].astype(jnp.bfloat16).reshape(out_ref.shape)


def channelize(samples, coefficients, channel_count):
    inputs, frame_count, frame_len = samples.shape
    taps = coefficients.shape[0]
    rows = 2 * CHANNEL_BLOCK
    columns = inputs * frame_count
    blocks = channel_count // CHANNEL_BLOCK
    slots = 4 * columns // LANES
    k_block = min(K_BLOCK, frame_len // 2)
    chunks = frame_len // k_block
    table = jnp.asarray(phase_table(frame_len, channel_count, CH0))
    return pl.pallas_call(
        functools.partial(channelize_kernel, frame_count),
        grid=(blocks,),
        in_specs=[pl.BlockSpec(memory_space=pltpu.HBM)] * 3,
        out_specs=pl.BlockSpec((CHANNEL_BLOCK, slots, LANES), lambda b: (b, 0, 0)),
        out_shape=jax.ShapeDtypeStruct((channel_count, slots, LANES), jnp.bfloat16),
        scratch_shapes=[
            pltpu.VMEM((chunks, columns, k_block), jnp.bfloat16),
            pltpu.VMEM((chunks, taps, k_block), jnp.float32),
            pltpu.VMEM((chunks, rows, k_block), jnp.float32),
            pltpu.VMEM((taps * rows, k_block), jnp.bfloat16),
            pltpu.VMEM((taps * rows, k_block), jnp.bfloat16),
            pltpu.VMEM((taps * rows, columns), jnp.float32),
            pltpu.VMEM((CHANNEL_BLOCK * slots, LANES), jnp.float32),
            pltpu.SemaphoreType.DMA((3, chunks)),
        ],
        compiler_params=pltpu.CompilerParams(
            dimension_semantics=("arbitrary",), vmem_limit_bytes=VMEM_LIMIT
        ),
        cost_estimate=pl.CostEstimate(
            flops=2 * channel_count * 2 * taps * columns * frame_len,
            bytes_accessed=2 * columns * frame_len,
            transcendentals=0,
        ),
        name="channelize",
    )(samples.reshape(columns, frame_len), coefficients, table)


def correlate_kernel(frame_count, st_count, ta_count, in_ref, out_ref, spectra):
    slots = in_ref.shape[1]
    half = slots // 2
    groups = half // 2
    per_row = LANES // frame_count
    all_inputs = st_count * groups * per_row
    position = lax.broadcasted_iota(jnp.int32, (half, LANES), 1) // frame_count

    def station(st, _):
        sums = []
        for ta in range(ta_count):
            block = in_ref[st * ta_count + ta].astype(jnp.float32)
            value = block[:half]
            if ta < ta_count - 1:
                value = value + in_ref[st * ta_count + ta + 1].astype(jnp.float32)[half:]
            sums.append(value)
        for column in range(ta_count * frame_count // LANES):
            for slot in range(per_row):
                result = None
                for place in range(per_row):
                    value = sums[column * per_row + place]
                    shift = ((place - slot) * frame_count) % LANES
                    if shift:
                        value = pltpu.roll(value, shift, 1)
                    result = value if result is None else jnp.where(position == place, value, result)
                for part in range(2):
                    first = part * all_inputs + st * groups * per_row + slot
                    spectra[pl.ds(first, groups, stride=per_row), column * LANES : (column + 1) * LANES] = result[
                        part * groups : (part + 1) * groups
                    ]
        return 0

    if st_count <= 8:
        for st in range(st_count):
            station(st, 0)
    else:
        lax.fori_loop(0, st_count, station, 0)
    real_part = spectra[:all_inputs, :].astype(jnp.bfloat16)
    imag_part = spectra[all_inputs:, :].astype(jnp.bfloat16)
    right = jnp.concatenate([real_part, imag_part], 1)
    left = jnp.concatenate([imag_part, -real_part], 1)
    scale = 1.0 / (ta_count * frame_count)
    for part, rows in enumerate((right, left)):
        product = lax.dot_general(rows, right, NT, preferred_element_type=jnp.float32)
        out_ref[0, part] = (product * scale).astype(jnp.bfloat16)


def correlate(arrived, frame_count, st_count, ta_count, all_inputs):
    return pl.pallas_call(
        functools.partial(correlate_kernel, frame_count, st_count, ta_count),
        in_specs=[pl.BlockSpec(memory_space=pltpu.VMEM)],
        out_specs=pl.BlockSpec(memory_space=pltpu.VMEM),
        out_shape=jax.ShapeDtypeStruct((1, 2, all_inputs, all_inputs), jnp.bfloat16),
        scratch_shapes=[pltpu.VMEM((2 * all_inputs, ta_count * frame_count), jnp.float32)],
        compiler_params=pltpu.CompilerParams(vmem_limit_bytes=32 * 1024 * 1024),
        name="correlate",
    )(arrived)


def on_device(samples, coefficients):
    st_count = lax.axis_size("st")
    ta_count = lax.axis_size("ta")
    inputs, frame_count, _ = samples.shape
    partial = channelize(samples, coefficients, st_count * ta_count)
    arrived = lax.all_to_all(partial, ("st", "ta"), split_axis=0, concat_axis=0, tiled=True)
    return correlate(arrived, frame_count, st_count, ta_count, st_count * inputs)


def solution(mesh):
    return jax.shard_map(
        on_device,
        mesh=mesh,
        in_specs=(P("st", "ta", None), P()),
        out_specs=P(("st", "ta"), None, None, None),
        check_vma=False,
    )
```

```python
import functools
import math

import jax
import jax.numpy as jnp
import numpy as np
from jax import lax
from jax.experimental import pallas as pl
from jax.experimental.pallas import tpu as pltpu
from jax.sharding import PartitionSpec as P

CH0 = 1024
LANES = 128
CHANNEL_BLOCK = 32
K_BLOCK = 2048
VMEM_LIMIT = 60 * 1024 * 1024
NT = (((1,), (1,)), ((), ()))


def phase_table(frame_len, channel_count, first_channel):
    channels = first_channel + np.arange(channel_count, dtype=np.int64)
    phases = (channels[:, None] * np.arange(frame_len, dtype=np.int64)[None, :]) % frame_len
    angles = 2.0 * math.pi / frame_len * phases
    parts = np.stack([np.cos(angles), -np.sin(angles)]) * frame_len**-0.5
    blocks = parts.reshape(2, channel_count // CHANNEL_BLOCK, CHANNEL_BLOCK, frame_len)
    return blocks.transpose(1, 0, 2, 3).reshape(-1, 2 * CHANNEL_BLOCK, frame_len).astype(np.float32)


def channelize_kernel(frame_count, x_hbm, coef_hbm, table_hbm, out_ref, x_in, coef_in, table_in, even, odd, total, turned, sems):
    block = pl.program_id(0)
    chunks, taps, k_block = coef_in.shape
    rows = table_in.shape[1]
    columns = x_in.shape[1]

    def table_copy(chunk):
        lanes = pl.ds(chunk * k_block, k_block)
        return pltpu.make_async_copy(table_hbm.at[block, :, lanes], table_in.at[chunk], sems.at[0, chunk])

    def coef_copy(chunk):
        lanes = pl.ds(chunk * k_block, k_block)
        return pltpu.make_async_copy(coef_hbm.at[:, lanes], coef_in.at[chunk], sems.at[1, chunk])

    def x_copy(chunk):
        lanes = pl.ds(chunk * k_block, k_block)
        return pltpu.make_async_copy(x_hbm.at[:, lanes], x_in.at[chunk], sems.at[2, chunk])

    def start_operands(chunk):
        coef_copy(chunk).start()
        table_copy(chunk).start()

    def wait_operands(chunk):
        coef_copy(chunk).wait()
        table_copy(chunk).wait()

    def fold(chunk):
        into = folded[chunk % 2]
        table = table_in[chunk]
        for tap in range(taps):
            coef = coef_in[chunk, tap : tap + 1, :]
            into[tap * rows : (tap + 1) * rows, :] = (table * coef).astype(jnp.bfloat16)

    def multiply(chunk):
        product = lax.dot_general(folded[chunk % 2][...], x_in[chunk], NT, preferred_element_type=jnp.float32)
        if chunk == 0:
            total[...] = product
        else:
            total[...] += product

    folded = (even, odd)
    start_operands(0)
    x_copy(0).start()
    start_operands(1)
    x_copy(1).start()
    wait_operands(0)
    fold(0)
    for chunk in range(chunks):
        if chunk + 2 < chunks:
            start_operands(chunk + 2)
            x_copy(chunk + 2).start()
        if chunk + 1 < chunks:
            wait_operands(chunk + 1)
        x_copy(chunk).wait()
        if chunk + 1 < chunks:
            fold(chunk + 1)
        multiply(chunk)

    half = rows // 2
    groups = columns // LANES
    slots = 4 * groups
    frame = lax.broadcasted_iota(jnp.int32, (rows, LANES), 1) % frame_count
    for group in range(groups):
        lanes = slice(group * LANES, (group + 1) * LANES)
        both = total[0:rows, lanes]
        own = both
        for tap in range(1, taps):
            moved = pltpu.roll(total[tap * rows : (tap + 1) * rows, lanes], LANES - tap, 1)
            both = both + moved
            own = own + jnp.where(frame < frame_count - tap, moved, 0.0)
        ahead = pltpu.roll(both - own, frame_count, 1)
        for part in range(2):
            turned[pl.ds(part * groups + group, half, stride=slots), :] = own[part * half : (part + 1) * half]
            turned[pl.ds((2 + part) * groups + group, half, stride=slots), :] = ahead[part * half : (part + 1) * half]
    out_ref[...] = turned[...].astype(jnp.bfloat16).reshape(out_ref.shape)


def channelize(samples, coefficients, channel_count):
    inputs, frame_count, frame_len = samples.shape
    taps = coefficients.shape[0]
    rows = 2 * CHANNEL_BLOCK
    columns = inputs * frame_count
    blocks = channel_count // CHANNEL_BLOCK
    slots = 4 * columns // LANES
    k_block = min(K_BLOCK, frame_len // 2)
    chunks = frame_len // k_block
    table = jnp.asarray(phase_table(frame_len, channel_count, CH0))
    return pl.pallas_call(
        functools.partial(channelize_kernel, frame_count),
        grid=(blocks,),
        in_specs=[pl.BlockSpec(memory_space=pltpu.HBM)] * 3,
        out_specs=pl.BlockSpec((CHANNEL_BLOCK, slots, LANES), lambda b: (b, 0, 0)),
        out_shape=jax.ShapeDtypeStruct((channel_count, slots, LANES), jnp.bfloat16),
        scratch_shapes=[
            pltpu.VMEM((chunks, columns, k_block), jnp.bfloat16),
            pltpu.VMEM((chunks, taps, k_block), jnp.float32),
            pltpu.VMEM((chunks, rows, k_block), jnp.float32),
            pltpu.VMEM((taps * rows, k_block), jnp.bfloat16),
            pltpu.VMEM((taps * rows, k_block), jnp.bfloat16),
            pltpu.VMEM((taps * rows, columns), jnp.float32),
            pltpu.VMEM((CHANNEL_BLOCK * slots, LANES), jnp.float32),
            pltpu.SemaphoreType.DMA((3, chunks)),
        ],
        compiler_params=pltpu.CompilerParams(
            dimension_semantics=("arbitrary",), vmem_limit_bytes=VMEM_LIMIT
        ),
        cost_estimate=pl.CostEstimate(
            flops=2 * channel_count * 2 * taps * columns * frame_len,
            bytes_accessed=2 * columns * frame_len,
            transcendentals=0,
        ),
        name="channelize",
    )(samples.reshape(columns, frame_len), coefficients, table)


def correlate_kernel(frame_count, st_count, ta_count, in_ref, out_ref, spectra):
    slots = in_ref.shape[1]
    half = slots // 2
    groups = half // 2
    per_row = LANES // frame_count
    all_inputs = st_count * groups * per_row
    position = lax.broadcasted_iota(jnp.int32, (half, LANES), 1) // frame_count

    def station(st, _):
        sums = []
        for ta in range(ta_count):
            block = in_ref[st * ta_count + ta].astype(jnp.float32)
            value = block[:half]
            if ta < ta_count - 1:
                value = value + in_ref[st * ta_count + ta + 1].astype(jnp.float32)[half:]
            sums.append(value)
        for column in range(ta_count * frame_count // LANES):
            for slot in range(per_row):
                result = None
                for place in range(per_row):
                    value = sums[column * per_row + place]
                    shift = ((place - slot) * frame_count) % LANES
                    if shift:
                        value = pltpu.roll(value, shift, 1)
                    result = value if result is None else jnp.where(position == place, value, result)
                for part in range(2):
                    first = part * all_inputs + st * groups * per_row + slot
                    spectra[pl.ds(first, groups, stride=per_row), column * LANES : (column + 1) * LANES] = result[
                        part * groups : (part + 1) * groups
                    ]
        return 0

    if st_count <= 8:
        for st in range(st_count):
            station(st, 0)
    else:
        lax.fori_loop(0, st_count, station, 0)
    real_part = spectra[:all_inputs, :].astype(jnp.bfloat16)
    imag_part = spectra[all_inputs:, :].astype(jnp.bfloat16)
    right = jnp.concatenate([real_part, imag_part], 1)
    left = jnp.concatenate([imag_part, -real_part], 1)
    scale = 1.0 / (ta_count * frame_count)
    for part, rows in enumerate((right, left)):
        product = lax.dot_general(rows, right, NT, preferred_element_type=jnp.float32)
        out_ref[0, part] = (product * scale).astype(jnp.bfloat16)


def correlate(arrived, frame_count, st_count, ta_count, all_inputs):
    return pl.pallas_call(
        functools.partial(correlate_kernel, frame_count, st_count, ta_count),
        in_specs=[pl.BlockSpec(memory_space=pltpu.VMEM)],
        out_specs=pl.BlockSpec(memory_space=pltpu.VMEM),
        out_shape=jax.ShapeDtypeStruct((1, 2, all_inputs, all_inputs), jnp.bfloat16),
        scratch_shapes=[pltpu.VMEM((2 * all_inputs, ta_count * frame_count), jnp.float32)],
        compiler_params=pltpu.CompilerParams(vmem_limit_bytes=32 * 1024 * 1024),
        name="correlate",
    )(arrived)


def on_device(samples, coefficients):
    st_count = lax.axis_size("st")
    ta_count = lax.axis_size("ta")
    inputs, frame_count, _ = samples.shape
    partial = channelize(samples, coefficients, st_count * ta_count)
    arrived = lax.all_to_all(partial, ("st", "ta"), split_axis=0, concat_axis=0, tiled=True)
    return correlate(arrived, frame_count, st_count, ta_count, st_count * inputs)


def solution(mesh):
    return jax.shard_map(
        on_device,
        mesh=mesh,
        in_specs=(P("st", "ta", None), P()),
        out_specs=P(("st", "ta"), None, None, None),
        check_vma=False,
    )
```

```python
import functools
import math

import jax
import jax.numpy as jnp
import numpy as np
from jax import lax
from jax.experimental import pallas as pl
from jax.experimental.pallas import tpu as pltpu
from jax.sharding import PartitionSpec as P

CH0 = 1024
LANES = 128
CHANNEL_BLOCK = 32
K_BLOCK = 2048
VMEM_LIMIT = 60 * 1024 * 1024
NT = (((1,), (1,)), ((), ()))


def phase_table(frame_len, channel_count, first_channel):
    channels = first_channel + np.arange(channel_count, dtype=np.int64)
    phases = (channels[:, None] * np.arange(frame_len, dtype=np.int64)[None, :]) % frame_len
    angles = 2.0 * math.pi / frame_len * phases
    parts = np.stack([np.cos(angles), -np.sin(angles)]) * frame_len**-0.5
    blocks = parts.reshape(2, channel_count // CHANNEL_BLOCK, CHANNEL_BLOCK, frame_len)
    return blocks.transpose(1, 0, 2, 3).reshape(-1, 2 * CHANNEL_BLOCK, frame_len).astype(jnp.bfloat16)


def channelize_kernel(frame_count, x_ref, coef_ref, table_ref, out_ref, folded, total, turned):
    step = pl.program_id(1)
    taps = coef_ref.shape[0]
    rows = table_ref.shape[1]
    table = table_ref[0]
    for tap in range(taps):
        folded[tap * rows : (tap + 1) * rows, :] = table * coef_ref[tap : tap + 1, :].astype(jnp.bfloat16)
    product = lax.dot_general(folded[...], x_ref[...], NT, preferred_element_type=jnp.float32)

    @pl.when(step == 0)
    def _():
        total[...] = product

    @pl.when(step > 0)
    def _():
        total[...] += product

    @pl.when(step == pl.num_programs(1) - 1)
    def _():
        half = rows // 2
        groups = total.shape[1] // LANES
        slots = 4 * groups
        frame = lax.broadcasted_iota(jnp.int32, (rows, LANES), 1) % frame_count
        for group in range(groups):
            lanes = slice(group * LANES, (group + 1) * LANES)
            both = total[0:rows, lanes]
            own = both
            for tap in range(1, taps):
                moved = pltpu.roll(total[tap * rows : (tap + 1) * rows, lanes], LANES - tap, 1)
                both = both + moved
                own = own + jnp.where(frame < frame_count - tap, moved, 0.0)
            ahead = pltpu.roll(both - own, frame_count, 1)
            for part in range(2):
                turned[pl.ds(part * groups + group, half, stride=slots), :] = own[part * half : (part + 1) * half]
                turned[pl.ds((2 + part) * groups + group, half, stride=slots), :] = ahead[
                    part * half : (part + 1) * half
                ]
        out_ref[...] = turned[...].astype(jnp.bfloat16).reshape(out_ref.shape)


def channelize(samples, coefficients, channel_count):
    inputs, frame_count, frame_len = samples.shape
    taps = coefficients.shape[0]
    rows = 2 * CHANNEL_BLOCK
    columns = inputs * frame_count
    blocks = channel_count // CHANNEL_BLOCK
    slots = 4 * columns // LANES
    k_block = min(K_BLOCK, frame_len)
    table = jnp.asarray(phase_table(frame_len, channel_count, CH0))
    return pl.pallas_call(
        functools.partial(channelize_kernel, frame_count),
        grid=(blocks, frame_len // k_block),
        in_specs=[
            pl.BlockSpec((columns, k_block), lambda b, k: (0, k)),
            pl.BlockSpec((taps, k_block), lambda b, k: (0, k)),
            pl.BlockSpec((1, rows, k_block), lambda b, k: (b, 0, k)),
        ],
        out_specs=pl.BlockSpec((CHANNEL_BLOCK, slots, LANES), lambda b, k: (b, 0, 0)),
        out_shape=jax.ShapeDtypeStruct((channel_count, slots, LANES), jnp.bfloat16),
        scratch_shapes=[
            pltpu.VMEM((taps * rows, k_block), jnp.bfloat16),
            pltpu.VMEM((taps * rows, columns), jnp.float32),
            pltpu.VMEM((CHANNEL_BLOCK * slots, LANES), jnp.float32),
        ],
        compiler_params=pltpu.CompilerParams(
            dimension_semantics=("arbitrary", "arbitrary"), vmem_limit_bytes=VMEM_LIMIT
        ),
        cost_estimate=pl.CostEstimate(
            flops=2 * channel_count * 2 * taps * columns * frame_len,
            bytes_accessed=2 * columns * frame_len,
            transcendentals=0,
        ),
        name="channelize",
    )(samples.reshape(columns, frame_len), coefficients, table)


def correlate_kernel(frame_count, st_count, ta_count, in_ref, out_ref, spectra):
    slots = in_ref.shape[1]
    half = slots // 2
    groups = half // 2
    per_row = LANES // frame_count
    all_inputs = st_count * groups * per_row
    position = lax.broadcasted_iota(jnp.int32, (half, LANES), 1) // frame_count

    def station(st, _):
        sums = []
        for ta in range(ta_count):
            block = in_ref[st * ta_count + ta].astype(jnp.float32)
            value = block[:half]
            if ta < ta_count - 1:
                value = value + in_ref[st * ta_count + ta + 1].astype(jnp.float32)[half:]
            sums.append(value)
        for column in range(ta_count * frame_count // LANES):
            for slot in range(per_row):
                result = None
                for place in range(per_row):
                    value = sums[column * per_row + place]
                    shift = ((place - slot) * frame_count) % LANES
                    if shift:
                        value = pltpu.roll(value, shift, 1)
                    result = value if result is None else jnp.where(position == place, value, result)
                for part in range(2):
                    first = part * all_inputs + st * groups * per_row + slot
                    spectra[pl.ds(first, groups, stride=per_row), column * LANES : (column + 1) * LANES] = result[
                        part * groups : (part + 1) * groups
                    ]
        return 0

    if st_count <= 8:
        for st in range(st_count):
            station(st, 0)
    else:
        lax.fori_loop(0, st_count, station, 0)
    real_part = spectra[:all_inputs, :].astype(jnp.bfloat16)
    imag_part = spectra[all_inputs:, :].astype(jnp.bfloat16)
    right = jnp.concatenate([real_part, imag_part], 1)
    left = jnp.concatenate([imag_part, -real_part], 1)
    scale = 1.0 / (ta_count * frame_count)
    for part, rows in enumerate((right, left)):
        product = lax.dot_general(rows, right, NT, preferred_element_type=jnp.float32)
        out_ref[0, part] = (product * scale).astype(jnp.bfloat16)


def correlate(arrived, frame_count, st_count, ta_count, all_inputs):
    return pl.pallas_call(
        functools.partial(correlate_kernel, frame_count, st_count, ta_count),
        in_specs=[pl.BlockSpec(memory_space=pltpu.VMEM)],
        out_specs=pl.BlockSpec(memory_space=pltpu.VMEM),
        out_shape=jax.ShapeDtypeStruct((1, 2, all_inputs, all_inputs), jnp.bfloat16),
        scratch_shapes=[pltpu.VMEM((2 * all_inputs, ta_count * frame_count), jnp.float32)],
        compiler_params=pltpu.CompilerParams(vmem_limit_bytes=32 * 1024 * 1024),
        name="correlate",
    )(arrived)


def on_device(samples, coefficients):
    st_count = lax.axis_size("st")
    ta_count = lax.axis_size("ta")
    inputs, frame_count, _ = samples.shape
    partial = channelize(samples, coefficients, st_count * ta_count)
    arrived = lax.all_to_all(partial, ("st", "ta"), split_axis=0, concat_axis=0, tiled=True)
    return correlate(arrived, frame_count, st_count, ta_count, st_count * inputs)


def solution(mesh):
    return jax.shard_map(
        on_device,
        mesh=mesh,
        in_specs=(P("st", "ta", None), P()),
        out_specs=P(("st", "ta"), None, None, None),
        check_vma=False,
    )
```

```python
import functools
import math

import jax
import jax.numpy as jnp
import numpy as np
from jax import lax
from jax.experimental import pallas as pl
from jax.experimental.pallas import tpu as pltpu
from jax.sharding import PartitionSpec as P

CH0 = 1024
LANES = 128
CHANNEL_BLOCK = 32
K_BLOCK = 2048
TILE = 256
VMEM_LIMIT = 60 * 1024 * 1024
NT = (((1,), (1,)), ((), ()))


def phase_table(frame_len, channel_count, first_channel):
    channels = first_channel + np.arange(channel_count, dtype=np.int64)
    phases = (channels[:, None] * np.arange(frame_len, dtype=np.int64)[None, :]) % frame_len
    angles = 2.0 * math.pi / frame_len * phases
    parts = np.stack([np.cos(angles), -np.sin(angles)]) * frame_len**-0.5
    blocks = parts.reshape(2, channel_count // CHANNEL_BLOCK, CHANNEL_BLOCK, frame_len)
    return blocks.transpose(1, 0, 2, 3).reshape(-1, 2 * CHANNEL_BLOCK, frame_len).astype(np.float32)


def channelize_kernel(frame_count, x_ref, coef_ref, table_ref, out_ref, folded, total, turned):
    step = pl.program_id(1)
    taps = coef_ref.shape[0]
    rows = table_ref.shape[1]
    table = table_ref[0]
    for tap in range(taps):
        folded[tap * rows : (tap + 1) * rows, :] = (table * coef_ref[tap : tap + 1, :]).astype(jnp.bfloat16)

    @pl.when(step == 0)
    def _():
        total[...] = jnp.zeros_like(total)

    for first in range(0, taps * rows, TILE):
        for column in range(0, total.shape[1], TILE):
            product = lax.dot_general(
                folded[first : first + TILE, :], x_ref[column : column + TILE, :], NT, preferred_element_type=jnp.float32
            )
            total[first : first + TILE, column : column + TILE] += product

    @pl.when(step == pl.num_programs(1) - 1)
    def _():
        half = rows // 2
        groups = total.shape[1] // LANES
        slots = 4 * groups
        frame = lax.broadcasted_iota(jnp.int32, (rows, LANES), 1) % frame_count
        for group in range(groups):
            lanes = slice(group * LANES, (group + 1) * LANES)
            both = total[0:rows, lanes]
            own = both
            for tap in range(1, taps):
                moved = pltpu.roll(total[tap * rows : (tap + 1) * rows, lanes], LANES - tap, 1)
                both = both + moved
                own = own + jnp.where(frame < frame_count - tap, moved, 0.0)
            ahead = pltpu.roll(both - own, frame_count, 1)
            for part in range(2):
                turned[pl.ds(part * groups + group, half, stride=slots), :] = own[part * half : (part + 1) * half]
                turned[pl.ds((2 + part) * groups + group, half, stride=slots), :] = ahead[
                    part * half : (part + 1) * half
                ]
        out_ref[...] = turned[...].astype(jnp.bfloat16).reshape(out_ref.shape)


def channelize(samples, coefficients, channel_count):
    inputs, frame_count, frame_len = samples.shape
    taps = coefficients.shape[0]
    rows = 2 * CHANNEL_BLOCK
    columns = inputs * frame_count
    blocks = channel_count // CHANNEL_BLOCK
    slots = 4 * columns // LANES
    k_block = min(K_BLOCK, frame_len)
    table = jnp.asarray(phase_table(frame_len, channel_count, CH0))
    return pl.pallas_call(
        functools.partial(channelize_kernel, frame_count),
        grid=(blocks, frame_len // k_block),
        in_specs=[
            pl.BlockSpec((columns, k_block), lambda b, k: (0, k)),
            pl.BlockSpec((taps, k_block), lambda b, k: (0, k)),
            pl.BlockSpec((1, rows, k_block), lambda b, k: (b, 0, k)),
        ],
        out_specs=pl.BlockSpec((CHANNEL_BLOCK, slots, LANES), lambda b, k: (b, 0, 0)),
        out_shape=jax.ShapeDtypeStruct((channel_count, slots, LANES), jnp.bfloat16),
        scratch_shapes=[
            pltpu.VMEM((taps * rows, k_block), jnp.bfloat16),
            pltpu.VMEM((taps * rows, columns), jnp.float32),
            pltpu.VMEM((CHANNEL_BLOCK * slots, LANES), jnp.float32),
        ],
        compiler_params=pltpu.CompilerParams(
            dimension_semantics=("arbitrary", "arbitrary"), vmem_limit_bytes=VMEM_LIMIT
        ),
        cost_estimate=pl.CostEstimate(
            flops=2 * channel_count * 2 * taps * columns * frame_len,
            bytes_accessed=2 * columns * frame_len,
            transcendentals=0,
        ),
        name="channelize",
    )(samples.reshape(columns, frame_len), coefficients, table)


def correlate_kernel(frame_count, st_count, ta_count, in_ref, out_ref, spectra):
    slots = in_ref.shape[1]
    half = slots // 2
    groups = half // 2
    per_row = LANES // frame_count
    all_inputs = st_count * groups * per_row
    position = lax.broadcasted_iota(jnp.int32, (half, LANES), 1) // frame_count

    def station(st, _):
        sums = []
        for ta in range(ta_count):
            block = in_ref[st * ta_count + ta].astype(jnp.float32)
            value = block[:half]
            if ta < ta_count - 1:
                value = value + in_ref[st * ta_count + ta + 1].astype(jnp.float32)[half:]
            sums.append(value)
        for column in range(ta_count * frame_count // LANES):
            for slot in range(per_row):
                result = None
                for place in range(per_row):
                    value = sums[column * per_row + place]
                    shift = ((place - slot) * frame_count) % LANES
                    if shift:
                        value = pltpu.roll(value, shift, 1)
                    result = value if result is None else jnp.where(position == place, value, result)
                for part in range(2):
                    first = part * all_inputs + st * groups * per_row + slot
                    spectra[pl.ds(first, groups, stride=per_row), column * LANES : (column + 1) * LANES] = result[
                        part * groups : (part + 1) * groups
                    ]
        return 0

    if st_count <= 8:
        for st in range(st_count):
            station(st, 0)
    else:
        lax.fori_loop(0, st_count, station, 0)
    real_part = spectra[:all_inputs, :].astype(jnp.bfloat16)
    imag_part = spectra[all_inputs:, :].astype(jnp.bfloat16)
    right = jnp.concatenate([real_part, imag_part], 1)
    left = jnp.concatenate([imag_part, -real_part], 1)
    scale = 1.0 / (ta_count * frame_count)
    for part, rows in enumerate((right, left)):
        product = lax.dot_general(rows, right, NT, preferred_element_type=jnp.float32)
        out_ref[0, part] = (product * scale).astype(jnp.bfloat16)


def correlate(arrived, frame_count, st_count, ta_count, all_inputs):
    return pl.pallas_call(
        functools.partial(correlate_kernel, frame_count, st_count, ta_count),
        in_specs=[pl.BlockSpec(memory_space=pltpu.VMEM)],
        out_specs=pl.BlockSpec(memory_space=pltpu.VMEM),
        out_shape=jax.ShapeDtypeStruct((1, 2, all_inputs, all_inputs), jnp.bfloat16),
        scratch_shapes=[pltpu.VMEM((2 * all_inputs, ta_count * frame_count), jnp.float32)],
        compiler_params=pltpu.CompilerParams(vmem_limit_bytes=32 * 1024 * 1024),
        name="correlate",
    )(arrived)


def on_device(samples, coefficients):
    st_count = lax.axis_size("st")
    ta_count = lax.axis_size("ta")
    inputs, frame_count, _ = samples.shape
    partial = channelize(samples, coefficients, st_count * ta_count)
    arrived = lax.all_to_all(partial, ("st", "ta"), split_axis=0, concat_axis=0, tiled=True)
    return correlate(arrived, frame_count, st_count, ta_count, st_count * inputs)


def solution(mesh):
    return jax.shard_map(
        on_device,
        mesh=mesh,
        in_specs=(P("st", "ta", None), P()),
        out_specs=P(("st", "ta"), None, None, None),
        check_vma=False,
    )
```

```python
import functools
import math

import jax
import jax.numpy as jnp
import numpy as np
from jax import lax
from jax.experimental import pallas as pl
from jax.experimental.pallas import tpu as pltpu
from jax.sharding import PartitionSpec as P

CH0 = 1024
LANES = 128
CHANNEL_BLOCK = 32
K_BLOCK = 2048
VMEM_LIMIT = 60 * 1024 * 1024
NT = (((1,), (1,)), ((), ()))


def phase_table(frame_len, channel_count, first_channel):
    channels = first_channel + np.arange(channel_count, dtype=np.int64)
    phases = (channels[:, None] * np.arange(frame_len, dtype=np.int64)[None, :]) % frame_len
    angles = 2.0 * math.pi / frame_len * phases
    parts = np.stack([np.cos(angles), -np.sin(angles)]) * frame_len**-0.5
    blocks = parts.reshape(2, channel_count // CHANNEL_BLOCK, CHANNEL_BLOCK, frame_len)
    return blocks.transpose(1, 0, 2, 3).reshape(-1, 2 * CHANNEL_BLOCK, frame_len).astype(np.float32)


def channelize_kernel(frame_count, x_ref, coef_ref, table_ref, out_ref, halves, folded, total, turned):
    step = pl.program_id(1)
    taps = coef_ref.shape[0]
    half = taps // 2
    rows = table_ref.shape[1]
    pairs = frame_count // taps
    inputs = x_ref.shape[0] // frame_count

    for pair in range(pairs):
        for first in range(0, inputs, 2):
            blocks = []
            for place in (first, first + 1):
                row = place * frame_count + pair * taps
                blocks.append(x_ref[row : row + taps, :].astype(jnp.float32))
            even = jnp.concatenate([block[:half] for block in blocks], 0)
            odd = jnp.concatenate([block[half:] for block in blocks], 0)
            row = (pair * inputs + first) * half
            for kind, value in enumerate((even, odd, even + odd)):
                halves[kind, row : row + taps, :] = value.astype(jnp.bfloat16)

    table = table_ref[0]
    for tap in range(half):
        low = coef_ref[tap : tap + 1, :]
        high = coef_ref[half + tap : half + tap + 1, :]
        for kind, coef in enumerate((high, low, low + high)):
            folded[kind, tap * rows : (tap + 1) * rows, :] = (table * coef).astype(jnp.bfloat16)

    @pl.when(step == 0)
    def _():
        total[...] = jnp.zeros_like(total)

    for kind in range(3):
        total[kind] += lax.dot_general(folded[kind], halves[kind], NT, preferred_element_type=jnp.float32)

    @pl.when(step == pl.num_programs(1) - 1)
    def _():
        frame = lax.broadcasted_iota(jnp.int32, (rows, LANES), 1) % half

        def shifted_sum(kind, pair):
            lanes = slice(pair * LANES, (pair + 1) * LANES)
            both = total[kind, 0:rows, lanes]
            inside = both
            for tap in range(1, half):
                moved = pltpu.roll(total[kind, tap * rows : (tap + 1) * rows, lanes], LANES - tap, 1)
                both = both + moved
                inside = inside + jnp.where(frame < half - tap, moved, 0.0)
            return inside, both - inside

        inside = {}
        before = {}
        for pair in range(pairs):
            (p0, c0), (p1, c1), (p2, c2) = (shifted_sum(kind, pair) for kind in range(3))
            for place, now, carry in (
                (2 * pair - 1, p0, c0),
                (2 * pair, p2 - p0 - p1, c2 - c0 - c1),
                (2 * pair + 1, p1, c1),
            ):
                inside[place] = inside[place] + now if place in inside else now
                before[place - 1] = before[place - 1] + carry if place - 1 in before else carry
        count = 2 * pairs
        channels = rows // 2
        slots = 4 * count
        for place in range(-2, count):
            value = inside.get(place)
            if place in before:
                carry = pltpu.roll(before[place], half, 1)
                value = carry if value is None else value + carry
            for part in range(2):
                slot = part * count + place if place >= 0 else (3 + part) * count + place
                turned[pl.ds(slot, channels, stride=slots), :] = value[part * channels : (part + 1) * channels]
        nothing = jnp.zeros((channels, LANES), jnp.float32)
        for part in range(2):
            for place in range(count - 2):
                turned[pl.ds((2 + part) * count + place, channels, stride=slots), :] = nothing
        out_ref[...] = turned[...].astype(jnp.bfloat16).reshape(out_ref.shape)


def channelize(samples, coefficients, channel_count):
    inputs, frame_count, frame_len = samples.shape
    taps = coefficients.shape[0]
    half = taps // 2
    rows = 2 * CHANNEL_BLOCK
    columns = inputs * frame_count
    blocks = channel_count // CHANNEL_BLOCK
    slots = 4 * frame_count // half
    k_block = min(K_BLOCK, frame_len)
    assert inputs * half == LANES and frame_count % taps == 0
    table = jnp.asarray(phase_table(frame_len, channel_count, CH0))
    return pl.pallas_call(
        functools.partial(channelize_kernel, frame_count),
        grid=(blocks, frame_len // k_block),
        in_specs=[
            pl.BlockSpec((columns, k_block), lambda b, k: (0, k)),
            pl.BlockSpec((taps, k_block), lambda b, k: (0, k)),
            pl.BlockSpec((1, rows, k_block), lambda b, k: (b, 0, k)),
        ],
        out_specs=pl.BlockSpec((CHANNEL_BLOCK, slots, LANES), lambda b, k: (b, 0, 0)),
        out_shape=jax.ShapeDtypeStruct((channel_count, slots, LANES), jnp.bfloat16),
        scratch_shapes=[
            pltpu.VMEM((3, columns // 2, k_block), jnp.bfloat16),
            pltpu.VMEM((3, half * rows, k_block), jnp.bfloat16),
            pltpu.VMEM((3, half * rows, columns // 2), jnp.float32),
            pltpu.VMEM((CHANNEL_BLOCK * slots, LANES), jnp.float32),
        ],
        compiler_params=pltpu.CompilerParams(
            dimension_semantics=("arbitrary", "arbitrary"), vmem_limit_bytes=VMEM_LIMIT
        ),
        cost_estimate=pl.CostEstimate(
            flops=3 * channel_count * taps * columns * frame_len,
            bytes_accessed=2 * columns * frame_len,
            transcendentals=0,
        ),
        name="channelize",
    )(samples.reshape(columns, frame_len), coefficients, table)


def correlate_kernel(half, st_count, ta_count, in_ref, out_ref, arranged, across, spectra):
    slots = in_ref.shape[1] // 2
    count = slots // 2
    inputs = LANES // half
    places = ta_count * count
    stations = LANES // places
    all_inputs = st_count * inputs
    position = lax.broadcasted_iota(jnp.int32, (inputs, LANES), 1) // places

    def station_group(group):
        for place in range(stations):
            st = group * stations + place
            for ta in range(ta_count):
                value = in_ref[st * ta_count + ta].astype(jnp.float32)[:slots]
                if ta < ta_count - 1:
                    value = value + in_ref[st * ta_count + ta + 1].astype(jnp.float32)[slots:]
                for part in range(2):
                    row = place * places + ta * count
                    arranged[part, row : row + count, :] = value[part * count : (part + 1) * count]
        for part in range(2):
            across[part] = arranged[part].T
            by_frame = [across[part, pl.ds(frame, inputs, stride=half), :] for frame in range(half)]
            for place in range(stations):
                result = None
                for frame in range(half):
                    shift = ((frame - place) * places) % LANES
                    value = pltpu.roll(by_frame[frame], shift, 1) if shift else by_frame[frame]
                    result = value if result is None else jnp.where(position == frame, value, result)
                first = part * all_inputs + (group * stations + place) * inputs
                if not isinstance(first, int):
                    first = pl.multiple_of(first, inputs)
                spectra[pl.ds(first, inputs), :] = result

    if st_count == stations:
        station_group(0)
    else:
        lax.fori_loop(0, st_count // stations, lambda group, _: (station_group(group), 0)[1], 0)
    real_part = spectra[:all_inputs, :].astype(jnp.bfloat16)
    imag_part = spectra[all_inputs:, :].astype(jnp.bfloat16)
    right = jnp.concatenate([real_part, imag_part], 1)
    left = jnp.concatenate([imag_part, -real_part], 1)
    scale = 1.0 / LANES
    for part, rows in enumerate((right, left)):
        product = lax.dot_general(rows, right, NT, preferred_element_type=jnp.float32)
        out_ref[0, part] = (product * scale).astype(jnp.bfloat16)


def correlate(arrived, half, frame_count, st_count, ta_count, all_inputs):
    assert ta_count * frame_count == LANES
    return pl.pallas_call(
        functools.partial(correlate_kernel, half, st_count, ta_count),
        in_specs=[pl.BlockSpec(memory_space=pltpu.VMEM)],
        out_specs=pl.BlockSpec(memory_space=pltpu.VMEM),
        out_shape=jax.ShapeDtypeStruct((1, 2, all_inputs, all_inputs), jnp.bfloat16),
        scratch_shapes=[
            pltpu.VMEM((2, LANES, LANES), jnp.float32),
            pltpu.VMEM((2, LANES, LANES), jnp.float32),
            pltpu.VMEM((2 * all_inputs, LANES), jnp.float32),
        ],
        compiler_params=pltpu.CompilerParams(vmem_limit_bytes=32 * 1024 * 1024),
        name="correlate",
    )(arrived)


def on_device(samples, coefficients):
    st_count = lax.axis_size("st")
    ta_count = lax.axis_size("ta")
    inputs, frame_count, _ = samples.shape
    partial = channelize(samples, coefficients, st_count * ta_count)
    arrived = lax.all_to_all(partial, ("st", "ta"), split_axis=0, concat_axis=0, tiled=True)
    return correlate(arrived, coefficients.shape[0] // 2, frame_count, st_count, ta_count, st_count * inputs)


def solution(mesh):
    return jax.shard_map(
        on_device,
        mesh=mesh,
        in_specs=(P("st", "ta", None), P()),
        out_specs=P(("st", "ta"), None, None, None),
        check_vma=False,
    )
```

```python
import functools
import math

import jax
import jax.numpy as jnp
import numpy as np
from jax import lax
from jax.experimental import pallas as pl
from jax.experimental.pallas import tpu as pltpu
from jax.sharding import PartitionSpec as P

CH0 = 1024
LANES = 128
CHANNEL_BLOCK = 32
K_BLOCK = 2048
VMEM_LIMIT = 60 * 1024 * 1024
NT = (((1,), (1,)), ((), ()))


def phase_table(frame_len, channel_count, first_channel):
    channels = first_channel + np.arange(channel_count, dtype=np.int64)
    phases = (channels[:, None] * np.arange(frame_len, dtype=np.int64)[None, :]) % frame_len
    angles = 2.0 * math.pi / frame_len * phases
    parts = np.stack([np.cos(angles), -np.sin(angles)]) * frame_len**-0.5
    blocks = parts.reshape(2, channel_count // CHANNEL_BLOCK, CHANNEL_BLOCK, frame_len)
    return blocks.transpose(1, 0, 2, 3).reshape(-1, 2 * CHANNEL_BLOCK, frame_len).astype(np.float32)


def channelize_kernel(frame_count, x_ref, coef_ref, table_ref, out_ref, total, turned):
    step = pl.program_id(1)
    taps = coef_ref.shape[0]
    rows = table_ref.shape[1]
    table = table_ref[0]
    folded = jnp.concatenate(
        [(table * coef_ref[tap : tap + 1, :]).astype(jnp.bfloat16) for tap in range(taps)], 0
    )

    @pl.when(step == 0)
    def _():
        total[...] = jnp.zeros_like(total)

    total[...] += lax.dot_general(folded, x_ref[...], NT, preferred_element_type=jnp.float32)

    @pl.when(step == pl.num_programs(1) - 1)
    def _():
        half = rows // 2
        groups = total.shape[1] // LANES
        slots = 4 * groups
        frame = lax.broadcasted_iota(jnp.int32, (rows, LANES), 1) % frame_count
        for group in range(groups):
            lanes = slice(group * LANES, (group + 1) * LANES)
            both = total[0:rows, lanes]
            own = both
            for tap in range(1, taps):
                moved = pltpu.roll(total[tap * rows : (tap + 1) * rows, lanes], LANES - tap, 1)
                both = both + moved
                own = own + jnp.where(frame < frame_count - tap, moved, 0.0)
            ahead = pltpu.roll(both - own, frame_count, 1)
            for part in range(2):
                turned[pl.ds(part * groups + group, half, stride=slots), :] = own[part * half : (part + 1) * half]
                turned[pl.ds((2 + part) * groups + group, half, stride=slots), :] = ahead[
                    part * half : (part + 1) * half
                ]
        out_ref[...] = turned[...].astype(jnp.bfloat16).reshape(out_ref.shape)


def channelize(samples, coefficients, channel_count):
    inputs, frame_count, frame_len = samples.shape
    taps = coefficients.shape[0]
    rows = 2 * CHANNEL_BLOCK
    columns = inputs * frame_count
    blocks = channel_count // CHANNEL_BLOCK
    slots = 4 * columns // LANES
    k_block = min(K_BLOCK, frame_len)
    table = jnp.asarray(phase_table(frame_len, channel_count, CH0))
    return pl.pallas_call(
        functools.partial(channelize_kernel, frame_count),
        grid=(blocks, frame_len // k_block),
        in_specs=[
            pl.BlockSpec((columns, k_block), lambda b, k: (0, k)),
            pl.BlockSpec((taps, k_block), lambda b, k: (0, k)),
            pl.BlockSpec((1, rows, k_block), lambda b, k: (b, 0, k)),
        ],
        out_specs=pl.BlockSpec((CHANNEL_BLOCK, slots, LANES), lambda b, k: (b, 0, 0)),
        out_shape=jax.ShapeDtypeStruct((channel_count, slots, LANES), jnp.bfloat16),
        scratch_shapes=[
            pltpu.VMEM((taps * rows, columns), jnp.float32),
            pltpu.VMEM((CHANNEL_BLOCK * slots, LANES), jnp.float32),
        ],
        compiler_params=pltpu.CompilerParams(
            dimension_semantics=("arbitrary", "arbitrary"), vmem_limit_bytes=VMEM_LIMIT
        ),
        cost_estimate=pl.CostEstimate(
            flops=2 * channel_count * 2 * taps * columns * frame_len,
            bytes_accessed=2 * columns * frame_len,
            transcendentals=0,
        ),
        name="channelize",
    )(samples.reshape(columns, frame_len), coefficients, table)


def correlate_kernel(frame_count, st_count, ta_count, in_ref, out_ref, spectra):
    slots = in_ref.shape[1]
    half = slots // 2
    groups = half // 2
    per_row = LANES // frame_count
    all_inputs = st_count * groups * per_row
    position = lax.broadcasted_iota(jnp.int32, (half, LANES), 1) // frame_count

    def station(st, _):
        sums = []
        for ta in range(ta_count):
            block = in_ref[st * ta_count + ta].astype(jnp.float32)
            value = block[:half]
            if ta < ta_count - 1:
                value = value + in_ref[st * ta_count + ta + 1].astype(jnp.float32)[half:]
            sums.append(value)
        for column in range(ta_count * frame_count // LANES):
            for slot in range(per_row):
                result = None
                for place in range(per_row):
                    value = sums[column * per_row + place]
                    shift = ((place - slot) * frame_count) % LANES
                    if shift:
                        value = pltpu.roll(value, shift, 1)
                    result = value if result is None else jnp.where(position == place, value, result)
                for part in range(2):
                    first = part * all_inputs + st * groups * per_row + slot
                    spectra[pl.ds(first, groups, stride=per_row), column * LANES : (column + 1) * LANES] = result[
                        part * groups : (part + 1) * groups
                    ]
        return 0

    if st_count <= 8:
        for st in range(st_count):
            station(st, 0)
    else:
        lax.fori_loop(0, st_count, station, 0)
    real_part = spectra[:all_inputs, :].astype(jnp.bfloat16)
    imag_part = spectra[all_inputs:, :].astype(jnp.bfloat16)
    right = jnp.concatenate([real_part, imag_part], 1)
    left = jnp.concatenate([imag_part, -real_part], 1)
    scale = 1.0 / (ta_count * frame_count)
    for part, rows in enumerate((right, left)):
        product = lax.dot_general(rows, right, NT, preferred_element_type=jnp.float32)
        out_ref[0, part] = (product * scale).astype(jnp.bfloat16)


def correlate(arrived, frame_count, st_count, ta_count, all_inputs):
    return pl.pallas_call(
        functools.partial(correlate_kernel, frame_count, st_count, ta_count),
        in_specs=[pl.BlockSpec(memory_space=pltpu.VMEM)],
        out_specs=pl.BlockSpec(memory_space=pltpu.VMEM),
        out_shape=jax.ShapeDtypeStruct((1, 2, all_inputs, all_inputs), jnp.bfloat16),
        scratch_shapes=[pltpu.VMEM((2 * all_inputs, ta_count * frame_count), jnp.float32)],
        compiler_params=pltpu.CompilerParams(vmem_limit_bytes=32 * 1024 * 1024),
        name="correlate",
    )(arrived)


def on_device(samples, coefficients):
    st_count = lax.axis_size("st")
    ta_count = lax.axis_size("ta")
    inputs, frame_count, _ = samples.shape
    partial = channelize(samples, coefficients, st_count * ta_count)
    arrived = lax.all_to_all(partial, ("st", "ta"), split_axis=0, concat_axis=0, tiled=True)
    return correlate(arrived, frame_count, st_count, ta_count, st_count * inputs)


def solution(mesh):
    return jax.shard_map(
        on_device,
        mesh=mesh,
        in_specs=(P("st", "ta", None), P()),
        out_specs=P(("st", "ta"), None, None, None),
        check_vma=False,
    )
```

```python
import functools
import math

import jax
import jax.numpy as jnp
import numpy as np
from jax import lax
from jax.experimental import pallas as pl
from jax.experimental.pallas import tpu as pltpu
from jax.sharding import PartitionSpec as P

CH0 = 1024
LANES = 128
CHANNEL_BLOCK = 32
K_BLOCK = 2048
VMEM_LIMIT = 60 * 1024 * 1024
NT = (((1,), (1,)), ((), ()))


def phase_table(frame_len, channel_count, first_channel):
    channels = first_channel + np.arange(channel_count, dtype=np.int64)
    phases = (channels[:, None] * np.arange(frame_len, dtype=np.int64)[None, :]) % frame_len
    angles = 2.0 * math.pi / frame_len * phases
    parts = np.stack([np.cos(angles), -np.sin(angles)]) * frame_len**-0.5
    blocks = parts.reshape(2, channel_count // CHANNEL_BLOCK, CHANNEL_BLOCK, frame_len)
    return blocks.transpose(1, 0, 2, 3).reshape(-1, 2 * CHANNEL_BLOCK, frame_len).astype(np.float32)


def channelize_kernel(frame_count, x_ref, coef_ref, table_ref, out_ref, halves, folded, total, turned):
    step = pl.program_id(1)
    taps = coef_ref.shape[0]
    half = taps // 2
    rows = table_ref.shape[1]
    pairs = frame_count // taps
    inputs = x_ref.shape[0] // frame_count

    for pair in range(pairs):
        for first in range(0, inputs, 2):
            blocks = []
            for place in (first, first + 1):
                row = place * frame_count + pair * taps
                blocks.append(x_ref[row : row + taps, :].astype(jnp.float32))
            even = jnp.concatenate([block[:half] for block in blocks], 0)
            odd = jnp.concatenate([block[half:] for block in blocks], 0)
            row = (pair * inputs + first) * half
            for kind, value in enumerate((even, odd, even + odd)):
                halves[kind, row : row + taps, :] = value.astype(jnp.bfloat16)

    table = table_ref[0]
    for tap in range(half):
        low = coef_ref[tap : tap + 1, :]
        high = coef_ref[half + tap : half + tap + 1, :]
        for kind, coef in enumerate((high, low, low + high)):
            folded[kind, tap * rows : (tap + 1) * rows, :] = (table * coef).astype(jnp.bfloat16)

    products = [
        lax.dot_general(folded[kind], halves[kind], NT, preferred_element_type=jnp.float32) for kind in range(3)
    ]

    @pl.when(step == 0)
    def _():
        for kind in range(3):
            total[kind] = products[kind]

    @pl.when(step > 0)
    def _():
        for kind in range(3):
            total[kind] += products[kind]

    @pl.when(step == pl.num_programs(1) - 1)
    def _():
        frame = lax.broadcasted_iota(jnp.int32, (rows, LANES), 1) % half

        def shifted_sum(kind, pair):
            lanes = slice(pair * LANES, (pair + 1) * LANES)
            both = total[kind, 0:rows, lanes]
            inside = both
            for tap in range(1, half):
                moved = pltpu.roll(total[kind, tap * rows : (tap + 1) * rows, lanes], LANES - tap, 1)
                both = both + moved
                inside = inside + jnp.where(frame < half - tap, moved, 0.0)
            return inside, both - inside

        inside = {}
        before = {}
        for pair in range(pairs):
            (p0, c0), (p1, c1), (p2, c2) = (shifted_sum(kind, pair) for kind in range(3))
            for place, now, carry in (
                (2 * pair - 1, p0, c0),
                (2 * pair, p2 - p0 - p1, c2 - c0 - c1),
                (2 * pair + 1, p1, c1),
            ):
                inside[place] = inside[place] + now if place in inside else now
                before[place - 1] = before[place - 1] + carry if place - 1 in before else carry
        count = 2 * pairs
        channels = rows // 2
        slots = 4 * count
        for place in range(-2, count):
            value = inside.get(place)
            if place in before:
                carry = pltpu.roll(before[place], half, 1)
                value = carry if value is None else value + carry
            for part in range(2):
                slot = part * count + place if place >= 0 else (3 + part) * count + place
                turned[pl.ds(slot, channels, stride=slots), :] = value[part * channels : (part + 1) * channels]
        nothing = jnp.zeros((channels, LANES), jnp.float32)
        for part in range(2):
            for place in range(count - 2):
                turned[pl.ds((2 + part) * count + place, channels, stride=slots), :] = nothing
        out_ref[...] = turned[...].astype(jnp.bfloat16).reshape(out_ref.shape)


def channelize(samples, coefficients, channel_count):
    inputs, frame_count, frame_len = samples.shape
    taps = coefficients.shape[0]
    half = taps // 2
    rows = 2 * CHANNEL_BLOCK
    columns = inputs * frame_count
    blocks = channel_count // CHANNEL_BLOCK
    slots = 4 * frame_count // half
    k_block = min(K_BLOCK, frame_len)
    assert inputs * half == LANES and frame_count % taps == 0
    table = jnp.asarray(phase_table(frame_len, channel_count, CH0))
    return pl.pallas_call(
        functools.partial(channelize_kernel, frame_count),
        grid=(blocks, frame_len // k_block),
        in_specs=[
            pl.BlockSpec((columns, k_block), lambda b, k: (0, k)),
            pl.BlockSpec((taps, k_block), lambda b, k: (0, k)),
            pl.BlockSpec((1, rows, k_block), lambda b, k: (b, 0, k)),
        ],
        out_specs=pl.BlockSpec((CHANNEL_BLOCK, slots, LANES), lambda b, k: (b, 0, 0)),
        out_shape=jax.ShapeDtypeStruct((channel_count, slots, LANES), jnp.bfloat16),
        scratch_shapes=[
            pltpu.VMEM((3, columns // 2, k_block), jnp.bfloat16),
            pltpu.VMEM((3, half * rows, k_block), jnp.bfloat16),
            pltpu.VMEM((3, half * rows, columns // 2), jnp.float32),
            pltpu.VMEM((CHANNEL_BLOCK * slots, LANES), jnp.float32),
        ],
        compiler_params=pltpu.CompilerParams(
            dimension_semantics=("arbitrary", "arbitrary"), vmem_limit_bytes=VMEM_LIMIT
        ),
        cost_estimate=pl.CostEstimate(
            flops=3 * channel_count * taps * columns * frame_len,
            bytes_accessed=2 * columns * frame_len,
            transcendentals=0,
        ),
        name="channelize",
    )(samples.reshape(columns, frame_len), coefficients, table)


def correlate_kernel(half, st_count, ta_count, in_ref, out_ref, arranged, across, spectra):
    slots = in_ref.shape[1] // 2
    count = slots // 2
    inputs = LANES // half
    places = ta_count * count
    stations = LANES // places
    all_inputs = st_count * inputs
    position = lax.broadcasted_iota(jnp.int32, (inputs, LANES), 1) // places

    def station_group(group):
        for place in range(stations):
            st = group * stations + place
            for ta in range(ta_count):
                value = in_ref[st * ta_count + ta].astype(jnp.float32)[:slots]
                if ta < ta_count - 1:
                    value = value + in_ref[st * ta_count + ta + 1].astype(jnp.float32)[slots:]
                for part in range(2):
                    row = place * places + ta * count
                    arranged[part, row : row + count, :] = value[part * count : (part + 1) * count]
        for part in range(2):
            across[part] = arranged[part].T
            by_frame = [across[part, pl.ds(frame, inputs, stride=half), :] for frame in range(half)]
            for place in range(stations):
                result = None
                for frame in range(half):
                    shift = ((frame - place) * places) % LANES
                    value = pltpu.roll(by_frame[frame], shift, 1) if shift else by_frame[frame]
                    result = value if result is None else jnp.where(position == frame, value, result)
                first = part * all_inputs + (group * stations + place) * inputs
                if not isinstance(first, int):
                    first = pl.multiple_of(first, inputs)
                spectra[pl.ds(first, inputs), :] = result

    if st_count == stations:
        station_group(0)
    else:
        lax.fori_loop(0, st_count // stations, lambda group, _: (station_group(group), 0)[1], 0)
    real_part = spectra[:all_inputs, :].astype(jnp.bfloat16)
    imag_part = spectra[all_inputs:, :].astype(jnp.bfloat16)
    right = jnp.concatenate([real_part, imag_part], 1)
    left = jnp.concatenate([imag_part, -real_part], 1)
    scale = 1.0 / LANES
    for part, rows in enumerate((right, left)):
        product = lax.dot_general(rows, right, NT, preferred_element_type=jnp.float32)
        out_ref[0, part] = (product * scale).astype(jnp.bfloat16)


def correlate(arrived, half, frame_count, st_count, ta_count, all_inputs):
    assert ta_count * frame_count == LANES
    return pl.pallas_call(
        functools.partial(correlate_kernel, half, st_count, ta_count),
        in_specs=[pl.BlockSpec(memory_space=pltpu.VMEM)],
        out_specs=pl.BlockSpec(memory_space=pltpu.VMEM),
        out_shape=jax.ShapeDtypeStruct((1, 2, all_inputs, all_inputs), jnp.bfloat16),
        scratch_shapes=[
            pltpu.VMEM((2, LANES, LANES), jnp.float32),
            pltpu.VMEM((2, LANES, LANES), jnp.float32),
            pltpu.VMEM((2 * all_inputs, LANES), jnp.float32),
        ],
        compiler_params=pltpu.CompilerParams(vmem_limit_bytes=32 * 1024 * 1024),
        name="correlate",
    )(arrived)


def on_device(samples, coefficients):
    st_count = lax.axis_size("st")
    ta_count = lax.axis_size("ta")
    inputs, frame_count, _ = samples.shape
    partial = channelize(samples, coefficients, st_count * ta_count)
    arrived = lax.all_to_all(partial, ("st", "ta"), split_axis=0, concat_axis=0, tiled=True)
    return correlate(arrived, coefficients.shape[0] // 2, frame_count, st_count, ta_count, st_count * inputs)


def solution(mesh):
    return jax.shard_map(
        on_device,
        mesh=mesh,
        in_specs=(P("st", "ta", None), P()),
        out_specs=P(("st", "ta"), None, None, None),
        check_vma=False,
    )
```

```python
import functools
import math

import jax
import jax.numpy as jnp
import numpy as np
from jax import lax
from jax.experimental import pallas as pl
from jax.experimental.pallas import tpu as pltpu
from jax.sharding import PartitionSpec as P

CH0 = 1024
LANES = 128
CHANNEL_BLOCK = 32
K_BLOCK = 2048
VMEM_LIMIT = 60 * 1024 * 1024
NT = (((1,), (1,)), ((), ()))


def phase_table(frame_len, channel_count, first_channel):
    channels = first_channel + np.arange(channel_count, dtype=np.int64)
    phases = (channels[:, None] * np.arange(frame_len, dtype=np.int64)[None, :]) % frame_len
    angles = 2.0 * math.pi / frame_len * phases
    parts = np.stack([np.cos(angles), -np.sin(angles)]) * frame_len**-0.5
    blocks = parts.reshape(2, channel_count // CHANNEL_BLOCK, CHANNEL_BLOCK, frame_len)
    return blocks.transpose(1, 0, 2, 3).reshape(-1, 2 * CHANNEL_BLOCK, frame_len).astype(np.float32)


def channelize_kernel(frame_count, x_ref, coef_ref, table_ref, out_ref, halves, folded, total, turned):
    step = pl.program_id(1)
    taps = coef_ref.shape[0]
    half = taps // 2
    rows = table_ref.shape[1]
    pairs = frame_count // taps
    inputs = x_ref.shape[0] // frame_count

    for pair in range(pairs):
        for first in range(0, inputs, 2):
            blocks = []
            for place in (first, first + 1):
                row = place * frame_count + pair * taps
                blocks.append(x_ref[row : row + taps, :].astype(jnp.float32))
            even = jnp.concatenate([block[:half] for block in blocks], 0)
            odd = jnp.concatenate([block[half:] for block in blocks], 0)
            row = (pair * inputs + first) * half
            for kind, value in enumerate((even, odd, even + odd)):
                halves[kind, row : row + taps, :] = value.astype(jnp.bfloat16)

    table = table_ref[0]
    for tap in range(half):
        low = coef_ref[tap : tap + 1, :]
        high = coef_ref[half + tap : half + tap + 1, :]
        for kind, coef in enumerate((high, low, low + high)):
            folded[kind, tap * rows : (tap + 1) * rows, :] = (table * coef).astype(jnp.bfloat16)

    for kind in range(3):
        total[step, kind] = lax.dot_general(
            folded[kind], halves[kind], NT, preferred_element_type=jnp.float32
        )

    @pl.when(step == pl.num_programs(1) - 1)
    def _():
        frame = lax.broadcasted_iota(jnp.int32, (rows, LANES), 1) % half

        def shifted_sum(kind, pair):
            lanes = slice(pair * LANES, (pair + 1) * LANES)

            def summed(tap):
                slots = [total[chunk, kind, tap * rows : (tap + 1) * rows, lanes] for chunk in range(total.shape[0])]
                return functools.reduce(jnp.add, slots)

            both = summed(0)
            inside = both
            for tap in range(1, half):
                moved = pltpu.roll(summed(tap), LANES - tap, 1)
                both = both + moved
                inside = inside + jnp.where(frame < half - tap, moved, 0.0)
            return inside, both - inside

        inside = {}
        before = {}
        for pair in range(pairs):
            (p0, c0), (p1, c1), (p2, c2) = (shifted_sum(kind, pair) for kind in range(3))
            for place, now, carry in (
                (2 * pair - 1, p0, c0),
                (2 * pair, p2 - p0 - p1, c2 - c0 - c1),
                (2 * pair + 1, p1, c1),
            ):
                inside[place] = inside[place] + now if place in inside else now
                before[place - 1] = before[place - 1] + carry if place - 1 in before else carry
        count = 2 * pairs
        channels = rows // 2
        slots = 4 * count
        for place in range(-2, count):
            value = inside.get(place)
            if place in before:
                carry = pltpu.roll(before[place], half, 1)
                value = carry if value is None else value + carry
            for part in range(2):
                slot = part * count + place if place >= 0 else (3 + part) * count + place
                turned[pl.ds(slot, channels, stride=slots), :] = value[part * channels : (part + 1) * channels]
        nothing = jnp.zeros((channels, LANES), jnp.float32)
        for part in range(2):
            for place in range(count - 2):
                turned[pl.ds((2 + part) * count + place, channels, stride=slots), :] = nothing
        out_ref[...] = turned[...].astype(jnp.bfloat16).reshape(out_ref.shape)


def channelize(samples, coefficients, channel_count):
    inputs, frame_count, frame_len = samples.shape
    taps = coefficients.shape[0]
    half = taps // 2
    rows = 2 * CHANNEL_BLOCK
    columns = inputs * frame_count
    blocks = channel_count // CHANNEL_BLOCK
    slots = 4 * frame_count // half
    k_block = min(K_BLOCK, frame_len)
    assert inputs * half == LANES and frame_count % taps == 0
    table = jnp.asarray(phase_table(frame_len, channel_count, CH0))
    return pl.pallas_call(
        functools.partial(channelize_kernel, frame_count),
        grid=(blocks, frame_len // k_block),
        in_specs=[
            pl.BlockSpec((columns, k_block), lambda b, k: (0, k)),
            pl.BlockSpec((taps, k_block), lambda b, k: (0, k)),
            pl.BlockSpec((1, rows, k_block), lambda b, k: (b, 0, k)),
        ],
        out_specs=pl.BlockSpec((CHANNEL_BLOCK, slots, LANES), lambda b, k: (b, 0, 0)),
        out_shape=jax.ShapeDtypeStruct((channel_count, slots, LANES), jnp.bfloat16),
        scratch_shapes=[
            pltpu.VMEM((3, columns // 2, k_block), jnp.bfloat16),
            pltpu.VMEM((3, half * rows, k_block), jnp.bfloat16),
            pltpu.VMEM((frame_len // k_block, 3, half * rows, columns // 2), jnp.float32),
            pltpu.VMEM((CHANNEL_BLOCK * slots, LANES), jnp.float32),
        ],
        compiler_params=pltpu.CompilerParams(
            dimension_semantics=("arbitrary", "arbitrary"), vmem_limit_bytes=VMEM_LIMIT
        ),
        cost_estimate=pl.CostEstimate(
            flops=3 * channel_count * taps * columns * frame_len,
            bytes_accessed=2 * columns * frame_len,
            transcendentals=0,
        ),
        name="channelize",
    )(samples.reshape(columns, frame_len), coefficients, table)


def correlate_kernel(half, st_count, ta_count, in_ref, out_ref, arranged, across, spectra):
    slots = in_ref.shape[1] // 2
    count = slots // 2
    inputs = LANES // half
    places = ta_count * count
    stations = LANES // places
    all_inputs = st_count * inputs
    position = lax.broadcasted_iota(jnp.int32, (inputs, LANES), 1) // places

    def station_group(group):
        for place in range(stations):
            st = group * stations + place
            for ta in range(ta_count):
                value = in_ref[st * ta_count + ta].astype(jnp.float32)[:slots]
                if ta < ta_count - 1:
                    value = value + in_ref[st * ta_count + ta + 1].astype(jnp.float32)[slots:]
                for part in range(2):
                    row = place * places + ta * count
                    arranged[part, row : row + count, :] = value[part * count : (part + 1) * count]
        for part in range(2):
            across[part] = arranged[part].T
            by_frame = [across[part, pl.ds(frame, inputs, stride=half), :] for frame in range(half)]
            for place in range(stations):
                result = None
                for frame in range(half):
                    shift = ((frame - place) * places) % LANES
                    value = pltpu.roll(by_frame[frame], shift, 1) if shift else by_frame[frame]
                    result = value if result is None else jnp.where(position == frame, value, result)
                first = part * all_inputs + (group * stations + place) * inputs
                if not isinstance(first, int):
                    first = pl.multiple_of(first, inputs)
                spectra[pl.ds(first, inputs), :] = result

    if st_count == stations:
        station_group(0)
    else:
        lax.fori_loop(0, st_count // stations, lambda group, _: (station_group(group), 0)[1], 0)
    real_part = spectra[:all_inputs, :].astype(jnp.bfloat16)
    imag_part = spectra[all_inputs:, :].astype(jnp.bfloat16)
    right = jnp.concatenate([real_part, imag_part], 1)
    left = jnp.concatenate([imag_part, -real_part], 1)
    scale = 1.0 / LANES
    for part, rows in enumerate((right, left)):
        product = lax.dot_general(rows, right, NT, preferred_element_type=jnp.float32)
        out_ref[0, part] = (product * scale).astype(jnp.bfloat16)


def correlate(arrived, half, frame_count, st_count, ta_count, all_inputs):
    assert ta_count * frame_count == LANES
    return pl.pallas_call(
        functools.partial(correlate_kernel, half, st_count, ta_count),
        in_specs=[pl.BlockSpec(memory_space=pltpu.VMEM)],
        out_specs=pl.BlockSpec(memory_space=pltpu.VMEM),
        out_shape=jax.ShapeDtypeStruct((1, 2, all_inputs, all_inputs), jnp.bfloat16),
        scratch_shapes=[
            pltpu.VMEM((2, LANES, LANES), jnp.float32),
            pltpu.VMEM((2, LANES, LANES), jnp.float32),
            pltpu.VMEM((2 * all_inputs, LANES), jnp.float32),
        ],
        compiler_params=pltpu.CompilerParams(vmem_limit_bytes=32 * 1024 * 1024),
        name="correlate",
    )(arrived)


def on_device(samples, coefficients):
    st_count = lax.axis_size("st")
    ta_count = lax.axis_size("ta")
    inputs, frame_count, _ = samples.shape
    partial = channelize(samples, coefficients, st_count * ta_count)
    arrived = lax.all_to_all(partial, ("st", "ta"), split_axis=0, concat_axis=0, tiled=True)
    return correlate(arrived, coefficients.shape[0] // 2, frame_count, st_count, ta_count, st_count * inputs)


def solution(mesh):
    return jax.shard_map(
        on_device,
        mesh=mesh,
        in_specs=(P("st", "ta", None), P()),
        out_specs=P(("st", "ta"), None, None, None),
        check_vma=False,
    )
```

```python
import functools
import math

import jax
import jax.numpy as jnp
import numpy as np
from jax import lax
from jax.experimental import pallas as pl
from jax.experimental.pallas import tpu as pltpu
from jax.sharding import PartitionSpec as P

CH0 = 1024
LANES = 128
CHANNEL_BLOCK = 32
K_BLOCK = 2048
VMEM_LIMIT = 60 * 1024 * 1024
NT = (((1,), (1,)), ((), ()))


def phase_table(frame_len, channel_count, first_channel):
    channels = first_channel + np.arange(channel_count, dtype=np.int64)
    phases = (channels[:, None] * np.arange(frame_len, dtype=np.int64)[None, :]) % frame_len
    angles = 2.0 * math.pi / frame_len * phases
    parts = np.stack([np.cos(angles), -np.sin(angles)]) * frame_len**-0.5
    blocks = parts.reshape(2, channel_count // CHANNEL_BLOCK, CHANNEL_BLOCK, frame_len)
    return blocks.transpose(1, 0, 2, 3).reshape(-1, 2 * CHANNEL_BLOCK, frame_len).astype(np.float32)


def channelize_kernel(frame_count, x_ref, coef_ref, table_ref, out_ref, halves, folded, total, turned):
    step = pl.program_id(1)
    taps = coef_ref.shape[0]
    half = taps // 2
    rows = table_ref.shape[1]
    pairs = frame_count // taps
    inputs = x_ref.shape[0] // frame_count

    table = table_ref[0]
    for kind in range(3):
        for pair in range(pairs):
            for first in range(0, inputs, 2):
                blocks = []
                for place in (first, first + 1):
                    row = place * frame_count + pair * taps
                    blocks.append(x_ref[row : row + taps, :].astype(jnp.float32))
                even = jnp.concatenate([block[:half] for block in blocks], 0)
                odd = jnp.concatenate([block[half:] for block in blocks], 0)
                row = (pair * inputs + first) * half
                halves[kind, row : row + taps, :] = (even, odd, even + odd)[kind].astype(jnp.bfloat16)
        for tap in range(half):
            low = coef_ref[tap : tap + 1, :]
            high = coef_ref[half + tap : half + tap + 1, :]
            coef = (high, low, low + high)[kind]
            folded[kind, tap * rows : (tap + 1) * rows, :] = (table * coef).astype(jnp.bfloat16)
        total[step, kind] = lax.dot_general(folded[kind], halves[kind], NT, preferred_element_type=jnp.float32)

    @pl.when(step == pl.num_programs(1) - 1)
    def _():
        frame = lax.broadcasted_iota(jnp.int32, (rows, LANES), 1) % half

        def shifted_sum(kind, pair):
            lanes = slice(pair * LANES, (pair + 1) * LANES)

            def summed(tap):
                slots = [total[chunk, kind, tap * rows : (tap + 1) * rows, lanes] for chunk in range(total.shape[0])]
                return functools.reduce(jnp.add, slots)

            both = summed(0)
            inside = both
            for tap in range(1, half):
                moved = pltpu.roll(summed(tap), LANES - tap, 1)
                both = both + moved
                inside = inside + jnp.where(frame < half - tap, moved, 0.0)
            return inside, both - inside

        inside = {}
        before = {}
        for pair in range(pairs):
            (p0, c0), (p1, c1), (p2, c2) = (shifted_sum(kind, pair) for kind in range(3))
            for place, now, carry in (
                (2 * pair - 1, p0, c0),
                (2 * pair, p2 - p0 - p1, c2 - c0 - c1),
                (2 * pair + 1, p1, c1),
            ):
                inside[place] = inside[place] + now if place in inside else now
                before[place - 1] = before[place - 1] + carry if place - 1 in before else carry
        count = 2 * pairs
        channels = rows // 2
        slots = 4 * count
        for place in range(-2, count):
            value = inside.get(place)
            if place in before:
                carry = pltpu.roll(before[place], half, 1)
                value = carry if value is None else value + carry
            for part in range(2):
                slot = part * count + place if place >= 0 else (3 + part) * count + place
                turned[pl.ds(slot, channels, stride=slots), :] = value[part * channels : (part + 1) * channels]
        nothing = jnp.zeros((channels, LANES), jnp.float32)
        for part in range(2):
            for place in range(count - 2):
                turned[pl.ds((2 + part) * count + place, channels, stride=slots), :] = nothing
        out_ref[...] = turned[...].astype(jnp.bfloat16).reshape(out_ref.shape)


def channelize(samples, coefficients, channel_count):
    inputs, frame_count, frame_len = samples.shape
    taps = coefficients.shape[0]
    half = taps // 2
    rows = 2 * CHANNEL_BLOCK
    columns = inputs * frame_count
    blocks = channel_count // CHANNEL_BLOCK
    slots = 4 * frame_count // half
    k_block = min(K_BLOCK, frame_len)
    assert inputs * half == LANES and frame_count % taps == 0
    table = jnp.asarray(phase_table(frame_len, channel_count, CH0))
    return pl.pallas_call(
        functools.partial(channelize_kernel, frame_count),
        grid=(blocks, frame_len // k_block),
        in_specs=[
            pl.BlockSpec((columns, k_block), lambda b, k: (0, k)),
            pl.BlockSpec((taps, k_block), lambda b, k: (0, k)),
            pl.BlockSpec((1, rows, k_block), lambda b, k: (b, 0, k)),
        ],
        out_specs=pl.BlockSpec((CHANNEL_BLOCK, slots, LANES), lambda b, k: (b, 0, 0)),
        out_shape=jax.ShapeDtypeStruct((channel_count, slots, LANES), jnp.bfloat16),
        scratch_shapes=[
            pltpu.VMEM((3, columns // 2, k_block), jnp.bfloat16),
            pltpu.VMEM((3, half * rows, k_block), jnp.bfloat16),
            pltpu.VMEM((frame_len // k_block, 3, half * rows, columns // 2), jnp.float32),
            pltpu.VMEM((CHANNEL_BLOCK * slots, LANES), jnp.float32),
        ],
        compiler_params=pltpu.CompilerParams(
            dimension_semantics=("arbitrary", "arbitrary"), vmem_limit_bytes=VMEM_LIMIT
        ),
        cost_estimate=pl.CostEstimate(
            flops=3 * channel_count * taps * columns * frame_len,
            bytes_accessed=2 * columns * frame_len,
            transcendentals=0,
        ),
        name="channelize",
    )(samples.reshape(columns, frame_len), coefficients, table)


def correlate_kernel(half, st_count, ta_count, in_ref, out_ref, arranged, across, spectra):
    slots = in_ref.shape[1] // 2
    count = slots // 2
    inputs = LANES // half
    places = ta_count * count
    stations = LANES // places
    all_inputs = st_count * inputs
    position = lax.broadcasted_iota(jnp.int32, (inputs, LANES), 1) // places

    def station_group(group):
        for place in range(stations):
            st = group * stations + place
            for ta in range(ta_count):
                value = in_ref[st * ta_count + ta].astype(jnp.float32)[:slots]
                if ta < ta_count - 1:
                    value = value + in_ref[st * ta_count + ta + 1].astype(jnp.float32)[slots:]
                for part in range(2):
                    row = place * places + ta * count
                    arranged[part, row : row + count, :] = value[part * count : (part + 1) * count]
        for part in range(2):
            across[part] = arranged[part].T
            by_frame = [across[part, pl.ds(frame, inputs, stride=half), :] for frame in range(half)]
            for place in range(stations):
                result = None
                for frame in range(half):
                    shift = ((frame - place) * places) % LANES
                    value = pltpu.roll(by_frame[frame], shift, 1) if shift else by_frame[frame]
                    result = value if result is None else jnp.where(position == frame, value, result)
                first = part * all_inputs + (group * stations + place) * inputs
                if not isinstance(first, int):
                    first = pl.multiple_of(first, inputs)
                spectra[pl.ds(first, inputs), :] = result

    if st_count == stations:
        station_group(0)
    else:
        lax.fori_loop(0, st_count // stations, lambda group, _: (station_group(group), 0)[1], 0)
    real_part = spectra[:all_inputs, :].astype(jnp.bfloat16)
    imag_part = spectra[all_inputs:, :].astype(jnp.bfloat16)
    right = jnp.concatenate([real_part, imag_part], 1)
    left = jnp.concatenate([imag_part, -real_part], 1)
    scale = 1.0 / LANES
    for part, rows in enumerate((right, left)):
        product = lax.dot_general(rows, right, NT, preferred_element_type=jnp.float32)
        out_ref[0, part] = (product * scale).astype(jnp.bfloat16)


def correlate(arrived, half, frame_count, st_count, ta_count, all_inputs):
    assert ta_count * frame_count == LANES
    return pl.pallas_call(
        functools.partial(correlate_kernel, half, st_count, ta_count),
        in_specs=[pl.BlockSpec(memory_space=pltpu.VMEM)],
        out_specs=pl.BlockSpec(memory_space=pltpu.VMEM),
        out_shape=jax.ShapeDtypeStruct((1, 2, all_inputs, all_inputs), jnp.bfloat16),
        scratch_shapes=[
            pltpu.VMEM((2, LANES, LANES), jnp.float32),
            pltpu.VMEM((2, LANES, LANES), jnp.float32),
            pltpu.VMEM((2 * all_inputs, LANES), jnp.float32),
        ],
        compiler_params=pltpu.CompilerParams(vmem_limit_bytes=32 * 1024 * 1024),
        name="correlate",
    )(arrived)


def on_device(samples, coefficients):
    st_count = lax.axis_size("st")
    ta_count = lax.axis_size("ta")
    inputs, frame_count, _ = samples.shape
    partial = channelize(samples, coefficients, st_count * ta_count)
    arrived = lax.all_to_all(partial, ("st", "ta"), split_axis=0, concat_axis=0, tiled=True)
    return correlate(arrived, coefficients.shape[0] // 2, frame_count, st_count, ta_count, st_count * inputs)


def solution(mesh):
    return jax.shard_map(
        on_device,
        mesh=mesh,
        in_specs=(P("st", "ta", None), P()),
        out_specs=P(("st", "ta"), None, None, None),
        check_vma=False,
    )
```

```python
import functools
import math

import jax
import jax.numpy as jnp
import numpy as np
from jax import lax
from jax.experimental import pallas as pl
from jax.experimental.pallas import tpu as pltpu
from jax.sharding import PartitionSpec as P

CH0 = 1024
LANES = 128
CHANNEL_BLOCK = 32
K_BLOCK = 2048
ROW_BLOCK = 256
VMEM_LIMIT = 60 * 1024 * 1024
NT = (((1,), (1,)), ((), ()))


def phase_table(frame_len, channel_count, first_channel):
    channels = first_channel + np.arange(channel_count, dtype=np.int64)
    phases = (channels[:, None] * np.arange(frame_len, dtype=np.int64)[None, :]) % frame_len
    angles = 2.0 * math.pi / frame_len * phases
    parts = np.stack([np.cos(angles), -np.sin(angles)]) * frame_len**-0.5
    blocks = parts.reshape(2, channel_count // CHANNEL_BLOCK, CHANNEL_BLOCK, frame_len)
    return blocks.transpose(1, 0, 2, 3).reshape(-1, 2 * CHANNEL_BLOCK, frame_len).astype(np.float32)


def channelize_kernel(frame_count, x_ref, coef_ref, table_ref, out_ref, halves, folded, total, turned):
    step = pl.program_id(1)
    taps = coef_ref.shape[0]
    half = taps // 2
    rows = table_ref.shape[1]
    pairs = frame_count // taps
    inputs = x_ref.shape[0] // frame_count

    table = table_ref[0]
    for kind in range(3):
        for pair in range(pairs):
            for first in range(0, inputs, 2):
                blocks = []
                for place in (first, first + 1):
                    row = place * frame_count + pair * taps
                    blocks.append(x_ref[row : row + taps, :].astype(jnp.float32))
                even = jnp.concatenate([block[:half] for block in blocks], 0)
                odd = jnp.concatenate([block[half:] for block in blocks], 0)
                row = (pair * inputs + first) * half
                halves[kind, row : row + taps, :] = (even, odd, even + odd)[kind].astype(jnp.bfloat16)
        for tap in range(half):
            low = coef_ref[tap : tap + 1, :]
            high = coef_ref[half + tap : half + tap + 1, :]
            coef = (high, low, low + high)[kind]
            folded[kind, tap * rows : (tap + 1) * rows, :] = (table * coef).astype(jnp.bfloat16)
        for first in range(0, half * rows, ROW_BLOCK):
            part = slice(first, first + ROW_BLOCK)
            total[step, kind, part, :] = lax.dot_general(
                folded[kind, part, :], halves[kind], NT, preferred_element_type=jnp.float32
            )

    @pl.when(step == pl.num_programs(1) - 1)
    def _():
        frame = lax.broadcasted_iota(jnp.int32, (rows, LANES), 1) % half

        def shifted_sum(kind, pair):
            lanes = slice(pair * LANES, (pair + 1) * LANES)

            def summed(tap):
                slots = [total[chunk, kind, tap * rows : (tap + 1) * rows, lanes] for chunk in range(total.shape[0])]
                return functools.reduce(jnp.add, slots)

            both = summed(0)
            inside = both
            for tap in range(1, half):
                moved = pltpu.roll(summed(tap), LANES - tap, 1)
                both = both + moved
                inside = inside + jnp.where(frame < half - tap, moved, 0.0)
            return inside, both - inside

        inside = {}
        before = {}
        for pair in range(pairs):
            (p0, c0), (p1, c1), (p2, c2) = (shifted_sum(kind, pair) for kind in range(3))
            for place, now, carry in (
                (2 * pair - 1, p0, c0),
                (2 * pair, p2 - p0 - p1, c2 - c0 - c1),
                (2 * pair + 1, p1, c1),
            ):
                inside[place] = inside[place] + now if place in inside else now
                before[place - 1] = before[place - 1] + carry if place - 1 in before else carry
        count = 2 * pairs
        channels = rows // 2
        slots = 4 * count
        for place in range(-2, count):
            value = inside.get(place)
            if place in before:
                carry = pltpu.roll(before[place], half, 1)
                value = carry if value is None else value + carry
            for part in range(2):
                slot = part * count + place if place >= 0 else (3 + part) * count + place
                turned[pl.ds(slot, channels, stride=slots), :] = value[part * channels : (part + 1) * channels]
        nothing = jnp.zeros((channels, LANES), jnp.float32)
        for part in range(2):
            for place in range(count - 2):
                turned[pl.ds((2 + part) * count + place, channels, stride=slots), :] = nothing
        out_ref[...] = turned[...].astype(jnp.bfloat16).reshape(out_ref.shape)


def channelize(samples, coefficients, channel_count):
    inputs, frame_count, frame_len = samples.shape
    taps = coefficients.shape[0]
    half = taps // 2
    rows = 2 * CHANNEL_BLOCK
    columns = inputs * frame_count
    blocks = channel_count // CHANNEL_BLOCK
    slots = 4 * frame_count // half
    k_block = min(K_BLOCK, frame_len)
    assert inputs * half == LANES and frame_count % taps == 0
    table = jnp.asarray(phase_table(frame_len, channel_count, CH0))
    return pl.pallas_call(
        functools.partial(channelize_kernel, frame_count),
        grid=(blocks, frame_len // k_block),
        in_specs=[
            pl.BlockSpec((columns, k_block), lambda b, k: (0, k)),
            pl.BlockSpec((taps, k_block), lambda b, k: (0, k)),
            pl.BlockSpec((1, rows, k_block), lambda b, k: (b, 0, k)),
        ],
        out_specs=pl.BlockSpec((CHANNEL_BLOCK, slots, LANES), lambda b, k: (b, 0, 0)),
        out_shape=jax.ShapeDtypeStruct((channel_count, slots, LANES), jnp.bfloat16),
        scratch_shapes=[
            pltpu.VMEM((3, columns // 2, k_block), jnp.bfloat16),
            pltpu.VMEM((3, half * rows, k_block), jnp.bfloat16),
            pltpu.VMEM((frame_len // k_block, 3, half * rows, columns // 2), jnp.float32),
            pltpu.VMEM((CHANNEL_BLOCK * slots, LANES), jnp.float32),
        ],
        compiler_params=pltpu.CompilerParams(
            dimension_semantics=("arbitrary", "arbitrary"), vmem_limit_bytes=VMEM_LIMIT
        ),
        cost_estimate=pl.CostEstimate(
            flops=3 * channel_count * taps * columns * frame_len,
            bytes_accessed=2 * columns * frame_len,
            transcendentals=0,
        ),
        name="channelize",
    )(samples.reshape(columns, frame_len), coefficients, table)


def correlate_kernel(half, st_count, ta_count, in_ref, out_ref, arranged, across, spectra):
    slots = in_ref.shape[1] // 2
    count = slots // 2
    inputs = LANES // half
    places = ta_count * count
    stations = LANES // places
    all_inputs = st_count * inputs
    position = lax.broadcasted_iota(jnp.int32, (inputs, LANES), 1) // places

    def station_group(group):
        for place in range(stations):
            st = group * stations + place
            for ta in range(ta_count):
                value = in_ref[st * ta_count + ta].astype(jnp.float32)[:slots]
                if ta < ta_count - 1:
                    value = value + in_ref[st * ta_count + ta + 1].astype(jnp.float32)[slots:]
                for part in range(2):
                    row = place * places + ta * count
                    arranged[part, row : row + count, :] = value[part * count : (part + 1) * count]
        for part in range(2):
            across[part] = arranged[part].T
            by_frame = [across[part, pl.ds(frame, inputs, stride=half), :] for frame in range(half)]
            for place in range(stations):
                result = None
                for frame in range(half):
                    shift = ((frame - place) * places) % LANES
                    value = pltpu.roll(by_frame[frame], shift, 1) if shift else by_frame[frame]
                    result = value if result is None else jnp.where(position == frame, value, result)
                first = part * all_inputs + (group * stations + place) * inputs
                if not isinstance(first, int):
                    first = pl.multiple_of(first, inputs)
                spectra[pl.ds(first, inputs), :] = result

    if st_count == stations:
        station_group(0)
    else:
        lax.fori_loop(0, st_count // stations, lambda group, _: (station_group(group), 0)[1], 0)
    real_part = spectra[:all_inputs, :].astype(jnp.bfloat16)
    imag_part = spectra[all_inputs:, :].astype(jnp.bfloat16)
    right = jnp.concatenate([real_part, imag_part], 1)
    left = jnp.concatenate([imag_part, -real_part], 1)
    scale = 1.0 / LANES
    for part, rows in enumerate((right, left)):
        product = lax.dot_general(rows, right, NT, preferred_element_type=jnp.float32)
        out_ref[0, part] = (product * scale).astype(jnp.bfloat16)


def correlate(arrived, half, frame_count, st_count, ta_count, all_inputs):
    assert ta_count * frame_count == LANES
    return pl.pallas_call(
        functools.partial(correlate_kernel, half, st_count, ta_count),
        in_specs=[pl.BlockSpec(memory_space=pltpu.VMEM)],
        out_specs=pl.BlockSpec(memory_space=pltpu.VMEM),
        out_shape=jax.ShapeDtypeStruct((1, 2, all_inputs, all_inputs), jnp.bfloat16),
        scratch_shapes=[
            pltpu.VMEM((2, LANES, LANES), jnp.float32),
            pltpu.VMEM((2, LANES, LANES), jnp.float32),
            pltpu.VMEM((2 * all_inputs, LANES), jnp.float32),
        ],
        compiler_params=pltpu.CompilerParams(vmem_limit_bytes=32 * 1024 * 1024),
        name="correlate",
    )(arrived)


def on_device(samples, coefficients):
    st_count = lax.axis_size("st")
    ta_count = lax.axis_size("ta")
    inputs, frame_count, _ = samples.shape
    partial = channelize(samples, coefficients, st_count * ta_count)
    arrived = lax.all_to_all(partial, ("st", "ta"), split_axis=0, concat_axis=0, tiled=True)
    return correlate(arrived, coefficients.shape[0] // 2, frame_count, st_count, ta_count, st_count * inputs)


def solution(mesh):
    return jax.shard_map(
        on_device,
        mesh=mesh,
        in_specs=(P("st", "ta", None), P()),
        out_specs=P(("st", "ta"), None, None, None),
        check_vma=False,
    )
```

```python
import functools
import math

import jax
import jax.numpy as jnp
import numpy as np
from jax import lax
from jax.experimental import pallas as pl
from jax.experimental.pallas import tpu as pltpu
from jax.sharding import PartitionSpec as P

CH0 = 1024
LANES = 128
CHANNEL_BLOCK = 32
K_BLOCK = 1024
VMEM_LIMIT = 60 * 1024 * 1024
NT = (((1,), (1,)), ((), ()))


def phase_table(frame_len, channel_count, first_channel):
    channels = first_channel + np.arange(channel_count, dtype=np.int64)
    phases = (channels[:, None] * np.arange(frame_len, dtype=np.int64)[None, :]) % frame_len
    angles = 2.0 * math.pi / frame_len * phases
    parts = np.stack([np.cos(angles), -np.sin(angles)]) * frame_len**-0.5
    blocks = parts.reshape(2, channel_count // CHANNEL_BLOCK, CHANNEL_BLOCK, frame_len)
    return blocks.transpose(1, 0, 2, 3).reshape(-1, 2 * CHANNEL_BLOCK, frame_len).astype(np.float32)


def channelize_kernel(frame_count, x_ref, coef_ref, table_ref, out_ref, halves, folded, total, turned):
    step = pl.program_id(1)
    taps = coef_ref.shape[0]
    half = taps // 2
    rows = table_ref.shape[1]
    pairs = frame_count // taps
    inputs = x_ref.shape[0] // frame_count

    table = table_ref[0]
    for kind in range(3):
        for pair in range(pairs):
            for first in range(0, inputs, 2):
                blocks = []
                for place in (first, first + 1):
                    row = place * frame_count + pair * taps
                    blocks.append(x_ref[row : row + taps, :].astype(jnp.float32))
                even = jnp.concatenate([block[:half] for block in blocks], 0)
                odd = jnp.concatenate([block[half:] for block in blocks], 0)
                row = (pair * inputs + first) * half
                halves[kind, row : row + taps, :] = (even, odd, even + odd)[kind].astype(jnp.bfloat16)
        for tap in range(half):
            low = coef_ref[tap : tap + 1, :]
            high = coef_ref[half + tap : half + tap + 1, :]
            coef = (high, low, low + high)[kind]
            folded[kind, tap * rows : (tap + 1) * rows, :] = (table * coef).astype(jnp.bfloat16)
        total[step, kind] = lax.dot_general(folded[kind], halves[kind], NT, preferred_element_type=jnp.float32)

    @pl.when(step == pl.num_programs(1) - 1)
    def _():
        frame = lax.broadcasted_iota(jnp.int32, (rows, LANES), 1) % half

        def shifted_sum(kind, pair):
            lanes = slice(pair * LANES, (pair + 1) * LANES)

            def summed(tap):
                slots = [total[chunk, kind, tap * rows : (tap + 1) * rows, lanes] for chunk in range(total.shape[0])]
                return functools.reduce(jnp.add, slots)

            both = summed(0)
            inside = both
            for tap in range(1, half):
                moved = pltpu.roll(summed(tap), LANES - tap, 1)
                both = both + moved
                inside = inside + jnp.where(frame < half - tap, moved, 0.0)
            return inside, both - inside

        inside = {}
        before = {}
        for pair in range(pairs):
            (p0, c0), (p1, c1), (p2, c2) = (shifted_sum(kind, pair) for kind in range(3))
            for place, now, carry in (
                (2 * pair - 1, p0, c0),
                (2 * pair, p2 - p0 - p1, c2 - c0 - c1),
                (2 * pair + 1, p1, c1),
            ):
                inside[place] = inside[place] + now if place in inside else now
                before[place - 1] = before[place - 1] + carry if place - 1 in before else carry
        count = 2 * pairs
        channels = rows // 2
        slots = 4 * count
        for place in range(-2, count):
            value = inside.get(place)
            if place in before:
                carry = pltpu.roll(before[place], half, 1)
                value = carry if value is None else value + carry
            for part in range(2):
                slot = part * count + place if place >= 0 else (3 + part) * count + place
                turned[pl.ds(slot, channels, stride=slots), :] = value[part * channels : (part + 1) * channels]
        nothing = jnp.zeros((channels, LANES), jnp.float32)
        for part in range(2):
            for place in range(count - 2):
                turned[pl.ds((2 + part) * count + place, channels, stride=slots), :] = nothing
        out_ref[...] = turned[...].astype(jnp.bfloat16).reshape(out_ref.shape)


def channelize(samples, coefficients, channel_count):
    inputs, frame_count, frame_len = samples.shape
    taps = coefficients.shape[0]
    half = taps // 2
    rows = 2 * CHANNEL_BLOCK
    columns = inputs * frame_count
    blocks = channel_count // CHANNEL_BLOCK
    slots = 4 * frame_count // half
    k_block = min(K_BLOCK, frame_len)
    assert inputs * half == LANES and frame_count % taps == 0
    table = jnp.asarray(phase_table(frame_len, channel_count, CH0))
    return pl.pallas_call(
        functools.partial(channelize_kernel, frame_count),
        grid=(blocks, frame_len // k_block),
        in_specs=[
            pl.BlockSpec((columns, k_block), lambda b, k: (0, k)),
            pl.BlockSpec((taps, k_block), lambda b, k: (0, k)),
            pl.BlockSpec((1, rows, k_block), lambda b, k: (b, 0, k)),
        ],
        out_specs=pl.BlockSpec((CHANNEL_BLOCK, slots, LANES), lambda b, k: (b, 0, 0)),
        out_shape=jax.ShapeDtypeStruct((channel_count, slots, LANES), jnp.bfloat16),
        scratch_shapes=[
            pltpu.VMEM((3, columns // 2, k_block), jnp.bfloat16),
            pltpu.VMEM((3, half * rows, k_block), jnp.bfloat16),
            pltpu.VMEM((frame_len // k_block, 3, half * rows, columns // 2), jnp.float32),
            pltpu.VMEM((CHANNEL_BLOCK * slots, LANES), jnp.float32),
        ],
        compiler_params=pltpu.CompilerParams(
            dimension_semantics=("arbitrary", "arbitrary"), vmem_limit_bytes=VMEM_LIMIT
        ),
        cost_estimate=pl.CostEstimate(
            flops=3 * channel_count * taps * columns * frame_len,
            bytes_accessed=2 * columns * frame_len,
            transcendentals=0,
        ),
        name="channelize",
    )(samples.reshape(columns, frame_len), coefficients, table)


def correlate_kernel(half, st_count, ta_count, in_ref, out_ref, arranged, across, spectra):
    slots = in_ref.shape[1] // 2
    count = slots // 2
    inputs = LANES // half
    places = ta_count * count
    stations = LANES // places
    all_inputs = st_count * inputs
    position = lax.broadcasted_iota(jnp.int32, (inputs, LANES), 1) // places

    def station_group(group):
        for place in range(stations):
            st = group * stations + place
            for ta in range(ta_count):
                value = in_ref[st * ta_count + ta].astype(jnp.float32)[:slots]
                if ta < ta_count - 1:
                    value = value + in_ref[st * ta_count + ta + 1].astype(jnp.float32)[slots:]
                for part in range(2):
                    row = place * places + ta * count
                    arranged[part, row : row + count, :] = value[part * count : (part + 1) * count]
        for part in range(2):
            across[part] = arranged[part].T
            by_frame = [across[part, pl.ds(frame, inputs, stride=half), :] for frame in range(half)]
            for place in range(stations):
                result = None
                for frame in range(half):
                    shift = ((frame - place) * places) % LANES
                    value = pltpu.roll(by_frame[frame], shift, 1) if shift else by_frame[frame]
                    result = value if result is None else jnp.where(position == frame, value, result)
                first = part * all_inputs + (group * stations + place) * inputs
                if not isinstance(first, int):
                    first = pl.multiple_of(first, inputs)
                spectra[pl.ds(first, inputs), :] = result

    if st_count == stations:
        station_group(0)
    else:
        lax.fori_loop(0, st_count // stations, lambda group, _: (station_group(group), 0)[1], 0)
    real_part = spectra[:all_inputs, :].astype(jnp.bfloat16)
    imag_part = spectra[all_inputs:, :].astype(jnp.bfloat16)
    right = jnp.concatenate([real_part, imag_part], 1)
    left = jnp.concatenate([imag_part, -real_part], 1)
    scale = 1.0 / LANES
    for part, rows in enumerate((right, left)):
        product = lax.dot_general(rows, right, NT, preferred_element_type=jnp.float32)
        out_ref[0, part] = (product * scale).astype(jnp.bfloat16)


def correlate(arrived, half, frame_count, st_count, ta_count, all_inputs):
    assert ta_count * frame_count == LANES
    return pl.pallas_call(
        functools.partial(correlate_kernel, half, st_count, ta_count),
        in_specs=[pl.BlockSpec(memory_space=pltpu.VMEM)],
        out_specs=pl.BlockSpec(memory_space=pltpu.VMEM),
        out_shape=jax.ShapeDtypeStruct((1, 2, all_inputs, all_inputs), jnp.bfloat16),
        scratch_shapes=[
            pltpu.VMEM((2, LANES, LANES), jnp.float32),
            pltpu.VMEM((2, LANES, LANES), jnp.float32),
            pltpu.VMEM((2 * all_inputs, LANES), jnp.float32),
        ],
        compiler_params=pltpu.CompilerParams(vmem_limit_bytes=32 * 1024 * 1024),
        name="correlate",
    )(arrived)


def on_device(samples, coefficients):
    st_count = lax.axis_size("st")
    ta_count = lax.axis_size("ta")
    inputs, frame_count, _ = samples.shape
    partial = channelize(samples, coefficients, st_count * ta_count)
    arrived = lax.all_to_all(partial, ("st", "ta"), split_axis=0, concat_axis=0, tiled=True)
    return correlate(arrived, coefficients.shape[0] // 2, frame_count, st_count, ta_count, st_count * inputs)


def solution(mesh):
    return jax.shard_map(
        on_device,
        mesh=mesh,
        in_specs=(P("st", "ta", None), P()),
        out_specs=P(("st", "ta"), None, None, None),
        check_vma=False,
    )
```

```python
import functools
import math

import jax
import jax.numpy as jnp
import numpy as np
from jax import lax
from jax.experimental import pallas as pl
from jax.experimental.pallas import tpu as pltpu
from jax.sharding import PartitionSpec as P

CH0 = 1024
LANES = 128
CHANNEL_BLOCK = 32
VMEM_LIMIT = 60 * 1024 * 1024
NT = (((1,), (1,)), ((), ()))


def phase_table(frame_len, channel_count, first_channel):
    channels = first_channel + np.arange(channel_count, dtype=np.int64)
    phases = (channels[:, None] * np.arange(frame_len, dtype=np.int64)[None, :]) % frame_len
    angles = 2.0 * math.pi / frame_len * phases
    parts = np.stack([np.cos(angles), -np.sin(angles)]) * frame_len**-0.5
    blocks = parts.reshape(2, channel_count // CHANNEL_BLOCK, CHANNEL_BLOCK, frame_len)
    return blocks.transpose(1, 0, 2, 3).reshape(-1, 2 * CHANNEL_BLOCK, frame_len).astype(np.float32)


def channelize_kernel(frame_count, cuts, x_hbm, coef_hbm, table_hbm, out_ref, x_in, coef_in, table_in, halves, folded, total, turned, sems):
    block = pl.program_id(0)
    taps = coef_hbm.shape[0]
    half = taps // 2
    rows = table_hbm.shape[1]
    pairs = frame_count // taps
    inputs = x_hbm.shape[0] // frame_count
    chunks = [slice(first, last) for first, last in zip(cuts[:-1], cuts[1:])]
    copies = []
    for chunk, lanes in enumerate(chunks):
        copies.append(
            [
                pltpu.make_async_copy(coef_hbm.at[:, lanes], coef_in.at[:, lanes], sems.at[chunk, 0]),
                pltpu.make_async_copy(table_hbm.at[block, :, lanes], table_in.at[:, lanes], sems.at[chunk, 1]),
                pltpu.make_async_copy(x_hbm.at[:, lanes], x_in.at[:, lanes], sems.at[chunk, 2]),
            ]
        )
        for copy in copies[-1]:
            copy.start()

    for chunk, columns in enumerate(chunks):
        for copy in copies[chunk]:
            copy.wait()
        table = table_in[:, columns]
        for kind in range(3):
            for pair in range(pairs):
                for first in range(0, inputs, 2):
                    blocks = []
                    for place in (first, first + 1):
                        row = place * frame_count + pair * taps
                        blocks.append(x_in[row : row + taps, columns].astype(jnp.float32))
                    even = jnp.concatenate([block[:half] for block in blocks], 0)
                    odd = jnp.concatenate([block[half:] for block in blocks], 0)
                    row = (pair * inputs + first) * half
                    halves[kind, row : row + taps, columns] = (even, odd, even + odd)[kind].astype(jnp.bfloat16)
            for tap in range(half):
                low = coef_in[tap : tap + 1, columns]
                high = coef_in[half + tap : half + tap + 1, columns]
                coef = (high, low, low + high)[kind]
                folded[kind, tap * rows : (tap + 1) * rows, columns] = (table * coef).astype(jnp.bfloat16)
            total[chunk, kind] = lax.dot_general(
                folded[kind, :, columns], halves[kind, :, columns], NT, preferred_element_type=jnp.float32
            )

    frame = lax.broadcasted_iota(jnp.int32, (rows, LANES), 1) % half

    def shifted_sum(kind, pair):
        lanes = slice(pair * LANES, (pair + 1) * LANES)

        def summed(tap):
            slots = [total[chunk, kind, tap * rows : (tap + 1) * rows, lanes] for chunk in range(total.shape[0])]
            return functools.reduce(jnp.add, slots)

        both = summed(0)
        inside = both
        for tap in range(1, half):
            moved = pltpu.roll(summed(tap), LANES - tap, 1)
            both = both + moved
            inside = inside + jnp.where(frame < half - tap, moved, 0.0)
        return inside, both - inside

    inside = {}
    before = {}
    for pair in range(pairs):
        (p0, c0), (p1, c1), (p2, c2) = (shifted_sum(kind, pair) for kind in range(3))
        for place, now, carry in (
            (2 * pair - 1, p0, c0),
            (2 * pair, p2 - p0 - p1, c2 - c0 - c1),
            (2 * pair + 1, p1, c1),
        ):
            inside[place] = inside[place] + now if place in inside else now
            before[place - 1] = before[place - 1] + carry if place - 1 in before else carry
    count = 2 * pairs
    channels = rows // 2
    slots = 4 * count
    for place in range(-2, count):
        value = inside.get(place)
        if place in before:
            carry = pltpu.roll(before[place], half, 1)
            value = carry if value is None else value + carry
        for part in range(2):
            slot = part * count + place if place >= 0 else (3 + part) * count + place
            turned[pl.ds(slot, channels, stride=slots), :] = value[part * channels : (part + 1) * channels]
    nothing = jnp.zeros((channels, LANES), jnp.float32)
    for part in range(2):
        for place in range(count - 2):
            turned[pl.ds((2 + part) * count + place, channels, stride=slots), :] = nothing
    out_ref[...] = turned[...].astype(jnp.bfloat16).reshape(out_ref.shape)


def channelize(samples, coefficients, channel_count):
    inputs, frame_count, frame_len = samples.shape
    taps = coefficients.shape[0]
    half = taps // 2
    rows = 2 * CHANNEL_BLOCK
    columns = inputs * frame_count
    blocks = channel_count // CHANNEL_BLOCK
    slots = 4 * frame_count // half
    cuts = (0, frame_len // 4, frame_len)
    chunks = len(cuts) - 1
    assert inputs * half == LANES and frame_count % taps == 0
    table = jnp.asarray(phase_table(frame_len, channel_count, CH0))
    return pl.pallas_call(
        functools.partial(channelize_kernel, frame_count, cuts),
        grid=(blocks,),
        in_specs=[pl.BlockSpec(memory_space=pl.ANY)] * 3,
        out_specs=pl.BlockSpec((CHANNEL_BLOCK, slots, LANES), lambda b: (b, 0, 0)),
        out_shape=jax.ShapeDtypeStruct((channel_count, slots, LANES), jnp.bfloat16),
        scratch_shapes=[
            pltpu.VMEM((columns, frame_len), jnp.bfloat16),
            pltpu.VMEM((taps, frame_len), jnp.float32),
            pltpu.VMEM((rows, frame_len), jnp.float32),
            pltpu.VMEM((3, columns // 2, frame_len), jnp.bfloat16),
            pltpu.VMEM((3, half * rows, frame_len), jnp.bfloat16),
            pltpu.VMEM((chunks, 3, half * rows, columns // 2), jnp.float32),
            pltpu.VMEM((CHANNEL_BLOCK * slots, LANES), jnp.float32),
            pltpu.SemaphoreType.DMA((chunks, 3)),
        ],
        compiler_params=pltpu.CompilerParams(dimension_semantics=("arbitrary",), vmem_limit_bytes=VMEM_LIMIT),
        cost_estimate=pl.CostEstimate(
            flops=3 * channel_count * taps * columns * frame_len,
            bytes_accessed=2 * columns * frame_len,
            transcendentals=0,
        ),
        name="channelize",
    )(samples.reshape(columns, frame_len), coefficients, table)


def correlate_kernel(half, st_count, ta_count, in_ref, out_ref, arranged, across, spectra):
    slots = in_ref.shape[1] // 2
    count = slots // 2
    inputs = LANES // half
    places = ta_count * count
    stations = LANES // places
    all_inputs = st_count * inputs
    position = lax.broadcasted_iota(jnp.int32, (inputs, LANES), 1) // places

    def station_group(group):
        for place in range(stations):
            st = group * stations + place
            for ta in range(ta_count):
                value = in_ref[st * ta_count + ta].astype(jnp.float32)[:slots]
                if ta < ta_count - 1:
                    value = value + in_ref[st * ta_count + ta + 1].astype(jnp.float32)[slots:]
                for part in range(2):
                    row = place * places + ta * count
                    arranged[part, row : row + count, :] = value[part * count : (part + 1) * count]
        for part in range(2):
            across[part] = arranged[part].T
            by_frame = [across[part, pl.ds(frame, inputs, stride=half), :] for frame in range(half)]
            for place in range(stations):
                result = None
                for frame in range(half):
                    shift = ((frame - place) * places) % LANES
                    value = pltpu.roll(by_frame[frame], shift, 1) if shift else by_frame[frame]
                    result = value if result is None else jnp.where(position == frame, value, result)
                first = part * all_inputs + (group * stations + place) * inputs
                if not isinstance(first, int):
                    first = pl.multiple_of(first, inputs)
                spectra[pl.ds(first, inputs), :] = result

    if st_count == stations:
        station_group(0)
    else:
        lax.fori_loop(0, st_count // stations, lambda group, _: (station_group(group), 0)[1], 0)
    real_part = spectra[:all_inputs, :].astype(jnp.bfloat16)
    imag_part = spectra[all_inputs:, :].astype(jnp.bfloat16)
    right = jnp.concatenate([real_part, imag_part], 1)
    left = jnp.concatenate([imag_part, -real_part], 1)
    scale = 1.0 / LANES
    for part, rows in enumerate((right, left)):
        product = lax.dot_general(rows, right, NT, preferred_element_type=jnp.float32)
        out_ref[0, part] = (product * scale).astype(jnp.bfloat16)


def correlate(arrived, half, frame_count, st_count, ta_count, all_inputs):
    assert ta_count * frame_count == LANES
    return pl.pallas_call(
        functools.partial(correlate_kernel, half, st_count, ta_count),
        in_specs=[pl.BlockSpec(memory_space=pltpu.VMEM)],
        out_specs=pl.BlockSpec(memory_space=pltpu.VMEM),
        out_shape=jax.ShapeDtypeStruct((1, 2, all_inputs, all_inputs), jnp.bfloat16),
        scratch_shapes=[
            pltpu.VMEM((2, LANES, LANES), jnp.float32),
            pltpu.VMEM((2, LANES, LANES), jnp.float32),
            pltpu.VMEM((2 * all_inputs, LANES), jnp.float32),
        ],
        compiler_params=pltpu.CompilerParams(vmem_limit_bytes=32 * 1024 * 1024),
        name="correlate",
    )(arrived)


def on_device(samples, coefficients):
    st_count = lax.axis_size("st")
    ta_count = lax.axis_size("ta")
    inputs, frame_count, _ = samples.shape
    partial = channelize(samples, coefficients, st_count * ta_count)
    arrived = lax.all_to_all(partial, ("st", "ta"), split_axis=0, concat_axis=0, tiled=True)
    return correlate(arrived, coefficients.shape[0] // 2, frame_count, st_count, ta_count, st_count * inputs)


def solution(mesh):
    return jax.shard_map(
        on_device,
        mesh=mesh,
        in_specs=(P("st", "ta", None), P()),
        out_specs=P(("st", "ta"), None, None, None),
        check_vma=False,
    )
```

```python
import functools
import math

import jax
import jax.numpy as jnp
import numpy as np
from jax import lax
from jax.experimental import pallas as pl
from jax.experimental.pallas import tpu as pltpu
from jax.sharding import PartitionSpec as P

CH0 = 1024
LANES = 128
CHANNEL_BLOCK = 32
K_BLOCK = 2048
VMEM_LIMIT = 55000 * 1024
NT = (((1,), (1,)), ((), ()))


def phase_table(frame_len, channel_count, first_channel):
    channels = first_channel + np.arange(channel_count, dtype=np.int64)
    phases = (channels[:, None] * np.arange(frame_len, dtype=np.int64)[None, :]) % frame_len
    angles = 2.0 * math.pi / frame_len * phases
    parts = np.stack([np.cos(angles), -np.sin(angles)]) * frame_len**-0.5
    blocks = parts.reshape(2, channel_count // CHANNEL_BLOCK, CHANNEL_BLOCK, frame_len)
    return blocks.transpose(1, 0, 2, 3).reshape(-1, 2 * CHANNEL_BLOCK, frame_len).astype(np.float32)


def channelize_kernel(frame_count, x_ref, coef_ref, table_ref, out_ref, halves, folded, total, turned):
    step = pl.program_id(1)
    taps = coef_ref.shape[0]
    half = taps // 2
    rows = table_ref.shape[1]
    pairs = frame_count // taps
    inputs = x_ref.shape[0] // frame_count

    table = table_ref[0]
    for kind in range(3):
        for pair in range(pairs):
            for first in range(0, inputs, 2):
                blocks = []
                for place in (first, first + 1):
                    row = place * frame_count + pair * taps
                    blocks.append(x_ref[row : row + taps, :].astype(jnp.float32))
                even = jnp.concatenate([block[:half] for block in blocks], 0)
                odd = jnp.concatenate([block[half:] for block in blocks], 0)
                row = (pair * inputs + first) * half
                halves[kind, row : row + taps, :] = (even, odd, even + odd)[kind].astype(jnp.bfloat16)
        for tap in range(half):
            low = coef_ref[tap : tap + 1, :]
            high = coef_ref[half + tap : half + tap + 1, :]
            coef = (high, low, low + high)[kind]
            folded[kind, tap * rows : (tap + 1) * rows, :] = (table * coef).astype(jnp.bfloat16)
        total[step, kind] = lax.dot_general(folded[kind], halves[kind], NT, preferred_element_type=jnp.float32)

    @pl.when(step == pl.num_programs(1) - 1)
    def _():
        frame = lax.broadcasted_iota(jnp.int32, (rows, LANES), 1) % half

        def shifted_sum(kind, pair):
            lanes = slice(pair * LANES, (pair + 1) * LANES)

            def summed(tap):
                slots = [total[chunk, kind, tap * rows : (tap + 1) * rows, lanes] for chunk in range(total.shape[0])]
                return functools.reduce(jnp.add, slots)

            both = summed(0)
            inside = both
            for tap in range(1, half):
                moved = pltpu.roll(summed(tap), LANES - tap, 1)
                both = both + moved
                inside = inside + jnp.where(frame < half - tap, moved, 0.0)
            return inside, both - inside

        inside = {}
        before = {}
        for pair in range(pairs):
            (p0, c0), (p1, c1), (p2, c2) = (shifted_sum(kind, pair) for kind in range(3))
            for place, now, carry in (
                (2 * pair - 1, p0, c0),
                (2 * pair, p2 - p0 - p1, c2 - c0 - c1),
                (2 * pair + 1, p1, c1),
            ):
                inside[place] = inside[place] + now if place in inside else now
                before[place - 1] = before[place - 1] + carry if place - 1 in before else carry
        count = 2 * pairs
        channels = rows // 2
        slots = 4 * count
        for place in range(-2, count):
            value = inside.get(place)
            if place in before:
                carry = pltpu.roll(before[place], half, 1)
                value = carry if value is None else value + carry
            for part in range(2):
                slot = part * count + place if place >= 0 else (3 + part) * count + place
                turned[pl.ds(slot, channels, stride=slots), :] = value[part * channels : (part + 1) * channels]
        nothing = jnp.zeros((channels, LANES), jnp.float32)
        for part in range(2):
            for place in range(count - 2):
                turned[pl.ds((2 + part) * count + place, channels, stride=slots), :] = nothing
        out_ref[...] = turned[...].astype(jnp.bfloat16).reshape(out_ref.shape)


def channelize(samples, coefficients, channel_count):
    inputs, frame_count, frame_len = samples.shape
    taps = coefficients.shape[0]
    half = taps // 2
    rows = 2 * CHANNEL_BLOCK
    columns = inputs * frame_count
    blocks = channel_count // CHANNEL_BLOCK
    slots = 4 * frame_count // half
    k_block = min(K_BLOCK, frame_len)
    assert inputs * half == LANES and frame_count % taps == 0
    table = jnp.asarray(phase_table(frame_len, channel_count, CH0))
    return pl.pallas_call(
        functools.partial(channelize_kernel, frame_count),
        grid=(blocks, frame_len // k_block),
        in_specs=[
            pl.BlockSpec((columns, k_block), lambda b, k: (0, k)),
            pl.BlockSpec((taps, k_block), lambda b, k: (0, k)),
            pl.BlockSpec((1, rows, k_block), lambda b, k: (b, 0, k)),
        ],
        out_specs=pl.BlockSpec((CHANNEL_BLOCK, slots, LANES), lambda b, k: (b, 0, 0)),
        out_shape=jax.ShapeDtypeStruct((channel_count, slots, LANES), jnp.bfloat16),
        scratch_shapes=[
            pltpu.VMEM((3, columns // 2, k_block), jnp.bfloat16),
            pltpu.VMEM((3, half * rows, k_block), jnp.bfloat16),
            pltpu.VMEM((frame_len // k_block, 3, half * rows, columns // 2), jnp.float32),
            pltpu.VMEM((CHANNEL_BLOCK * slots, LANES), jnp.float32),
        ],
        compiler_params=pltpu.CompilerParams(
            dimension_semantics=("arbitrary", "arbitrary"), vmem_limit_bytes=VMEM_LIMIT
        ),
        cost_estimate=pl.CostEstimate(
            flops=3 * channel_count * taps * columns * frame_len,
            bytes_accessed=2 * columns * frame_len,
            transcendentals=0,
        ),
        name="channelize",
    )(samples.reshape(columns, frame_len), coefficients, table)


def correlate_kernel(half, st_count, ta_count, in_ref, out_ref, arranged, across, spectra):
    slots = in_ref.shape[1] // 2
    count = slots // 2
    inputs = LANES // half
    places = ta_count * count
    stations = LANES // places
    all_inputs = st_count * inputs
    position = lax.broadcasted_iota(jnp.int32, (inputs, LANES), 1) // places

    def station_group(group):
        for place in range(stations):
            st = group * stations + place
            for ta in range(ta_count):
                value = in_ref[st * ta_count + ta].astype(jnp.float32)[:slots]
                if ta < ta_count - 1:
                    value = value + in_ref[st * ta_count + ta + 1].astype(jnp.float32)[slots:]
                for part in range(2):
                    row = place * places + ta * count
                    arranged[part, row : row + count, :] = value[part * count : (part + 1) * count]
        for part in range(2):
            across[part] = arranged[part].T
            by_frame = [across[part, pl.ds(frame, inputs, stride=half), :] for frame in range(half)]
            for place in range(stations):
                result = None
                for frame in range(half):
                    shift = ((frame - place) * places) % LANES
                    value = pltpu.roll(by_frame[frame], shift, 1) if shift else by_frame[frame]
                    result = value if result is None else jnp.where(position == frame, value, result)
                first = part * all_inputs + (group * stations + place) * inputs
                if not isinstance(first, int):
                    first = pl.multiple_of(first, inputs)
                spectra[pl.ds(first, inputs), :] = result

    if st_count == stations:
        station_group(0)
    else:
        lax.fori_loop(0, st_count // stations, lambda group, _: (station_group(group), 0)[1], 0)
    real_part = spectra[:all_inputs, :].astype(jnp.bfloat16)
    imag_part = spectra[all_inputs:, :].astype(jnp.bfloat16)
    right = jnp.concatenate([real_part, imag_part], 1)
    left = jnp.concatenate([imag_part, -real_part], 1)
    scale = 1.0 / LANES
    for part, rows in enumerate((right, left)):
        product = lax.dot_general(rows, right, NT, preferred_element_type=jnp.float32)
        out_ref[0, part] = (product * scale).astype(jnp.bfloat16)


def correlate(arrived, half, frame_count, st_count, ta_count, all_inputs):
    assert ta_count * frame_count == LANES
    return pl.pallas_call(
        functools.partial(correlate_kernel, half, st_count, ta_count),
        in_specs=[pl.BlockSpec(memory_space=pltpu.VMEM)],
        out_specs=pl.BlockSpec(memory_space=pltpu.VMEM),
        out_shape=jax.ShapeDtypeStruct((1, 2, all_inputs, all_inputs), jnp.bfloat16),
        scratch_shapes=[
            pltpu.VMEM((2, LANES, LANES), jnp.float32),
            pltpu.VMEM((2, LANES, LANES), jnp.float32),
            pltpu.VMEM((2 * all_inputs, LANES), jnp.float32),
        ],
        compiler_params=pltpu.CompilerParams(vmem_limit_bytes=32 * 1024 * 1024),
        name="correlate",
    )(arrived)


def on_device(samples, coefficients):
    st_count = lax.axis_size("st")
    ta_count = lax.axis_size("ta")
    inputs, frame_count, _ = samples.shape
    partial = channelize(samples, coefficients, st_count * ta_count)
    arrived = lax.all_to_all(partial, ("st", "ta"), split_axis=0, concat_axis=0, tiled=True)
    return correlate(arrived, coefficients.shape[0] // 2, frame_count, st_count, ta_count, st_count * inputs)


def solution(mesh):
    return jax.shard_map(
        on_device,
        mesh=mesh,
        in_specs=(P("st", "ta", None), P()),
        out_specs=P(("st", "ta"), None, None, None),
        check_vma=False,
    )
```

```python
import functools
import math

import jax
import jax.numpy as jnp
import numpy as np
from jax import lax
from jax.experimental import pallas as pl
from jax.experimental.pallas import tpu as pltpu
from jax.sharding import PartitionSpec as P

CH0 = 1024
LANES = 128
CHANNEL_BLOCK = 32
K_BLOCK = 2048
VMEM_LIMIT = 55000 * 1024
NT = (((1,), (1,)), ((), ()))


def phase_table(frame_len, channel_count, first_channel):
    channels = first_channel + np.arange(channel_count, dtype=np.int64)
    phases = (channels[:, None] * np.arange(frame_len, dtype=np.int64)[None, :]) % frame_len
    angles = 2.0 * math.pi / frame_len * phases
    parts = np.stack([np.cos(angles), -np.sin(angles)]) * frame_len**-0.5
    blocks = parts.reshape(2, channel_count // CHANNEL_BLOCK, CHANNEL_BLOCK, frame_len)
    return blocks.transpose(1, 0, 2, 3).reshape(-1, 2 * CHANNEL_BLOCK, frame_len).astype(np.float32)


def channelize_kernel(frame_count, x_ref, coef_ref, table_ref, out_ref, halves, folded, total, turned):
    step = pl.program_id(1)
    taps = coef_ref.shape[0]
    half = taps // 2
    rows = table_ref.shape[1]
    pairs = frame_count // taps
    inputs = x_ref.shape[0] // frame_count

    table = table_ref[0]
    for kind in range(3):
        for pair in range(pairs):
            for first in range(0, inputs, 2):
                blocks = []
                for place in (first, first + 1):
                    row = place * frame_count + pair * taps
                    blocks.append(x_ref[row : row + taps, :].astype(jnp.float32))
                even = jnp.concatenate([block[:half] for block in blocks], 0)
                odd = jnp.concatenate([block[half:] for block in blocks], 0)
                row = (pair * inputs + first) * half
                halves[kind, row : row + taps, :] = (even, odd, even + odd)[kind].astype(jnp.bfloat16)
        for tap in range(half):
            low = coef_ref[tap : tap + 1, :]
            high = coef_ref[half + tap : half + tap + 1, :]
            coef = (high, low, low + high)[kind]
            folded[kind, tap * rows : (tap + 1) * rows, :] = (table * coef).astype(jnp.bfloat16)
        total[step, kind] = lax.dot_general(folded[kind], halves[kind], NT, preferred_element_type=jnp.float32)

    @pl.when(step == pl.num_programs(1) - 1)
    def _():
        frame = lax.broadcasted_iota(jnp.int32, (rows, LANES), 1) % half

        def shifted_sum(kind, pair):
            lanes = slice(pair * LANES, (pair + 1) * LANES)

            def summed(tap):
                slots = [total[chunk, kind, tap * rows : (tap + 1) * rows, lanes] for chunk in range(total.shape[0])]
                return functools.reduce(jnp.add, slots)

            both = summed(0)
            inside = both
            for tap in range(1, half):
                moved = pltpu.roll(summed(tap), LANES - tap, 1)
                both = both + moved
                inside = inside + jnp.where(frame < half - tap, moved, 0.0)
            return inside, both - inside

        inside = {}
        before = {}
        for pair in range(pairs):
            (p0, c0), (p1, c1), (p2, c2) = (shifted_sum(kind, pair) for kind in range(3))
            for place, now, carry in (
                (2 * pair - 1, p0, c0),
                (2 * pair, p2 - p0 - p1, c2 - c0 - c1),
                (2 * pair + 1, p1, c1),
            ):
                inside[place] = inside[place] + now if place in inside else now
                before[place - 1] = before[place - 1] + carry if place - 1 in before else carry
        channels = rows // 2
        for place in range(-2, 2 * pairs):
            value = inside.get(place)
            if place in before:
                carry = pltpu.roll(before[place], half, 1)
                value = carry if value is None else value + carry
            for part in range(2):
                row, column = (place, part) if place >= 0 else (2 * part + place + 2, 2)
                turned[column, pl.ds(row, channels, stride=2 * pairs), :] = value[part * channels : (part + 1) * channels]
        for column in range(3):
            lanes = slice(column * LANES, (column + 1) * LANES)
            for channel in range(channels):
                block = turned[column, channel * 2 * pairs : (channel + 1) * 2 * pairs, :]
                out_ref[channel, :, lanes] = block.astype(jnp.bfloat16)


def channelize(samples, coefficients, channel_count):
    inputs, frame_count, frame_len = samples.shape
    taps = coefficients.shape[0]
    half = taps // 2
    rows = 2 * CHANNEL_BLOCK
    columns = inputs * frame_count
    blocks = channel_count // CHANNEL_BLOCK
    slots = frame_count // half
    assert slots == 4
    k_block = min(K_BLOCK, frame_len)
    assert inputs * half == LANES and frame_count % taps == 0
    table = jnp.asarray(phase_table(frame_len, channel_count, CH0))
    return pl.pallas_call(
        functools.partial(channelize_kernel, frame_count),
        grid=(blocks, frame_len // k_block),
        in_specs=[
            pl.BlockSpec((columns, k_block), lambda b, k: (0, k)),
            pl.BlockSpec((taps, k_block), lambda b, k: (0, k)),
            pl.BlockSpec((1, rows, k_block), lambda b, k: (b, 0, k)),
        ],
        out_specs=pl.BlockSpec((CHANNEL_BLOCK, slots, 3 * LANES), lambda b, k: (b, 0, 0)),
        out_shape=jax.ShapeDtypeStruct((channel_count, slots, 3 * LANES), jnp.bfloat16),
        scratch_shapes=[
            pltpu.VMEM((3, columns // 2, k_block), jnp.bfloat16),
            pltpu.VMEM((3, half * rows, k_block), jnp.bfloat16),
            pltpu.VMEM((frame_len // k_block, 3, half * rows, columns // 2), jnp.float32),
            pltpu.VMEM((3, CHANNEL_BLOCK * slots, LANES), jnp.float32),
        ],
        compiler_params=pltpu.CompilerParams(
            dimension_semantics=("arbitrary", "arbitrary"), vmem_limit_bytes=VMEM_LIMIT
        ),
        cost_estimate=pl.CostEstimate(
            flops=3 * channel_count * taps * columns * frame_len,
            bytes_accessed=2 * columns * frame_len,
            transcendentals=0,
        ),
        name="channelize",
    )(samples.reshape(columns, frame_len), coefficients, table)


def correlate_kernel(half, st_count, ta_count, in_ref, out_ref, arranged, across, spectra):
    count = in_ref.shape[1]
    inputs = LANES // half
    places = ta_count * count
    stations = LANES // places
    all_inputs = st_count * inputs
    position = lax.broadcasted_iota(jnp.int32, (inputs, LANES), 1) // places

    def station_group(group):
        for place in range(stations):
            st = group * stations + place
            for ta in range(ta_count):
                row = place * places + ta * count
                own = in_ref[st * ta_count + ta].astype(jnp.float32)
                for part in range(2):
                    arranged[part, row : row + count, :] = own[:, part * LANES : (part + 1) * LANES]
                if ta < ta_count - 1:
                    ahead = in_ref[st * ta_count + ta + 1].astype(jnp.float32)[:, 2 * LANES :]
                    for part in range(2):
                        arranged[part, row + count - 2 : row + count, :] += ahead[2 * part : 2 * part + 2]
        for part in range(2):
            across[part] = arranged[part].T
            by_frame = [across[part, pl.ds(frame, inputs, stride=half), :] for frame in range(half)]
            for place in range(stations):
                result = None
                for frame in range(half):
                    shift = ((frame - place) * places) % LANES
                    value = pltpu.roll(by_frame[frame], shift, 1) if shift else by_frame[frame]
                    result = value if result is None else jnp.where(position == frame, value, result)
                first = part * all_inputs + (group * stations + place) * inputs
                if not isinstance(first, int):
                    first = pl.multiple_of(first, inputs)
                spectra[pl.ds(first, inputs), :] = result

    if st_count == stations:
        station_group(0)
    else:
        lax.fori_loop(0, st_count // stations, lambda group, _: (station_group(group), 0)[1], 0)
    real_part = spectra[:all_inputs, :].astype(jnp.bfloat16)
    imag_part = spectra[all_inputs:, :].astype(jnp.bfloat16)
    right = jnp.concatenate([real_part, imag_part], 1)
    left = jnp.concatenate([imag_part, -real_part], 1)
    scale = 1.0 / LANES
    for part, rows in enumerate((right, left)):
        product = lax.dot_general(rows, right, NT, preferred_element_type=jnp.float32)
        out_ref[0, part] = (product * scale).astype(jnp.bfloat16)


def correlate(arrived, half, frame_count, st_count, ta_count, all_inputs):
    assert ta_count * frame_count == LANES
    return pl.pallas_call(
        functools.partial(correlate_kernel, half, st_count, ta_count),
        in_specs=[pl.BlockSpec(memory_space=pltpu.VMEM)],
        out_specs=pl.BlockSpec(memory_space=pltpu.VMEM),
        out_shape=jax.ShapeDtypeStruct((1, 2, all_inputs, all_inputs), jnp.bfloat16),
        scratch_shapes=[
            pltpu.VMEM((2, LANES, LANES), jnp.float32),
            pltpu.VMEM((2, LANES, LANES), jnp.float32),
            pltpu.VMEM((2 * all_inputs, LANES), jnp.float32),
        ],
        compiler_params=pltpu.CompilerParams(vmem_limit_bytes=32 * 1024 * 1024),
        name="correlate",
    )(arrived)


def on_device(samples, coefficients):
    st_count = lax.axis_size("st")
    ta_count = lax.axis_size("ta")
    inputs, frame_count, _ = samples.shape
    partial = channelize(samples, coefficients, st_count * ta_count)
    arrived = lax.all_to_all(partial, ("st", "ta"), split_axis=0, concat_axis=0, tiled=True)
    return correlate(arrived, coefficients.shape[0] // 2, frame_count, st_count, ta_count, st_count * inputs)


def solution(mesh):
    return jax.shard_map(
        on_device,
        mesh=mesh,
        in_specs=(P("st", "ta", None), P()),
        out_specs=P(("st", "ta"), None, None, None),
        check_vma=False,
    )
```

```python
import functools
import math

import jax
import jax.numpy as jnp
import numpy as np
from jax import lax
from jax.experimental import pallas as pl
from jax.experimental.pallas import tpu as pltpu
from jax.sharding import PartitionSpec as P

CH0 = 1024
LANES = 128
CHANNEL_BLOCK = 32
K_BLOCK = 4096
VMEM_LIMIT = 55000 * 1024
NT = (((1,), (1,)), ((), ()))


def phase_table(frame_len, channel_count, first_channel):
    channels = first_channel + np.arange(channel_count, dtype=np.int64)
    phases = (channels[:, None] * np.arange(frame_len, dtype=np.int64)[None, :]) % frame_len
    angles = 2.0 * math.pi / frame_len * phases
    parts = np.stack([np.cos(angles), -np.sin(angles)]) * frame_len**-0.5
    blocks = parts.reshape(2, channel_count // CHANNEL_BLOCK, CHANNEL_BLOCK, frame_len)
    return blocks.transpose(1, 0, 2, 3).reshape(-1, 2 * CHANNEL_BLOCK, frame_len).astype(np.float32)


def channelize_kernel(frame_count, x_ref, coef_ref, table_ref, out_ref, halves, folded, total, turned):
    step = pl.program_id(1)
    taps = coef_ref.shape[0]
    half = taps // 2
    rows = table_ref.shape[1]
    pairs = frame_count // taps
    inputs = x_ref.shape[0] // frame_count

    table = table_ref[0]
    for kind in range(3):
        for pair in range(pairs):
            for first in range(0, inputs, 2):
                blocks = []
                for place in (first, first + 1):
                    row = place * frame_count + pair * taps
                    blocks.append(x_ref[row : row + taps, :].astype(jnp.float32))
                even = jnp.concatenate([block[:half] for block in blocks], 0)
                odd = jnp.concatenate([block[half:] for block in blocks], 0)
                row = (pair * inputs + first) * half
                halves[kind, row : row + taps, :] = (even, odd, even + odd)[kind].astype(jnp.bfloat16)
        for tap in range(half):
            low = coef_ref[tap : tap + 1, :]
            high = coef_ref[half + tap : half + tap + 1, :]
            coef = (high, low, low + high)[kind]
            folded[kind, tap * rows : (tap + 1) * rows, :] = (table * coef).astype(jnp.bfloat16)
        total[step, kind] = lax.dot_general(folded[kind], halves[kind], NT, preferred_element_type=jnp.float32)

    @pl.when(step == pl.num_programs(1) - 1)
    def _():
        frame = lax.broadcasted_iota(jnp.int32, (rows, LANES), 1) % half

        def shifted_sum(kind, pair):
            lanes = slice(pair * LANES, (pair + 1) * LANES)

            def summed(tap):
                slots = [total[chunk, kind, tap * rows : (tap + 1) * rows, lanes] for chunk in range(total.shape[0])]
                return functools.reduce(jnp.add, slots)

            both = summed(0)
            inside = both
            for tap in range(1, half):
                moved = pltpu.roll(summed(tap), LANES - tap, 1)
                both = both + moved
                inside = inside + jnp.where(frame < half - tap, moved, 0.0)
            return inside, both - inside

        inside = {}
        before = {}
        for pair in range(pairs):
            (p0, c0), (p1, c1), (p2, c2) = (shifted_sum(kind, pair) for kind in range(3))
            for place, now, carry in (
                (2 * pair - 1, p0, c0),
                (2 * pair, p2 - p0 - p1, c2 - c0 - c1),
                (2 * pair + 1, p1, c1),
            ):
                inside[place] = inside[place] + now if place in inside else now
                before[place - 1] = before[place - 1] + carry if place - 1 in before else carry
        channels = rows // 2
        for place in range(-2, 2 * pairs):
            value = inside.get(place)
            if place in before:
                carry = pltpu.roll(before[place], half, 1)
                value = carry if value is None else value + carry
            for part in range(2):
                row, column = (place, part) if place >= 0 else (2 * part + place + 2, 2)
                turned[column, pl.ds(row, channels, stride=2 * pairs), :] = value[part * channels : (part + 1) * channels]
        for column in range(3):
            lanes = slice(column * LANES, (column + 1) * LANES)
            for channel in range(channels):
                block = turned[column, channel * 2 * pairs : (channel + 1) * 2 * pairs, :]
                out_ref[channel, :, lanes] = block.astype(jnp.bfloat16)


def channelize(samples, coefficients, channel_count):
    inputs, frame_count, frame_len = samples.shape
    taps = coefficients.shape[0]
    half = taps // 2
    rows = 2 * CHANNEL_BLOCK
    columns = inputs * frame_count
    blocks = channel_count // CHANNEL_BLOCK
    slots = frame_count // half
    assert slots == 4
    k_block = min(K_BLOCK, frame_len)
    assert inputs * half == LANES and frame_count % taps == 0
    table = jnp.asarray(phase_table(frame_len, channel_count, CH0))
    return pl.pallas_call(
        functools.partial(channelize_kernel, frame_count),
        grid=(blocks, frame_len // k_block),
        in_specs=[
            pl.BlockSpec((columns, k_block), lambda b, k: (0, k)),
            pl.BlockSpec((taps, k_block), lambda b, k: (0, k)),
            pl.BlockSpec((1, rows, k_block), lambda b, k: (b, 0, k)),
        ],
        out_specs=pl.BlockSpec((CHANNEL_BLOCK, slots, 3 * LANES), lambda b, k: (b, 0, 0)),
        out_shape=jax.ShapeDtypeStruct((channel_count, slots, 3 * LANES), jnp.bfloat16),
        scratch_shapes=[
            pltpu.VMEM((3, columns // 2, k_block), jnp.bfloat16),
            pltpu.VMEM((3, half * rows, k_block), jnp.bfloat16),
            pltpu.VMEM((frame_len // k_block, 3, half * rows, columns // 2), jnp.float32),
            pltpu.VMEM((3, CHANNEL_BLOCK * slots, LANES), jnp.float32),
        ],
        compiler_params=pltpu.CompilerParams(
            dimension_semantics=("arbitrary", "arbitrary"), vmem_limit_bytes=VMEM_LIMIT
        ),
        cost_estimate=pl.CostEstimate(
            flops=3 * channel_count * taps * columns * frame_len,
            bytes_accessed=2 * columns * frame_len,
            transcendentals=0,
        ),
        name="channelize",
    )(samples.reshape(columns, frame_len), coefficients, table)


def correlate_kernel(half, st_count, ta_count, in_ref, out_ref, arranged, across, spectra):
    count = in_ref.shape[1]
    inputs = LANES // half
    places = ta_count * count
    stations = LANES // places
    all_inputs = st_count * inputs
    position = lax.broadcasted_iota(jnp.int32, (inputs, LANES), 1) // places

    def station_group(group):
        for place in range(stations):
            st = group * stations + place
            for ta in range(ta_count):
                row = place * places + ta * count
                own = in_ref[st * ta_count + ta].astype(jnp.float32)
                for part in range(2):
                    arranged[part, row : row + count, :] = own[:, part * LANES : (part + 1) * LANES]
                if ta < ta_count - 1:
                    ahead = in_ref[st * ta_count + ta + 1].astype(jnp.float32)[:, 2 * LANES :]
                    for part in range(2):
                        arranged[part, row + count - 2 : row + count, :] += ahead[2 * part : 2 * part + 2]
        for part in range(2):
            across[part] = arranged[part].T
            by_frame = [across[part, pl.ds(frame, inputs, stride=half), :] for frame in range(half)]
            for place in range(stations):
                result = None
                for frame in range(half):
                    shift = ((frame - place) * places) % LANES
                    value = pltpu.roll(by_frame[frame], shift, 1) if shift else by_frame[frame]
                    result = value if result is None else jnp.where(position == frame, value, result)
                first = part * all_inputs + (group * stations + place) * inputs
                if not isinstance(first, int):
                    first = pl.multiple_of(first, inputs)
                spectra[pl.ds(first, inputs), :] = result

    if st_count == stations:
        station_group(0)
    else:
        lax.fori_loop(0, st_count // stations, lambda group, _: (station_group(group), 0)[1], 0)
    real_part = spectra[:all_inputs, :].astype(jnp.bfloat16)
    imag_part = spectra[all_inputs:, :].astype(jnp.bfloat16)
    right = jnp.concatenate([real_part, imag_part], 1)
    left = jnp.concatenate([imag_part, -real_part], 1)
    scale = 1.0 / LANES
    for part, rows in enumerate((right, left)):
        product = lax.dot_general(rows, right, NT, preferred_element_type=jnp.float32)
        out_ref[0, part] = (product * scale).astype(jnp.bfloat16)


def correlate(arrived, half, frame_count, st_count, ta_count, all_inputs):
    assert ta_count * frame_count == LANES
    return pl.pallas_call(
        functools.partial(correlate_kernel, half, st_count, ta_count),
        in_specs=[pl.BlockSpec(memory_space=pltpu.VMEM)],
        out_specs=pl.BlockSpec(memory_space=pltpu.VMEM),
        out_shape=jax.ShapeDtypeStruct((1, 2, all_inputs, all_inputs), jnp.bfloat16),
        scratch_shapes=[
            pltpu.VMEM((2, LANES, LANES), jnp.float32),
            pltpu.VMEM((2, LANES, LANES), jnp.float32),
            pltpu.VMEM((2 * all_inputs, LANES), jnp.float32),
        ],
        compiler_params=pltpu.CompilerParams(vmem_limit_bytes=32 * 1024 * 1024),
        name="correlate",
    )(arrived)


def on_device(samples, coefficients):
    st_count = lax.axis_size("st")
    ta_count = lax.axis_size("ta")
    inputs, frame_count, _ = samples.shape
    partial = channelize(samples, coefficients, st_count * ta_count)
    arrived = lax.all_to_all(partial, ("st", "ta"), split_axis=0, concat_axis=0, tiled=True)
    return correlate(arrived, coefficients.shape[0] // 2, frame_count, st_count, ta_count, st_count * inputs)


def solution(mesh):
    return jax.shard_map(
        on_device,
        mesh=mesh,
        in_specs=(P("st", "ta", None), P()),
        out_specs=P(("st", "ta"), None, None, None),
        check_vma=False,
    )
```

```python
import functools
import math

import jax
import jax.numpy as jnp
import numpy as np
from jax import lax
from jax.experimental import pallas as pl
from jax.experimental.pallas import tpu as pltpu
from jax.sharding import PartitionSpec as P

CH0 = 1024
LANES = 128
CHANNEL_BLOCK = 32
K_BLOCK = 2048
VMEM_LIMIT = 55000 * 1024
NT = (((1,), (1,)), ((), ()))


def phase_table(frame_len, channel_count, first_channel):
    channels = first_channel + np.arange(channel_count, dtype=np.int64)
    phases = (channels[:, None] * np.arange(frame_len, dtype=np.int64)[None, :]) % frame_len
    angles = 2.0 * math.pi / frame_len * phases
    parts = np.stack([np.cos(angles), -np.sin(angles)]) * frame_len**-0.5
    blocks = parts.reshape(2, channel_count // CHANNEL_BLOCK, CHANNEL_BLOCK, frame_len)
    return blocks.transpose(1, 0, 2, 3).reshape(-1, 2 * CHANNEL_BLOCK, frame_len).astype(np.float32)


def channelize_kernel(
    frame_count, x_hbm, coef_hbm, table_hbm, out_ref, x_in, coef_in, table_in, halves, folded, total, turned, sems
):
    block = pl.program_id(0)
    chunks, taps, k_block = coef_in.shape
    half = taps // 2
    rows = table_in.shape[1]
    pairs = frame_count // taps
    inputs = x_in.shape[1] // frame_count

    def copies(chunk):
        lanes = pl.ds(pl.multiple_of(chunk * k_block, k_block), k_block)
        return (
            pltpu.make_async_copy(coef_hbm.at[:, lanes], coef_in.at[chunk], sems.at[0, chunk]),
            pltpu.make_async_copy(table_hbm.at[block, :, lanes], table_in.at[chunk], sems.at[1, chunk]),
            pltpu.make_async_copy(x_hbm.at[:, lanes], x_in.at[chunk], sems.at[2, chunk]),
        )

    for chunk in range(2):
        for copy in copies(chunk):
            copy.start()

    def multiply(chunk, _):
        @pl.when(chunk + 2 < chunks)
        def _():
            for copy in copies(chunk + 2):
                copy.start()

        for copy in copies(chunk):
            copy.wait()
        table = table_in[chunk]
        for kind in range(3):
            for pair in range(pairs):
                for first in range(0, inputs, 2):
                    blocks = []
                    for place in (first, first + 1):
                        row = place * frame_count + pair * taps
                        blocks.append(x_in[chunk, row : row + taps, :].astype(jnp.float32))
                    even = jnp.concatenate([value[:half] for value in blocks], 0)
                    odd = jnp.concatenate([value[half:] for value in blocks], 0)
                    row = (pair * inputs + first) * half
                    halves[kind, row : row + taps, :] = (even, odd, even + odd)[kind].astype(jnp.bfloat16)
            for tap in range(half):
                low = coef_in[chunk, tap : tap + 1, :]
                high = coef_in[chunk, half + tap : half + tap + 1, :]
                coef = (high, low, low + high)[kind]
                folded[kind, tap * rows : (tap + 1) * rows, :] = (table * coef).astype(jnp.bfloat16)
            total[chunk, kind] = lax.dot_general(folded[kind], halves[kind], NT, preferred_element_type=jnp.float32)
        return 0

    lax.fori_loop(0, chunks, multiply, 0)

    frame = lax.broadcasted_iota(jnp.int32, (rows, LANES), 1) % half

    def shifted_sum(kind, pair):
        lanes = slice(pair * LANES, (pair + 1) * LANES)

        def summed(tap):
            slots = [total[chunk, kind, tap * rows : (tap + 1) * rows, lanes] for chunk in range(total.shape[0])]
            return functools.reduce(jnp.add, slots)

        both = summed(0)
        inside = both
        for tap in range(1, half):
            moved = pltpu.roll(summed(tap), LANES - tap, 1)
            both = both + moved
            inside = inside + jnp.where(frame < half - tap, moved, 0.0)
        return inside, both - inside

    inside = {}
    before = {}
    for pair in range(pairs):
        (p0, c0), (p1, c1), (p2, c2) = (shifted_sum(kind, pair) for kind in range(3))
        for place, now, carry in (
            (2 * pair - 1, p0, c0),
            (2 * pair, p2 - p0 - p1, c2 - c0 - c1),
            (2 * pair + 1, p1, c1),
        ):
            inside[place] = inside[place] + now if place in inside else now
            before[place - 1] = before[place - 1] + carry if place - 1 in before else carry
    channels = rows // 2
    for place in range(-2, 2 * pairs):
        value = inside.get(place)
        if place in before:
            carry = pltpu.roll(before[place], half, 1)
            value = carry if value is None else value + carry
        for part in range(2):
            row, column = (place, part) if place >= 0 else (2 * part + place + 2, 2)
            turned[column, pl.ds(row, channels, stride=2 * pairs), :] = value[part * channels : (part + 1) * channels]
    for column in range(3):
        lanes = slice(column * LANES, (column + 1) * LANES)
        for channel in range(channels):
            block = turned[column, channel * 2 * pairs : (channel + 1) * 2 * pairs, :]
            out_ref[channel, :, lanes] = block.astype(jnp.bfloat16)


def channelize(samples, coefficients, channel_count):
    inputs, frame_count, frame_len = samples.shape
    taps = coefficients.shape[0]
    half = taps // 2
    rows = 2 * CHANNEL_BLOCK
    columns = inputs * frame_count
    blocks = channel_count // CHANNEL_BLOCK
    slots = frame_count // half
    assert slots == 4
    k_block = min(K_BLOCK, frame_len // 2)
    chunks = frame_len // k_block
    assert inputs * half == LANES and frame_count % taps == 0
    table = jnp.asarray(phase_table(frame_len, channel_count, CH0))
    return pl.pallas_call(
        functools.partial(channelize_kernel, frame_count),
        grid=(blocks,),
        in_specs=[pl.BlockSpec(memory_space=pl.ANY)] * 3,
        out_specs=pl.BlockSpec((CHANNEL_BLOCK, slots, 3 * LANES), lambda b: (b, 0, 0)),
        out_shape=jax.ShapeDtypeStruct((channel_count, slots, 3 * LANES), jnp.bfloat16),
        scratch_shapes=[
            pltpu.VMEM((chunks, columns, k_block), jnp.bfloat16),
            pltpu.VMEM((chunks, taps, k_block), jnp.float32),
            pltpu.VMEM((chunks, rows, k_block), jnp.float32),
            pltpu.VMEM((3, columns // 2, k_block), jnp.bfloat16),
            pltpu.VMEM((3, half * rows, k_block), jnp.bfloat16),
            pltpu.VMEM((chunks, 3, half * rows, columns // 2), jnp.float32),
            pltpu.VMEM((3, CHANNEL_BLOCK * slots, LANES), jnp.float32),
            pltpu.SemaphoreType.DMA((3, chunks)),
        ],
        compiler_params=pltpu.CompilerParams(
            dimension_semantics=("arbitrary",), vmem_limit_bytes=VMEM_LIMIT
        ),
        cost_estimate=pl.CostEstimate(
            flops=3 * channel_count * taps * columns * frame_len,
            bytes_accessed=2 * columns * frame_len,
            transcendentals=0,
        ),
        name="channelize",
    )(samples.reshape(columns, frame_len), coefficients, table)


def correlate_kernel(half, st_count, ta_count, in_ref, out_ref, arranged, across, spectra):
    count = in_ref.shape[1]
    inputs = LANES // half
    places = ta_count * count
    stations = LANES // places
    all_inputs = st_count * inputs
    position = lax.broadcasted_iota(jnp.int32, (inputs, LANES), 1) // places

    def station_group(group):
        for place in range(stations):
            st = group * stations + place
            for ta in range(ta_count):
                row = place * places + ta * count
                own = in_ref[st * ta_count + ta].astype(jnp.float32)
                for part in range(2):
                    arranged[part, row : row + count, :] = own[:, part * LANES : (part + 1) * LANES]
                if ta < ta_count - 1:
                    ahead = in_ref[st * ta_count + ta + 1].astype(jnp.float32)[:, 2 * LANES :]
                    for part in range(2):
                        arranged[part, row + count - 2 : row + count, :] += ahead[2 * part : 2 * part + 2]
        for part in range(2):
            across[part] = arranged[part].T
            by_frame = [across[part, pl.ds(frame, inputs, stride=half), :] for frame in range(half)]
            for place in range(stations):
                result = None
                for frame in range(half):
                    shift = ((frame - place) * places) % LANES
                    value = pltpu.roll(by_frame[frame], shift, 1) if shift else by_frame[frame]
                    result = value if result is None else jnp.where(position == frame, value, result)
                first = part * all_inputs + (group * stations + place) * inputs
                if not isinstance(first, int):
                    first = pl.multiple_of(first, inputs)
                spectra[pl.ds(first, inputs), :] = result

    if st_count == stations:
        station_group(0)
    else:
        lax.fori_loop(0, st_count // stations, lambda group, _: (station_group(group), 0)[1], 0)
    real_part = spectra[:all_inputs, :].astype(jnp.bfloat16)
    imag_part = spectra[all_inputs:, :].astype(jnp.bfloat16)
    right = jnp.concatenate([real_part, imag_part], 1)
    left = jnp.concatenate([imag_part, -real_part], 1)
    scale = 1.0 / LANES
    for part, rows in enumerate((right, left)):
        product = lax.dot_general(rows, right, NT, preferred_element_type=jnp.float32)
        out_ref[0, part] = (product * scale).astype(jnp.bfloat16)


def correlate(arrived, half, frame_count, st_count, ta_count, all_inputs):
    assert ta_count * frame_count == LANES
    return pl.pallas_call(
        functools.partial(correlate_kernel, half, st_count, ta_count),
        in_specs=[pl.BlockSpec(memory_space=pltpu.VMEM)],
        out_specs=pl.BlockSpec(memory_space=pltpu.VMEM),
        out_shape=jax.ShapeDtypeStruct((1, 2, all_inputs, all_inputs), jnp.bfloat16),
        scratch_shapes=[
            pltpu.VMEM((2, LANES, LANES), jnp.float32),
            pltpu.VMEM((2, LANES, LANES), jnp.float32),
            pltpu.VMEM((2 * all_inputs, LANES), jnp.float32),
        ],
        compiler_params=pltpu.CompilerParams(vmem_limit_bytes=32 * 1024 * 1024),
        name="correlate",
    )(arrived)


def on_device(samples, coefficients):
    st_count = lax.axis_size("st")
    ta_count = lax.axis_size("ta")
    inputs, frame_count, _ = samples.shape
    partial = channelize(samples, coefficients, st_count * ta_count)
    arrived = lax.all_to_all(partial, ("st", "ta"), split_axis=0, concat_axis=0, tiled=True)
    return correlate(arrived, coefficients.shape[0] // 2, frame_count, st_count, ta_count, st_count * inputs)


def solution(mesh):
    return jax.shard_map(
        on_device,
        mesh=mesh,
        in_specs=(P("st", "ta", None), P()),
        out_specs=P(("st", "ta"), None, None, None),
        check_vma=False,
    )
```

```python
import functools
import math

import jax
import jax.numpy as jnp
import numpy as np
from jax import lax
from jax.experimental import pallas as pl
from jax.experimental.pallas import tpu as pltpu
from jax.sharding import PartitionSpec as P

CH0 = 1024
LANES = 128
CHANNEL_BLOCK = 32
K_BLOCK = 2048
VMEM_LIMIT = 55000 * 1024
NT = (((1,), (1,)), ((), ()))


def phase_table(frame_len, channel_count, first_channel):
    channels = first_channel + np.arange(channel_count, dtype=np.int64)
    phases = (channels[:, None] * np.arange(frame_len, dtype=np.int64)[None, :]) % frame_len
    angles = 2.0 * math.pi / frame_len * phases
    parts = np.stack([np.cos(angles), -np.sin(angles)]) * frame_len**-0.5
    blocks = parts.reshape(2, channel_count // CHANNEL_BLOCK, CHANNEL_BLOCK, frame_len)
    return blocks.transpose(1, 0, 2, 3).reshape(-1, 2 * CHANNEL_BLOCK, frame_len).astype(np.float32)


def channelize_kernel(
    frame_count, x_hbm, coef_hbm, table_hbm, out_ref, x_in, coef_in, table_in, halves, folded, halves_odd, folded_odd, total, turned, sems
):
    block = pl.program_id(0)
    chunks, taps, k_block = coef_in.shape
    half = taps // 2
    rows = table_in.shape[1]
    pairs = frame_count // taps
    inputs = x_in.shape[1] // frame_count

    def copies(chunk):
        lanes = pl.ds(pl.multiple_of(chunk * k_block, k_block), k_block)
        return (
            pltpu.make_async_copy(coef_hbm.at[:, lanes], coef_in.at[chunk], sems.at[0, chunk]),
            pltpu.make_async_copy(table_hbm.at[block, :, lanes], table_in.at[chunk], sems.at[1, chunk]),
            pltpu.make_async_copy(x_hbm.at[:, lanes], x_in.at[chunk], sems.at[2, chunk]),
        )

    def start(chunk):
        for copy in copies(chunk):
            copy.start()

    def wait(chunk):
        for copy in copies(chunk):
            copy.wait()

    def form(chunk, halves, folded):
        table = table_in[chunk]
        for kind in range(3):
            for pair in range(pairs):
                for first in range(0, inputs, 2):
                    blocks = []
                    for place in (first, first + 1):
                        row = place * frame_count + pair * taps
                        blocks.append(x_in[chunk, row : row + taps, :].astype(jnp.float32))
                    even = jnp.concatenate([value[:half] for value in blocks], 0)
                    odd = jnp.concatenate([value[half:] for value in blocks], 0)
                    row = (pair * inputs + first) * half
                    halves[kind, row : row + taps, :] = (even, odd, even + odd)[kind].astype(jnp.bfloat16)
            for tap in range(half):
                low = coef_in[chunk, tap : tap + 1, :]
                high = coef_in[chunk, half + tap : half + tap + 1, :]
                coef = (high, low, low + high)[kind]
                folded[kind, tap * rows : (tap + 1) * rows, :] = (table * coef).astype(jnp.bfloat16)

    def multiply(chunk, halves, folded):
        for kind in range(3):
            total[chunk, kind] = lax.dot_general(folded[kind], halves[kind], NT, preferred_element_type=jnp.float32)

    start(0)
    start(1)
    wait(0)
    form(0, halves, folded)

    def two_chunks(turn, _):
        chunk = 2 * turn

        @pl.when(chunk + 2 < chunks)
        def _():
            start(chunk + 2)
            start(chunk + 3)

        wait(chunk + 1)
        multiply(chunk, halves, folded)
        form(chunk + 1, halves_odd, folded_odd)

        @pl.when(chunk + 2 < chunks)
        def _():
            wait(chunk + 2)

        multiply(chunk + 1, halves_odd, folded_odd)
        form(jnp.minimum(chunk + 2, chunks - 1), halves, folded)
        return 0

    lax.fori_loop(0, chunks // 2, two_chunks, 0)

    frame = lax.broadcasted_iota(jnp.int32, (rows, LANES), 1) % half

    def shifted_sum(kind, pair):
        lanes = slice(pair * LANES, (pair + 1) * LANES)

        def summed(tap):
            slots = [total[chunk, kind, tap * rows : (tap + 1) * rows, lanes] for chunk in range(total.shape[0])]
            return functools.reduce(jnp.add, slots)

        both = summed(0)
        inside = both
        for tap in range(1, half):
            moved = pltpu.roll(summed(tap), LANES - tap, 1)
            both = both + moved
            inside = inside + jnp.where(frame < half - tap, moved, 0.0)
        return inside, both - inside

    inside = {}
    before = {}
    for pair in range(pairs):
        (p0, c0), (p1, c1), (p2, c2) = (shifted_sum(kind, pair) for kind in range(3))
        for place, now, carry in (
            (2 * pair - 1, p0, c0),
            (2 * pair, p2 - p0 - p1, c2 - c0 - c1),
            (2 * pair + 1, p1, c1),
        ):
            inside[place] = inside[place] + now if place in inside else now
            before[place - 1] = before[place - 1] + carry if place - 1 in before else carry
    channels = rows // 2
    for place in range(-2, 2 * pairs):
        value = inside.get(place)
        if place in before:
            carry = pltpu.roll(before[place], half, 1)
            value = carry if value is None else value + carry
        for part in range(2):
            row, column = (place, part) if place >= 0 else (2 * part + place + 2, 2)
            turned[column, pl.ds(row, channels, stride=2 * pairs), :] = value[part * channels : (part + 1) * channels]
    for column in range(3):
        lanes = slice(column * LANES, (column + 1) * LANES)
        for channel in range(channels):
            block = turned[column, channel * 2 * pairs : (channel + 1) * 2 * pairs, :]
            out_ref[channel, :, lanes] = block.astype(jnp.bfloat16)


def channelize(samples, coefficients, channel_count):
    inputs, frame_count, frame_len = samples.shape
    taps = coefficients.shape[0]
    half = taps // 2
    rows = 2 * CHANNEL_BLOCK
    columns = inputs * frame_count
    blocks = channel_count // CHANNEL_BLOCK
    slots = frame_count // half
    assert slots == 4
    k_block = min(K_BLOCK, frame_len // 2)
    chunks = frame_len // k_block
    assert chunks % 2 == 0
    assert inputs * half == LANES and frame_count % taps == 0
    table = jnp.asarray(phase_table(frame_len, channel_count, CH0))
    return pl.pallas_call(
        functools.partial(channelize_kernel, frame_count),
        grid=(blocks,),
        in_specs=[pl.BlockSpec(memory_space=pl.ANY)] * 3,
        out_specs=pl.BlockSpec((CHANNEL_BLOCK, slots, 3 * LANES), lambda b: (b, 0, 0)),
        out_shape=jax.ShapeDtypeStruct((channel_count, slots, 3 * LANES), jnp.bfloat16),
        scratch_shapes=[
            pltpu.VMEM((chunks, columns, k_block), jnp.bfloat16),
            pltpu.VMEM((chunks, taps, k_block), jnp.float32),
            pltpu.VMEM((chunks, rows, k_block), jnp.float32),
            pltpu.VMEM((3, columns // 2, k_block), jnp.bfloat16),
            pltpu.VMEM((3, half * rows, k_block), jnp.bfloat16),
            pltpu.VMEM((3, columns // 2, k_block), jnp.bfloat16),
            pltpu.VMEM((3, half * rows, k_block), jnp.bfloat16),
            pltpu.VMEM((chunks, 3, half * rows, columns // 2), jnp.float32),
            pltpu.VMEM((3, CHANNEL_BLOCK * slots, LANES), jnp.float32),
            pltpu.SemaphoreType.DMA((3, chunks)),
        ],
        compiler_params=pltpu.CompilerParams(
            dimension_semantics=("arbitrary",), vmem_limit_bytes=VMEM_LIMIT
        ),
        cost_estimate=pl.CostEstimate(
            flops=3 * channel_count * taps * columns * frame_len,
            bytes_accessed=2 * columns * frame_len,
            transcendentals=0,
        ),
        name="channelize",
    )(samples.reshape(columns, frame_len), coefficients, table)


def correlate_kernel(half, st_count, ta_count, in_ref, out_ref, arranged, across, spectra):
    count = in_ref.shape[1]
    inputs = LANES // half
    places = ta_count * count
    stations = LANES // places
    all_inputs = st_count * inputs
    position = lax.broadcasted_iota(jnp.int32, (inputs, LANES), 1) // places

    def station_group(group):
        for place in range(stations):
            st = group * stations + place
            for ta in range(ta_count):
                row = place * places + ta * count
                own = in_ref[st * ta_count + ta].astype(jnp.float32)
                for part in range(2):
                    arranged[part, row : row + count, :] = own[:, part * LANES : (part + 1) * LANES]
                if ta < ta_count - 1:
                    ahead = in_ref[st * ta_count + ta + 1].astype(jnp.float32)[:, 2 * LANES :]
                    for part in range(2):
                        arranged[part, row + count - 2 : row + count, :] += ahead[2 * part : 2 * part + 2]
        for part in range(2):
            across[part] = arranged[part].T
            by_frame = [across[part, pl.ds(frame, inputs, stride=half), :] for frame in range(half)]
            for place in range(stations):
                result = None
                for frame in range(half):
                    shift = ((frame - place) * places) % LANES
                    value = pltpu.roll(by_frame[frame], shift, 1) if shift else by_frame[frame]
                    result = value if result is None else jnp.where(position == frame, value, result)
                first = part * all_inputs + (group * stations + place) * inputs
                if not isinstance(first, int):
                    first = pl.multiple_of(first, inputs)
                spectra[pl.ds(first, inputs), :] = result

    if st_count == stations:
        station_group(0)
    else:
        lax.fori_loop(0, st_count // stations, lambda group, _: (station_group(group), 0)[1], 0)
    real_part = spectra[:all_inputs, :].astype(jnp.bfloat16)
    imag_part = spectra[all_inputs:, :].astype(jnp.bfloat16)
    right = jnp.concatenate([real_part, imag_part], 1)
    left = jnp.concatenate([imag_part, -real_part], 1)
    scale = 1.0 / LANES
    for part, rows in enumerate((right, left)):
        product = lax.dot_general(rows, right, NT, preferred_element_type=jnp.float32)
        out_ref[0, part] = (product * scale).astype(jnp.bfloat16)


def correlate(arrived, half, frame_count, st_count, ta_count, all_inputs):
    assert ta_count * frame_count == LANES
    return pl.pallas_call(
        functools.partial(correlate_kernel, half, st_count, ta_count),
        in_specs=[pl.BlockSpec(memory_space=pltpu.VMEM)],
        out_specs=pl.BlockSpec(memory_space=pltpu.VMEM),
        out_shape=jax.ShapeDtypeStruct((1, 2, all_inputs, all_inputs), jnp.bfloat16),
        scratch_shapes=[
            pltpu.VMEM((2, LANES, LANES), jnp.float32),
            pltpu.VMEM((2, LANES, LANES), jnp.float32),
            pltpu.VMEM((2 * all_inputs, LANES), jnp.float32),
        ],
        compiler_params=pltpu.CompilerParams(vmem_limit_bytes=32 * 1024 * 1024),
        name="correlate",
    )(arrived)


def on_device(samples, coefficients):
    st_count = lax.axis_size("st")
    ta_count = lax.axis_size("ta")
    inputs, frame_count, _ = samples.shape
    partial = channelize(samples, coefficients, st_count * ta_count)
    arrived = lax.all_to_all(partial, ("st", "ta"), split_axis=0, concat_axis=0, tiled=True)
    return correlate(arrived, coefficients.shape[0] // 2, frame_count, st_count, ta_count, st_count * inputs)


def solution(mesh):
    return jax.shard_map(
        on_device,
        mesh=mesh,
        in_specs=(P("st", "ta", None), P()),
        out_specs=P(("st", "ta"), None, None, None),
        check_vma=False,
    )
```

```python
import functools
import math

import jax
import jax.numpy as jnp
import numpy as np
from jax import lax
from jax.experimental import pallas as pl
from jax.experimental.pallas import tpu as pltpu
from jax.sharding import PartitionSpec as P

CH0 = 1024
LANES = 128
CHANNEL_BLOCK = 32
K_BLOCK = 2048
VMEM_LIMIT = 55000 * 1024
NT = (((1,), (1,)), ((), ()))


def phase_table(frame_len, channel_count, first_channel):
    channels = first_channel + np.arange(channel_count, dtype=np.int64)
    phases = (channels[:, None] * np.arange(frame_len, dtype=np.int64)[None, :]) % frame_len
    angles = 2.0 * math.pi / frame_len * phases
    parts = np.stack([np.cos(angles), -np.sin(angles)]) * frame_len**-0.5
    blocks = parts.reshape(2, channel_count // CHANNEL_BLOCK, CHANNEL_BLOCK, frame_len)
    return blocks.transpose(1, 0, 2, 3).reshape(-1, 2 * CHANNEL_BLOCK, frame_len).astype(np.float32)


def channelize_kernel(frame_count, x_ref, coef_ref, table_ref, out_ref, halves, folded, total, turned):
    step = pl.program_id(1)
    taps = coef_ref.shape[0]
    half = taps // 2
    rows = table_ref.shape[1]
    pairs = frame_count // taps
    inputs = x_ref.shape[0] // frame_count

    table = table_ref[0]
    for pair in range(pairs):
        for first in range(0, inputs, 2):
            top, bottom = [
                x_ref[place * frame_count + pair * taps : place * frame_count + (pair + 1) * taps, :]
                for place in (first, first + 1)
            ]
            even = jnp.concatenate([top[:half], bottom[:half]], 0)
            odd = jnp.concatenate([top[half:], bottom[half:]], 0)
            row = (pair * inputs + first) * half
            halves[0, row : row + taps, :] = even
            halves[1, row : row + taps, :] = odd
            halves[2, row : row + taps, :] = even + odd
    for kind in range(3):
        for tap in range(half):
            low = coef_ref[tap : tap + 1, :]
            high = coef_ref[half + tap : half + tap + 1, :]
            coef = (high, low, low + high)[kind]
            folded[kind, tap * rows : (tap + 1) * rows, :] = (table * coef).astype(jnp.bfloat16)
        total[step, kind] = lax.dot_general(folded[kind], halves[kind], NT, preferred_element_type=jnp.float32)

    @pl.when(step == pl.num_programs(1) - 1)
    def _():
        frame = lax.broadcasted_iota(jnp.int32, (rows, LANES), 1) % half

        def shifted_sum(kind, pair):
            lanes = slice(pair * LANES, (pair + 1) * LANES)

            def summed(tap):
                slots = [total[chunk, kind, tap * rows : (tap + 1) * rows, lanes] for chunk in range(total.shape[0])]
                return functools.reduce(jnp.add, slots)

            both = summed(0)
            inside = both
            for tap in range(1, half):
                moved = pltpu.roll(summed(tap), LANES - tap, 1)
                both = both + moved
                inside = inside + jnp.where(frame < half - tap, moved, 0.0)
            return inside, both - inside

        inside = {}
        before = {}
        for pair in range(pairs):
            (p0, c0), (p1, c1), (p2, c2) = (shifted_sum(kind, pair) for kind in range(3))
            for place, now, carry in (
                (2 * pair - 1, p0, c0),
                (2 * pair, p2 - p0 - p1, c2 - c0 - c1),
                (2 * pair + 1, p1, c1),
            ):
                inside[place] = inside[place] + now if place in inside else now
                before[place - 1] = before[place - 1] + carry if place - 1 in before else carry
        channels = rows // 2
        for place in range(-2, 2 * pairs):
            value = inside.get(place)
            if place in before:
                carry = pltpu.roll(before[place], half, 1)
                value = carry if value is None else value + carry
            for part in range(2):
                row, column = (place, part) if place >= 0 else (2 * part + place + 2, 2)
                turned[column, pl.ds(row, channels, stride=2 * pairs), :] = value[part * channels : (part + 1) * channels]
        for column in range(3):
            lanes = slice(column * LANES, (column + 1) * LANES)
            for channel in range(channels):
                block = turned[column, channel * 2 * pairs : (channel + 1) * 2 * pairs, :]
                out_ref[channel, :, lanes] = block.astype(jnp.bfloat16)


def channelize(samples, coefficients, channel_count):
    inputs, frame_count, frame_len = samples.shape
    taps = coefficients.shape[0]
    half = taps // 2
    rows = 2 * CHANNEL_BLOCK
    columns = inputs * frame_count
    blocks = channel_count // CHANNEL_BLOCK
    slots = frame_count // half
    assert slots == 4
    k_block = min(K_BLOCK, frame_len)
    assert inputs * half == LANES and frame_count % taps == 0
    table = jnp.asarray(phase_table(frame_len, channel_count, CH0))
    return pl.pallas_call(
        functools.partial(channelize_kernel, frame_count),
        grid=(blocks, frame_len // k_block),
        in_specs=[
            pl.BlockSpec((columns, k_block), lambda b, k: (0, k)),
            pl.BlockSpec((taps, k_block), lambda b, k: (0, k)),
            pl.BlockSpec((1, rows, k_block), lambda b, k: (b, 0, k)),
        ],
        out_specs=pl.BlockSpec((CHANNEL_BLOCK, slots, 3 * LANES), lambda b, k: (b, 0, 0)),
        out_shape=jax.ShapeDtypeStruct((channel_count, slots, 3 * LANES), jnp.bfloat16),
        scratch_shapes=[
            pltpu.VMEM((3, columns // 2, k_block), jnp.bfloat16),
            pltpu.VMEM((3, half * rows, k_block), jnp.bfloat16),
            pltpu.VMEM((frame_len // k_block, 3, half * rows, columns // 2), jnp.float32),
            pltpu.VMEM((3, CHANNEL_BLOCK * slots, LANES), jnp.float32),
        ],
        compiler_params=pltpu.CompilerParams(
            dimension_semantics=("arbitrary", "arbitrary"), vmem_limit_bytes=VMEM_LIMIT
        ),
        cost_estimate=pl.CostEstimate(
            flops=3 * channel_count * taps * columns * frame_len,
            bytes_accessed=2 * columns * frame_len,
            transcendentals=0,
        ),
        name="channelize",
    )(samples.reshape(columns, frame_len), coefficients, table)


def correlate_kernel(half, st_count, ta_count, in_ref, out_ref, arranged, across, spectra):
    count = in_ref.shape[1]
    inputs = LANES // half
    places = ta_count * count
    stations = LANES // places
    all_inputs = st_count * inputs
    position = lax.broadcasted_iota(jnp.int32, (inputs, LANES), 1) // places

    def station_group(group):
        for place in range(stations):
            st = group * stations + place
            for ta in range(ta_count):
                row = place * places + ta * count
                own = in_ref[st * ta_count + ta].astype(jnp.float32)
                for part in range(2):
                    arranged[part, row : row + count, :] = own[:, part * LANES : (part + 1) * LANES]
                if ta < ta_count - 1:
                    ahead = in_ref[st * ta_count + ta + 1].astype(jnp.float32)[:, 2 * LANES :]
                    for part in range(2):
                        arranged[part, row + count - 2 : row + count, :] += ahead[2 * part : 2 * part + 2]
        for part in range(2):
            across[part] = arranged[part].T
            by_frame = [across[part, pl.ds(frame, inputs, stride=half), :] for frame in range(half)]
            for place in range(stations):
                result = None
                for frame in range(half):
                    shift = ((frame - place) * places) % LANES
                    value = pltpu.roll(by_frame[frame], shift, 1) if shift else by_frame[frame]
                    result = value if result is None else jnp.where(position == frame, value, result)
                first = part * all_inputs + (group * stations + place) * inputs
                if not isinstance(first, int):
                    first = pl.multiple_of(first, inputs)
                spectra[pl.ds(first, inputs), :] = result

    if st_count == stations:
        station_group(0)
    else:
        lax.fori_loop(0, st_count // stations, lambda group, _: (station_group(group), 0)[1], 0)
    real_part = spectra[:all_inputs, :].astype(jnp.bfloat16)
    imag_part = spectra[all_inputs:, :].astype(jnp.bfloat16)
    right = jnp.concatenate([real_part, imag_part], 1)
    left = jnp.concatenate([imag_part, -real_part], 1)
    scale = 1.0 / LANES
    for part, rows in enumerate((right, left)):
        product = lax.dot_general(rows, right, NT, preferred_element_type=jnp.float32)
        out_ref[0, part] = (product * scale).astype(jnp.bfloat16)


def correlate(arrived, half, frame_count, st_count, ta_count, all_inputs):
    assert ta_count * frame_count == LANES
    return pl.pallas_call(
        functools.partial(correlate_kernel, half, st_count, ta_count),
        in_specs=[pl.BlockSpec(memory_space=pltpu.VMEM)],
        out_specs=pl.BlockSpec(memory_space=pltpu.VMEM),
        out_shape=jax.ShapeDtypeStruct((1, 2, all_inputs, all_inputs), jnp.bfloat16),
        scratch_shapes=[
            pltpu.VMEM((2, LANES, LANES), jnp.float32),
            pltpu.VMEM((2, LANES, LANES), jnp.float32),
            pltpu.VMEM((2 * all_inputs, LANES), jnp.float32),
        ],
        compiler_params=pltpu.CompilerParams(vmem_limit_bytes=32 * 1024 * 1024),
        name="correlate",
    )(arrived)


def on_device(samples, coefficients):
    st_count = lax.axis_size("st")
    ta_count = lax.axis_size("ta")
    inputs, frame_count, _ = samples.shape
    partial = channelize(samples, coefficients, st_count * ta_count)
    arrived = lax.all_to_all(partial, ("st", "ta"), split_axis=0, concat_axis=0, tiled=True)
    return correlate(arrived, coefficients.shape[0] // 2, frame_count, st_count, ta_count, st_count * inputs)


def solution(mesh):
    return jax.shard_map(
        on_device,
        mesh=mesh,
        in_specs=(P("st", "ta", None), P()),
        out_specs=P(("st", "ta"), None, None, None),
        check_vma=False,
    )
```

```python
import functools
import math

import jax
import jax.numpy as jnp
import numpy as np
from jax import lax
from jax.experimental import pallas as pl
from jax.experimental.pallas import tpu as pltpu
from jax.sharding import PartitionSpec as P

CH0 = 1024
LANES = 128
CHANNEL_BLOCK = 32
K_BLOCK = 2048
VMEM_LIMIT = 55000 * 1024
NT = (((1,), (1,)), ((), ()))


def phase_table(frame_len, channel_count, first_channel):
    channels = first_channel + np.arange(channel_count, dtype=np.int64)
    phases = (channels[:, None] * np.arange(frame_len, dtype=np.int64)[None, :]) % frame_len
    angles = 2.0 * math.pi / frame_len * phases
    parts = np.stack([np.cos(angles), -np.sin(angles)]) * frame_len**-0.5
    blocks = parts.reshape(2, channel_count // CHANNEL_BLOCK, CHANNEL_BLOCK, frame_len)
    return blocks.transpose(1, 0, 2, 3).reshape(-1, 2 * CHANNEL_BLOCK, frame_len).astype(np.float32)


def channelize_kernel(frame_count, x_ref, coef_ref, table_ref, out_ref, halves, folded, total, turned):
    step = pl.program_id(1)
    taps = coef_ref.shape[0]
    half = taps // 2
    rows = table_ref.shape[1]
    pairs = frame_count // taps
    inputs = x_ref.shape[0] // frame_count

    table = table_ref[0]
    for pair in range(pairs):
        for first in range(0, inputs, 2):
            top, bottom = [
                x_ref[place * frame_count + pair * taps : place * frame_count + (pair + 1) * taps, :]
                for place in (first, first + 1)
            ]
            even = jnp.concatenate([top[:half], bottom[:half]], 0)
            odd = jnp.concatenate([top[half:], bottom[half:]], 0)
            row = (pair * inputs + first) * half
            halves[0, row : row + taps, :] = even
            halves[1, row : row + taps, :] = odd
            halves[2, row : row + taps, :] = even + odd
    for kind in range(3):
        for tap in range(half):
            low = coef_ref[tap : tap + 1, :]
            high = coef_ref[half + tap : half + tap + 1, :]
            coef = (high, low, low + high)[kind]
            folded[kind, tap * rows : (tap + 1) * rows, :] = (table * coef).astype(jnp.bfloat16)
        total[step, kind] = lax.dot_general(folded[kind], halves[kind], NT, preferred_element_type=jnp.float32)

    @pl.when(step == pl.num_programs(1) - 1)
    def _():
        frame = lax.broadcasted_iota(jnp.int32, (rows, LANES), 1) % half

        def shifted_sum(kind, pair):
            lanes = slice(pair * LANES, (pair + 1) * LANES)

            def summed(tap):
                slots = [total[chunk, kind, tap * rows : (tap + 1) * rows, lanes] for chunk in range(total.shape[0])]
                return functools.reduce(jnp.add, slots)

            both = summed(0)
            inside = both
            for tap in range(1, half):
                moved = pltpu.roll(summed(tap), LANES - tap, 1)
                both = both + moved
                inside = inside + jnp.where(frame < half - tap, moved, 0.0)
            return inside, both - inside

        inside = {}
        before = {}
        for pair in range(pairs):
            (p0, c0), (p1, c1), (p2, c2) = (shifted_sum(kind, pair) for kind in range(3))
            for place, now, carry in (
                (2 * pair - 1, p0, c0),
                (2 * pair, p2 - p0 - p1, c2 - c0 - c1),
                (2 * pair + 1, p1, c1),
            ):
                inside[place] = inside[place] + now if place in inside else now
                before[place - 1] = before[place - 1] + carry if place - 1 in before else carry
        channels = rows // 2
        for place in range(-2, 2 * pairs):
            value = inside.get(place)
            if place in before:
                carry = pltpu.roll(before[place], half, 1)
                value = carry if value is None else value + carry
            for part in range(2):
                row, column = (place, part) if place >= 0 else (2 * part + place + 2, 2)
                turned[column, pl.ds(row, channels, stride=2 * pairs), :] = value[part * channels : (part + 1) * channels]
        for column in range(3):
            lanes = slice(column * LANES, (column + 1) * LANES)
            for channel in range(channels):
                block = turned[column, channel * 2 * pairs : (channel + 1) * 2 * pairs, :]
                out_ref[channel, :, lanes] = block.astype(jnp.bfloat16)


def channelize(samples, coefficients, channel_count):
    inputs, frame_count, frame_len = samples.shape
    taps = coefficients.shape[0]
    half = taps // 2
    rows = 2 * CHANNEL_BLOCK
    columns = inputs * frame_count
    blocks = channel_count // CHANNEL_BLOCK
    slots = frame_count // half
    assert slots == 4
    k_block = min(K_BLOCK, frame_len)
    assert inputs * half == LANES and frame_count % taps == 0
    table = jnp.asarray(phase_table(frame_len, channel_count, CH0))
    return pl.pallas_call(
        functools.partial(channelize_kernel, frame_count),
        grid=(blocks, frame_len // k_block),
        in_specs=[
            pl.BlockSpec((columns, k_block), lambda b, k: (0, k)),
            pl.BlockSpec((taps, k_block), lambda b, k: (0, k)),
            pl.BlockSpec((1, rows, k_block), lambda b, k: (b, 0, k)),
        ],
        out_specs=pl.BlockSpec((CHANNEL_BLOCK, slots, 3 * LANES), lambda b, k: (b, 0, 0)),
        out_shape=jax.ShapeDtypeStruct((channel_count, slots, 3 * LANES), jnp.bfloat16),
        scratch_shapes=[
            pltpu.VMEM((3, columns // 2, k_block), jnp.bfloat16),
            pltpu.VMEM((3, half * rows, k_block), jnp.bfloat16),
            pltpu.VMEM((frame_len // k_block, 3, half * rows, columns // 2), jnp.float32),
            pltpu.VMEM((3, CHANNEL_BLOCK * slots, LANES), jnp.float32),
        ],
        compiler_params=pltpu.CompilerParams(
            dimension_semantics=("arbitrary", "arbitrary"), vmem_limit_bytes=VMEM_LIMIT
        ),
        cost_estimate=pl.CostEstimate(
            flops=3 * channel_count * taps * columns * frame_len,
            bytes_accessed=2 * columns * frame_len,
            transcendentals=0,
        ),
        name="channelize",
    )(samples.reshape(columns, frame_len), coefficients, table)


def correlate_kernel(half, st_count, ta_count, in_ref, out_ref, arranged, across, spectra):
    sources, count, _ = in_ref.shape
    inputs = LANES // half
    places = ta_count * count
    stations = LANES // places
    all_inputs = st_count * inputs
    position = lax.broadcasted_iota(jnp.int32, (inputs, LANES), 1) // places

    def plane(column):
        lanes = slice(column * LANES, (column + 1) * LANES)
        return in_ref[:, :, lanes].astype(jnp.float32).reshape(sources * count, LANES)

    row = lax.broadcasted_iota(jnp.int32, (sources * count, LANES), 0)
    takes = (row % count >= count - 2) & (row % places < places - count)
    ahead = plane(2)
    for part in range(2):
        moved = pltpu.roll(ahead, sources * count - (2 + 2 * part), 0)
        arranged[part] = plane(part) + jnp.where(takes, moved, 0.0)

    def station_group(group):
        for part in range(2):
            first = group * LANES
            if not isinstance(first, int):
                first = pl.multiple_of(first, LANES)
            across[part] = arranged[part, pl.ds(first, LANES), :].T
            by_frame = [across[part, pl.ds(frame, inputs, stride=half), :] for frame in range(half)]
            for place in range(stations):
                result = None
                for frame in range(half):
                    shift = ((frame - place) * places) % LANES
                    value = pltpu.roll(by_frame[frame], shift, 1) if shift else by_frame[frame]
                    result = value if result is None else jnp.where(position == frame, value, result)
                first = (group * stations + place) * inputs
                if not isinstance(first, int):
                    first = pl.multiple_of(first, inputs)
                spectra[part, pl.ds(first, inputs), :] = result

    if st_count == stations:
        station_group(0)
    else:
        lax.fori_loop(0, st_count // stations, lambda group, _: (station_group(group), 0)[1], 0)
    real_part = spectra[0].astype(jnp.bfloat16)
    imag_part = spectra[1].astype(jnp.bfloat16)
    right = jnp.concatenate([real_part, imag_part], 1)
    left = jnp.concatenate([imag_part, -real_part], 1)
    scale = 1.0 / LANES
    for part, rows in enumerate((right, left)):
        product = lax.dot_general(rows, right, NT, preferred_element_type=jnp.float32)
        out_ref[0, part] = (product * scale).astype(jnp.bfloat16)


def correlate(arrived, half, frame_count, st_count, ta_count, all_inputs):
    assert ta_count * frame_count == LANES
    return pl.pallas_call(
        functools.partial(correlate_kernel, half, st_count, ta_count),
        in_specs=[pl.BlockSpec(memory_space=pltpu.VMEM)],
        out_specs=pl.BlockSpec(memory_space=pltpu.VMEM),
        out_shape=jax.ShapeDtypeStruct((1, 2, all_inputs, all_inputs), jnp.bfloat16),
        scratch_shapes=[
            pltpu.VMEM((2, arrived.shape[0] * arrived.shape[1], LANES), jnp.float32),
            pltpu.VMEM((2, LANES, LANES), jnp.float32),
            pltpu.VMEM((2, all_inputs, LANES), jnp.float32),
        ],
        compiler_params=pltpu.CompilerParams(vmem_limit_bytes=32 * 1024 * 1024),
        name="correlate",
    )(arrived)


def on_device(samples, coefficients):
    st_count = lax.axis_size("st")
    ta_count = lax.axis_size("ta")
    inputs, frame_count, _ = samples.shape
    partial = channelize(samples, coefficients, st_count * ta_count)
    arrived = lax.all_to_all(partial, ("st", "ta"), split_axis=0, concat_axis=0, tiled=True)
    return correlate(arrived, coefficients.shape[0] // 2, frame_count, st_count, ta_count, st_count * inputs)


def solution(mesh):
    return jax.shard_map(
        on_device,
        mesh=mesh,
        in_specs=(P("st", "ta", None), P()),
        out_specs=P(("st", "ta"), None, None, None),
        check_vma=False,
    )
```

```python
import functools
import math

import jax
import jax.numpy as jnp
import numpy as np
from jax import lax
from jax.experimental import pallas as pl
from jax.experimental.pallas import tpu as pltpu
from jax.sharding import PartitionSpec as P

CH0 = 1024
LANES = 128
CHANNEL_BLOCK = 32
K_BLOCK = 2048
VMEM_LIMIT = 55000 * 1024
NT = (((1,), (1,)), ((), ()))


def phase_table(frame_len, channel_count, first_channel):
    channels = first_channel + np.arange(channel_count, dtype=np.int64)
    phases = (channels[:, None] * np.arange(frame_len, dtype=np.int64)[None, :]) % frame_len
    angles = 2.0 * math.pi / frame_len * phases
    parts = np.stack([np.cos(angles), -np.sin(angles)]) * frame_len**-0.5
    blocks = parts.reshape(2, channel_count // CHANNEL_BLOCK, CHANNEL_BLOCK, frame_len)
    return blocks.transpose(1, 0, 2, 3).reshape(-1, 2 * CHANNEL_BLOCK, frame_len).astype(np.float32)


def channelize_kernel(frame_count, x_ref, coef_ref, table_ref, out_ref, halves, folded, total, sums, turned):
    step = pl.program_id(1)
    taps = coef_ref.shape[0]
    half = taps // 2
    rows = table_ref.shape[1]
    pairs = frame_count // taps
    inputs = x_ref.shape[0] // frame_count

    table = table_ref[0]
    for pair in range(pairs):
        for first in range(0, inputs, 2):
            top, bottom = [
                x_ref[place * frame_count + pair * taps : place * frame_count + (pair + 1) * taps, :]
                for place in (first, first + 1)
            ]
            even = jnp.concatenate([top[:half], bottom[:half]], 0)
            odd = jnp.concatenate([top[half:], bottom[half:]], 0)
            row = (pair * inputs + first) * half
            halves[0, row : row + taps, :] = even
            halves[1, row : row + taps, :] = odd
            halves[2, row : row + taps, :] = even + odd
    for kind in range(3):
        for tap in range(half):
            low = coef_ref[tap : tap + 1, :]
            high = coef_ref[half + tap : half + tap + 1, :]
            coef = (high, low, low + high)[kind]
            folded[kind, tap * rows : (tap + 1) * rows, :] = (table * coef).astype(jnp.bfloat16)
        total[step, kind] = lax.dot_general(folded[kind], halves[kind], NT, preferred_element_type=jnp.float32)

    @pl.when(step == pl.num_programs(1) - 1)
    def _():
        frame = lax.broadcasted_iota(jnp.int32, (rows, LANES), 1) % half

        def shifted_sum(index, _):
            kind, pair = index // pairs, index % pairs
            lanes = pl.ds(pl.multiple_of(pair * LANES, LANES), LANES)

            def summed(tap):
                slots = [total[chunk, kind, tap * rows : (tap + 1) * rows, lanes] for chunk in range(total.shape[0])]
                return functools.reduce(jnp.add, slots)

            both = summed(0)
            within = both
            for tap in range(1, half):
                moved = pltpu.roll(summed(tap), LANES - tap, 1)
                both = both + moved
                within = within + jnp.where(frame < half - tap, moved, 0.0)
            sums[index, 0] = within
            sums[index, 1] = both - within
            return 0

        lax.fori_loop(0, 3 * pairs, shifted_sum, 0)
        inside = {}
        before = {}
        for pair in range(pairs):
            (p0, c0), (p1, c1), (p2, c2) = ((sums[kind * pairs + pair, 0], sums[kind * pairs + pair, 1]) for kind in range(3))
            for place, now, carry in (
                (2 * pair - 1, p0, c0),
                (2 * pair, p2 - p0 - p1, c2 - c0 - c1),
                (2 * pair + 1, p1, c1),
            ):
                inside[place] = inside[place] + now if place in inside else now
                before[place - 1] = before[place - 1] + carry if place - 1 in before else carry
        channels = rows // 2
        for place in range(-2, 2 * pairs):
            value = inside.get(place)
            if place in before:
                carry = pltpu.roll(before[place], half, 1)
                value = carry if value is None else value + carry
            for part in range(2):
                row, column = (place, part) if place >= 0 else (2 * part + place + 2, 2)
                turned[column, pl.ds(row, channels, stride=2 * pairs), :] = value[part * channels : (part + 1) * channels]
        for column in range(3):
            lanes = slice(column * LANES, (column + 1) * LANES)
            for channel in range(channels):
                block = turned[column, channel * 2 * pairs : (channel + 1) * 2 * pairs, :]
                out_ref[channel, :, lanes] = block.astype(jnp.bfloat16)


def channelize(samples, coefficients, channel_count):
    inputs, frame_count, frame_len = samples.shape
    taps = coefficients.shape[0]
    half = taps // 2
    rows = 2 * CHANNEL_BLOCK
    columns = inputs * frame_count
    blocks = channel_count // CHANNEL_BLOCK
    slots = frame_count // half
    assert slots == 4
    k_block = min(K_BLOCK, frame_len)
    assert inputs * half == LANES and frame_count % taps == 0
    table = jnp.asarray(phase_table(frame_len, channel_count, CH0))
    return pl.pallas_call(
        functools.partial(channelize_kernel, frame_count),
        grid=(blocks, frame_len // k_block),
        in_specs=[
            pl.BlockSpec((columns, k_block), lambda b, k: (0, k)),
            pl.BlockSpec((taps, k_block), lambda b, k: (0, k)),
            pl.BlockSpec((1, rows, k_block), lambda b, k: (b, 0, k)),
        ],
        out_specs=pl.BlockSpec((CHANNEL_BLOCK, slots, 3 * LANES), lambda b, k: (b, 0, 0)),
        out_shape=jax.ShapeDtypeStruct((channel_count, slots, 3 * LANES), jnp.bfloat16),
        scratch_shapes=[
            pltpu.VMEM((3, columns // 2, k_block), jnp.bfloat16),
            pltpu.VMEM((3, half * rows, k_block), jnp.bfloat16),
            pltpu.VMEM((frame_len // k_block, 3, half * rows, columns // 2), jnp.float32),
            pltpu.VMEM((3 * frame_count // taps, 2, rows, LANES), jnp.float32),
            pltpu.VMEM((3, CHANNEL_BLOCK * slots, LANES), jnp.float32),
        ],
        compiler_params=pltpu.CompilerParams(
            dimension_semantics=("arbitrary", "arbitrary"), vmem_limit_bytes=VMEM_LIMIT
        ),
        cost_estimate=pl.CostEstimate(
            flops=3 * channel_count * taps * columns * frame_len,
            bytes_accessed=2 * columns * frame_len,
            transcendentals=0,
        ),
        name="channelize",
    )(samples.reshape(columns, frame_len), coefficients, table)


def correlate_kernel(half, st_count, ta_count, in_ref, out_ref, arranged, across, spectra):
    count = in_ref.shape[1]
    inputs = LANES // half
    places = ta_count * count
    stations = LANES // places
    all_inputs = st_count * inputs
    position = lax.broadcasted_iota(jnp.int32, (inputs, LANES), 1) // places

    def station_group(group):
        for place in range(stations):
            st = group * stations + place
            for ta in range(ta_count):
                row = place * places + ta * count
                own = in_ref[st * ta_count + ta].astype(jnp.float32)
                for part in range(2):
                    arranged[part, row : row + count, :] = own[:, part * LANES : (part + 1) * LANES]
                if ta < ta_count - 1:
                    ahead = in_ref[st * ta_count + ta + 1].astype(jnp.float32)[:, 2 * LANES :]
                    for part in range(2):
                        arranged[part, row + count - 2 : row + count, :] += ahead[2 * part : 2 * part + 2]
        for part in range(2):
            across[part] = arranged[part].T
            by_frame = [across[part, pl.ds(frame, inputs, stride=half), :] for frame in range(half)]
            for place in range(stations):
                result = None
                for frame in range(half):
                    shift = ((frame - place) * places) % LANES
                    value = pltpu.roll(by_frame[frame], shift, 1) if shift else by_frame[frame]
                    result = value if result is None else jnp.where(position == frame, value, result)
                first = part * all_inputs + (group * stations + place) * inputs
                if not isinstance(first, int):
                    first = pl.multiple_of(first, inputs)
                spectra[pl.ds(first, inputs), :] = result

    if st_count == stations:
        station_group(0)
    else:
        lax.fori_loop(0, st_count // stations, lambda group, _: (station_group(group), 0)[1], 0)
    real_part = spectra[:all_inputs, :].astype(jnp.bfloat16)
    imag_part = spectra[all_inputs:, :].astype(jnp.bfloat16)
    right = jnp.concatenate([real_part, imag_part], 1)
    left = jnp.concatenate([imag_part, -real_part], 1)
    scale = 1.0 / LANES
    for part, rows in enumerate((right, left)):
        product = lax.dot_general(rows, right, NT, preferred_element_type=jnp.float32)
        out_ref[0, part] = (product * scale).astype(jnp.bfloat16)


def correlate(arrived, half, frame_count, st_count, ta_count, all_inputs):
    assert ta_count * frame_count == LANES
    return pl.pallas_call(
        functools.partial(correlate_kernel, half, st_count, ta_count),
        in_specs=[pl.BlockSpec(memory_space=pltpu.VMEM)],
        out_specs=pl.BlockSpec(memory_space=pltpu.VMEM),
        out_shape=jax.ShapeDtypeStruct((1, 2, all_inputs, all_inputs), jnp.bfloat16),
        scratch_shapes=[
            pltpu.VMEM((2, LANES, LANES), jnp.float32),
            pltpu.VMEM((2, LANES, LANES), jnp.float32),
            pltpu.VMEM((2 * all_inputs, LANES), jnp.float32),
        ],
        compiler_params=pltpu.CompilerParams(vmem_limit_bytes=32 * 1024 * 1024),
        name="correlate",
    )(arrived)


def on_device(samples, coefficients):
    st_count = lax.axis_size("st")
    ta_count = lax.axis_size("ta")
    inputs, frame_count, _ = samples.shape
    partial = channelize(samples, coefficients, st_count * ta_count)
    arrived = lax.all_to_all(partial, ("st", "ta"), split_axis=0, concat_axis=0, tiled=True)
    return correlate(arrived, coefficients.shape[0] // 2, frame_count, st_count, ta_count, st_count * inputs)


def solution(mesh):
    return jax.shard_map(
        on_device,
        mesh=mesh,
        in_specs=(P("st", "ta", None), P()),
        out_specs=P(("st", "ta"), None, None, None),
        check_vma=False,
    )
```

```python
import functools
import math

import jax
import jax.numpy as jnp
import numpy as np
from jax import lax
from jax.experimental import pallas as pl
from jax.experimental.pallas import tpu as pltpu
from jax.sharding import PartitionSpec as P

CH0 = 1024
LANES = 128
CHANNEL_BLOCK = 32
K_BLOCK = 2048
ROW_GROUP = 16
VMEM_LIMIT = 55000 * 1024
NT = (((1,), (1,)), ((), ()))


def phase_table(frame_len, channel_count, first_channel):
    channels = first_channel + np.arange(channel_count, dtype=np.int64)
    phases = (channels[:, None] * np.arange(frame_len, dtype=np.int64)[None, :]) % frame_len
    angles = 2.0 * math.pi / frame_len * phases
    parts = np.stack([np.cos(angles), -np.sin(angles)]) * frame_len**-0.5
    blocks = parts.reshape(2, channel_count // CHANNEL_BLOCK, CHANNEL_BLOCK, frame_len)
    return blocks.transpose(1, 0, 2, 3).reshape(-1, 2 * CHANNEL_BLOCK, frame_len).astype(np.float32)


def channelize_kernel(frame_count, x_ref, coef_ref, table_ref, out_ref, halves, folded, total, turned):
    step = pl.program_id(1)
    taps = coef_ref.shape[0]
    half = taps // 2
    rows = table_ref.shape[1]
    pairs = frame_count // taps
    inputs = x_ref.shape[0] // frame_count

    table = table_ref[0]
    for pair in range(pairs):
        for first in range(0, inputs, 2):
            top, bottom = [
                x_ref[place * frame_count + pair * taps : place * frame_count + (pair + 1) * taps, :]
                for place in (first, first + 1)
            ]
            even = jnp.concatenate([top[:half], bottom[:half]], 0)
            odd = jnp.concatenate([top[half:], bottom[half:]], 0)
            row = (pair * inputs + first) * half
            halves[0, row : row + taps, :] = even
            halves[1, row : row + taps, :] = odd
            halves[2, row : row + taps, :] = even + odd
    for kind in range(3):
        for tap in range(half):
            low = coef_ref[tap : tap + 1, :]
            high = coef_ref[half + tap : half + tap + 1, :]
            coef = (high, low, low + high)[kind]
            folded[kind, tap * rows : (tap + 1) * rows, :] = (table * coef).astype(jnp.bfloat16)
        total[step, kind] = lax.dot_general(folded[kind], halves[kind], NT, preferred_element_type=jnp.float32)

    @pl.when(step == pl.num_programs(1) - 1)
    def _():
        channels = rows // 2
        count = 2 * pairs
        frame = lax.broadcasted_iota(jnp.int32, (ROW_GROUP, LANES), 1) % half
        for group in range(0, rows, ROW_GROUP):
            part, channel = group // channels, group % channels

            def summed(kind, pair, tap):
                rows_of = slice(tap * rows + group, tap * rows + group + ROW_GROUP)
                lanes = slice(pair * LANES, (pair + 1) * LANES)
                return functools.reduce(jnp.add, [total[c, kind, rows_of, lanes] for c in range(total.shape[0])])

            inside = {}
            outside = {}
            for tap in range(half):
                at = {}
                for pair in range(pairs):
                    high, low, mixed = (summed(kind, pair, tap) for kind in range(3))
                    before = 2 * pair - 1
                    at[before] = at[before] + high if before in at else high
                    at[2 * pair] = mixed - high - low
                    at[2 * pair + 1] = low
                for place, value in at.items():
                    if tap == 0:
                        inside[place] = value
                        continue
                    moved = pltpu.roll(value, LANES - tap, 1)
                    stays = frame < half - tap
                    inside[place] = inside[place] + jnp.where(stays, moved, 0.0)
                    leaves = jnp.where(stays, 0.0, moved)
                    outside[place] = outside[place] + leaves if place in outside else leaves
            for place in range(-2, count):
                value = inside.get(place)
                if place + 1 in outside:
                    carry = pltpu.roll(outside[place + 1], half, 1)
                    value = carry if value is None else value + carry
                row, column = (place, part) if place >= 0 else (2 * part + place + 2, 2)
                turned[column, pl.ds(channel * count + row, ROW_GROUP, stride=count), :] = value
        for column in range(3):
            lanes = slice(column * LANES, (column + 1) * LANES)
            for channel in range(channels):
                block = turned[column, channel * count : (channel + 1) * count, :]
                out_ref[channel, :, lanes] = block.astype(jnp.bfloat16)


def channelize(samples, coefficients, channel_count):
    inputs, frame_count, frame_len = samples.shape
    taps = coefficients.shape[0]
    half = taps // 2
    rows = 2 * CHANNEL_BLOCK
    columns = inputs * frame_count
    blocks = channel_count // CHANNEL_BLOCK
    slots = frame_count // half
    assert slots == 4
    k_block = min(K_BLOCK, frame_len)
    assert inputs * half == LANES and frame_count % taps == 0
    table = jnp.asarray(phase_table(frame_len, channel_count, CH0))
    return pl.pallas_call(
        functools.partial(channelize_kernel, frame_count),
        grid=(blocks, frame_len // k_block),
        in_specs=[
            pl.BlockSpec((columns, k_block), lambda b, k: (0, k)),
            pl.BlockSpec((taps, k_block), lambda b, k: (0, k)),
            pl.BlockSpec((1, rows, k_block), lambda b, k: (b, 0, k)),
        ],
        out_specs=pl.BlockSpec((CHANNEL_BLOCK, slots, 3 * LANES), lambda b, k: (b, 0, 0)),
        out_shape=jax.ShapeDtypeStruct((channel_count, slots, 3 * LANES), jnp.bfloat16),
        scratch_shapes=[
            pltpu.VMEM((3, columns // 2, k_block), jnp.bfloat16),
            pltpu.VMEM((3, half * rows, k_block), jnp.bfloat16),
            pltpu.VMEM((frame_len // k_block, 3, half * rows, columns // 2), jnp.float32),
            pltpu.VMEM((3, CHANNEL_BLOCK * slots, LANES), jnp.float32),
        ],
        compiler_params=pltpu.CompilerParams(
            dimension_semantics=("arbitrary", "arbitrary"), vmem_limit_bytes=VMEM_LIMIT
        ),
        cost_estimate=pl.CostEstimate(
            flops=3 * channel_count * taps * columns * frame_len,
            bytes_accessed=2 * columns * frame_len,
            transcendentals=0,
        ),
        name="channelize",
    )(samples.reshape(columns, frame_len), coefficients, table)


def correlate_kernel(half, st_count, ta_count, in_ref, out_ref, arranged, across, spectra):
    count = in_ref.shape[1]
    inputs = LANES // half
    places = ta_count * count
    stations = LANES // places
    all_inputs = st_count * inputs
    position = lax.broadcasted_iota(jnp.int32, (inputs, LANES), 1) // places

    def station_group(group):
        for place in range(stations):
            st = group * stations + place
            for ta in range(ta_count):
                row = place * places + ta * count
                own = in_ref[st * ta_count + ta].astype(jnp.float32)
                for part in range(2):
                    arranged[part, row : row + count, :] = own[:, part * LANES : (part + 1) * LANES]
                if ta < ta_count - 1:
                    ahead = in_ref[st * ta_count + ta + 1].astype(jnp.float32)[:, 2 * LANES :]
                    for part in range(2):
                        arranged[part, row + count - 2 : row + count, :] += ahead[2 * part : 2 * part + 2]
        for part in range(2):
            across[part] = arranged[part].T
            by_frame = [across[part, pl.ds(frame, inputs, stride=half), :] for frame in range(half)]
            for place in range(stations):
                result = None
                for frame in range(half):
                    shift = ((frame - place) * places) % LANES
                    value = pltpu.roll(by_frame[frame], shift, 1) if shift else by_frame[frame]
                    result = value if result is None else jnp.where(position == frame, value, result)
                first = part * all_inputs + (group * stations + place) * inputs
                if not isinstance(first, int):
                    first = pl.multiple_of(first, inputs)
                spectra[pl.ds(first, inputs), :] = result

    if st_count == stations:
        station_group(0)
    else:
        lax.fori_loop(0, st_count // stations, lambda group, _: (station_group(group), 0)[1], 0)
    real_part = spectra[:all_inputs, :].astype(jnp.bfloat16)
    imag_part = spectra[all_inputs:, :].astype(jnp.bfloat16)
    right = jnp.concatenate([real_part, imag_part], 1)
    left = jnp.concatenate([imag_part, -real_part], 1)
    scale = 1.0 / LANES
    for part, rows in enumerate((right, left)):
        product = lax.dot_general(rows, right, NT, preferred_element_type=jnp.float32)
        out_ref[0, part] = (product * scale).astype(jnp.bfloat16)


def correlate(arrived, half, frame_count, st_count, ta_count, all_inputs):
    assert ta_count * frame_count == LANES
    return pl.pallas_call(
        functools.partial(correlate_kernel, half, st_count, ta_count),
        in_specs=[pl.BlockSpec(memory_space=pltpu.VMEM)],
        out_specs=pl.BlockSpec(memory_space=pltpu.VMEM),
        out_shape=jax.ShapeDtypeStruct((1, 2, all_inputs, all_inputs), jnp.bfloat16),
        scratch_shapes=[
            pltpu.VMEM((2, LANES, LANES), jnp.float32),
            pltpu.VMEM((2, LANES, LANES), jnp.float32),
            pltpu.VMEM((2 * all_inputs, LANES), jnp.float32),
        ],
        compiler_params=pltpu.CompilerParams(vmem_limit_bytes=32 * 1024 * 1024),
        name="correlate",
    )(arrived)


def on_device(samples, coefficients):
    st_count = lax.axis_size("st")
    ta_count = lax.axis_size("ta")
    inputs, frame_count, _ = samples.shape
    partial = channelize(samples, coefficients, st_count * ta_count)
    arrived = lax.all_to_all(partial, ("st", "ta"), split_axis=0, concat_axis=0, tiled=True)
    return correlate(arrived, coefficients.shape[0] // 2, frame_count, st_count, ta_count, st_count * inputs)


def solution(mesh):
    return jax.shard_map(
        on_device,
        mesh=mesh,
        in_specs=(P("st", "ta", None), P()),
        out_specs=P(("st", "ta"), None, None, None),
        check_vma=False,
    )
```

```python
import functools
import math

import jax
import jax.numpy as jnp
import numpy as np
from jax import lax
from jax.experimental import pallas as pl
from jax.experimental.pallas import tpu as pltpu
from jax.sharding import PartitionSpec as P

CH0 = 1024
LANES = 128
CHANNEL_BLOCK = 32
K_BLOCK = 2048
VMEM_LIMIT = 55000 * 1024
NT = (((1,), (1,)), ((), ()))


def phase_table(frame_len, channel_count, first_channel):
    channels = first_channel + np.arange(channel_count, dtype=np.int64)
    phases = (channels[:, None] * np.arange(frame_len, dtype=np.int64)[None, :]) % frame_len
    angles = 2.0 * math.pi / frame_len * phases
    parts = np.stack([np.cos(angles), -np.sin(angles)]) * frame_len**-0.5
    blocks = parts.reshape(2, channel_count // CHANNEL_BLOCK, CHANNEL_BLOCK, frame_len)
    return blocks.transpose(1, 0, 2, 3).reshape(-1, 2 * CHANNEL_BLOCK, frame_len).astype(np.float32)


def channelize_kernel(frame_count, x_ref, coef_ref, table_ref, out_ref, halves, folded, total, turned):
    step = pl.program_id(1)
    taps = coef_ref.shape[0]
    half = taps // 2
    rows = table_ref.shape[1]
    pairs = frame_count // taps
    inputs = x_ref.shape[0] // frame_count

    table = table_ref[0]
    for pair in range(pairs):
        for first in range(0, inputs, 2):
            top, bottom = [
                x_ref[place * frame_count + pair * taps : place * frame_count + (pair + 1) * taps, :]
                for place in (first, first + 1)
            ]
            even = jnp.concatenate([top[:half], bottom[:half]], 0)
            odd = jnp.concatenate([top[half:], bottom[half:]], 0)
            row = (pair * inputs + first) * half
            halves[0, row : row + taps, :] = even
            halves[1, row : row + taps, :] = odd
            halves[2, row : row + taps, :] = even + odd
    for kind in range(3):
        for tap in range(half):
            low = coef_ref[tap : tap + 1, :]
            high = coef_ref[half + tap : half + tap + 1, :]
            coef = (high, low, low + high)[kind]
            folded[kind, tap * rows : (tap + 1) * rows, :] = (table * coef).astype(jnp.bfloat16)
        total[step, kind] = lax.dot_general(folded[kind], halves[kind], NT, preferred_element_type=jnp.float32)

    @pl.when(step == pl.num_programs(1) - 1)
    def _():
        frame = lax.broadcasted_iota(jnp.int32, (rows, LANES), 1) % half

        def shifted_sum(kind, pair):
            lanes = slice(pair * LANES, (pair + 1) * LANES)

            def summed(tap):
                slots = [total[chunk, kind, tap * rows : (tap + 1) * rows, lanes] for chunk in range(total.shape[0])]
                return functools.reduce(jnp.add, slots)

            both = summed(0)
            inside = both
            for tap in range(1, half):
                moved = pltpu.roll(summed(tap), LANES - tap, 1)
                both = both + moved
                inside = inside + jnp.where(frame < half - tap, moved, 0.0)
            return inside, both - inside

        inside = {}
        before = {}
        for pair in range(pairs):
            (p0, c0), (p1, c1), (p2, c2) = (shifted_sum(kind, pair) for kind in range(3))
            for place, now, carry in (
                (2 * pair - 1, p0, c0),
                (2 * pair, p2 - p0 - p1, c2 - c0 - c1),
                (2 * pair + 1, p1, c1),
            ):
                inside[place] = inside[place] + now if place in inside else now
                before[place - 1] = before[place - 1] + carry if place - 1 in before else carry
        channels = rows // 2
        for place in range(-2, 2 * pairs):
            value = inside.get(place)
            if place in before:
                carry = pltpu.roll(before[place], half, 1)
                value = carry if value is None else value + carry
            for part in range(2):
                row, column = (place, part) if place >= 0 else (2 * part + place + 2, 2)
                turned[column, pl.ds(row, channels, stride=2 * pairs), :] = value[part * channels : (part + 1) * channels]
        for column in range(3):
            lanes = slice(column * LANES, (column + 1) * LANES)
            out_ref[:, :, lanes] = turned[column].reshape(channels, 2 * pairs, LANES).astype(jnp.bfloat16)


def channelize(samples, coefficients, channel_count):
    inputs, frame_count, frame_len = samples.shape
    taps = coefficients.shape[0]
    half = taps // 2
    rows = 2 * CHANNEL_BLOCK
    columns = inputs * frame_count
    blocks = channel_count // CHANNEL_BLOCK
    slots = frame_count // half
    assert slots == 4
    k_block = min(K_BLOCK, frame_len)
    assert inputs * half == LANES and frame_count % taps == 0
    table = jnp.asarray(phase_table(frame_len, channel_count, CH0))
    return pl.pallas_call(
        functools.partial(channelize_kernel, frame_count),
        grid=(blocks, frame_len // k_block),
        in_specs=[
            pl.BlockSpec((columns, k_block), lambda b, k: (0, k)),
            pl.BlockSpec((taps, k_block), lambda b, k: (0, k)),
            pl.BlockSpec((1, rows, k_block), lambda b, k: (b, 0, k)),
        ],
        out_specs=pl.BlockSpec((CHANNEL_BLOCK, slots, 3 * LANES), lambda b, k: (b, 0, 0)),
        out_shape=jax.ShapeDtypeStruct((channel_count, slots, 3 * LANES), jnp.bfloat16),
        scratch_shapes=[
            pltpu.VMEM((3, columns // 2, k_block), jnp.bfloat16),
            pltpu.VMEM((3, half * rows, k_block), jnp.bfloat16),
            pltpu.VMEM((frame_len // k_block, 3, half * rows, columns // 2), jnp.float32),
            pltpu.VMEM((3, CHANNEL_BLOCK * slots, LANES), jnp.float32),
        ],
        compiler_params=pltpu.CompilerParams(
            dimension_semantics=("arbitrary", "arbitrary"), vmem_limit_bytes=VMEM_LIMIT
        ),
        cost_estimate=pl.CostEstimate(
            flops=3 * channel_count * taps * columns * frame_len,
            bytes_accessed=2 * columns * frame_len,
            transcendentals=0,
        ),
        name="channelize",
    )(samples.reshape(columns, frame_len), coefficients, table)


def correlate_kernel(half, st_count, ta_count, in_ref, out_ref, arranged, across, spectra):
    count = in_ref.shape[1]
    inputs = LANES // half
    places = ta_count * count
    stations = LANES // places
    all_inputs = st_count * inputs
    position = lax.broadcasted_iota(jnp.int32, (inputs, LANES), 1) // places

    def station_group(group):
        for place in range(stations):
            st = group * stations + place
            for ta in range(ta_count):
                row = place * places + ta * count
                own = in_ref[st * ta_count + ta].astype(jnp.float32)
                for part in range(2):
                    arranged[part, row : row + count, :] = own[:, part * LANES : (part + 1) * LANES]
                if ta < ta_count - 1:
                    ahead = in_ref[st * ta_count + ta + 1].astype(jnp.float32)[:, 2 * LANES :]
                    for part in range(2):
                        arranged[part, row + count - 2 : row + count, :] += ahead[2 * part : 2 * part + 2]
        for part in range(2):
            across[part] = arranged[part].T
            by_frame = [across[part, pl.ds(frame, inputs, stride=half), :] for frame in range(half)]
            for place in range(stations):
                result = None
                for frame in range(half):
                    shift = ((frame - place) * places) % LANES
                    value = pltpu.roll(by_frame[frame], shift, 1) if shift else by_frame[frame]
                    result = value if result is None else jnp.where(position == frame, value, result)
                first = part * all_inputs + (group * stations + place) * inputs
                if not isinstance(first, int):
                    first = pl.multiple_of(first, inputs)
                spectra[pl.ds(first, inputs), :] = result

    if st_count == stations:
        station_group(0)
    else:
        lax.fori_loop(0, st_count // stations, lambda group, _: (station_group(group), 0)[1], 0)
    real_part = spectra[:all_inputs, :].astype(jnp.bfloat16)
    imag_part = spectra[all_inputs:, :].astype(jnp.bfloat16)
    right = jnp.concatenate([real_part, imag_part], 1)
    left = jnp.concatenate([imag_part, -real_part], 1)
    scale = 1.0 / LANES
    for part, rows in enumerate((right, left)):
        product = lax.dot_general(rows, right, NT, preferred_element_type=jnp.float32)
        out_ref[0, part] = (product * scale).astype(jnp.bfloat16)


def correlate(arrived, half, frame_count, st_count, ta_count, all_inputs):
    assert ta_count * frame_count == LANES
    return pl.pallas_call(
        functools.partial(correlate_kernel, half, st_count, ta_count),
        in_specs=[pl.BlockSpec(memory_space=pltpu.VMEM)],
        out_specs=pl.BlockSpec(memory_space=pltpu.VMEM),
        out_shape=jax.ShapeDtypeStruct((1, 2, all_inputs, all_inputs), jnp.bfloat16),
        scratch_shapes=[
            pltpu.VMEM((2, LANES, LANES), jnp.float32),
            pltpu.VMEM((2, LANES, LANES), jnp.float32),
            pltpu.VMEM((2 * all_inputs, LANES), jnp.float32),
        ],
        compiler_params=pltpu.CompilerParams(vmem_limit_bytes=32 * 1024 * 1024),
        name="correlate",
    )(arrived)


def on_device(samples, coefficients):
    st_count = lax.axis_size("st")
    ta_count = lax.axis_size("ta")
    inputs, frame_count, _ = samples.shape
    partial = channelize(samples, coefficients, st_count * ta_count)
    arrived = lax.all_to_all(partial, ("st", "ta"), split_axis=0, concat_axis=0, tiled=True)
    return correlate(arrived, coefficients.shape[0] // 2, frame_count, st_count, ta_count, st_count * inputs)


def solution(mesh):
    return jax.shard_map(
        on_device,
        mesh=mesh,
        in_specs=(P("st", "ta", None), P()),
        out_specs=P(("st", "ta"), None, None, None),
        check_vma=False,
    )
```
